32 devices in a mesh: rep: 4 (over y, x), shard: 8 (over z, core).
Axes of the slice: x: 2, y: 2, z: 4, core: 2. Of those that a mesh axis runs over, the one named last changes fastest.
Arguments:
- latents: float32 [128, 16, 256], P(('rep', 'shard')), may hold values from -6 to 6
- target_noise: float32 [128, 16, 256], P(('rep', 'shard')), may hold values from -6 to 6
- labels: int32 [128], P(('rep', 'shard')), may hold values from 0 to 999
- time_steps: int32 [128], P(('rep', 'shard')), may hold values from 0 to 999
- inner_weights: float32 [2, 768, 10752], P(None, 'shard'), may hold values from -0.4330127 to 0.4330127
- outer_weights: float32 [2, 3086, 768], P(None, None, 'shard'), may hold values from -1.2 to 1.2
- embed_table: float32 [2043, 768], P(None, 'shard'), may hold values from -2 to 2
- final_mod: float32 [769, 1536], P(None, 'shard'), may hold values from -1.2 to 1.2
- head_weights: float32 [769, 16], replicated, may hold values from -0.21875 to 0.21875
- inner_moment: float32 [2, 768, 10752], P(None, 'shard'), may hold values from -3e-06 to 3e-06
- inner_square: float32 [2, 768, 10752], P(None, 'shard'), may hold values from 1e-15 to 1e-13
- outer_moment: float32 [2, 3086, 768], P(None, None, 'shard'), may hold values from -3e-06 to 3e-06
- outer_square: float32 [2, 3086, 768], P(None, None, 'shard'), may hold values from 1e-15 to 1e-13
- embed_moment: float32 [2043, 768], P(None, 'shard'), may hold values from -3e-06 to 3e-06
- embed_square: float32 [2043, 768], P(None, 'shard'), may hold values from 1e-15 to 1e-13
- final_moment: float32 [769, 1536], P(None, 'shard'), may hold values from -3e-06 to 3e-06
- final_square: float32 [769, 1536], P(None, 'shard'), may hold values from 1e-15 to 1e-13
- head_moment: float32 [769, 16], replicated, may hold values from -3e-06 to 3e-06
- head_square: float32 [769, 16], replicated, may hold values from 1e-15 to 1e-13
Outputs:
- mean_loss: float32 [], replicated
- grad_norm: float32 [], replicated
- inner_new: float32 [2, 768, 10752], P(None, 'shard')
- inner_moment_new: float32 [2, 768, 10752], P(None, 'shard')
- inner_square_new: float32 [2, 768, 10752], P(None, 'shard')
- inner_copy: bfloat16 [2, 768, 10752], P(None, 'shard')
- outer_new: float32 [2, 3086, 768], P(None, None, 'shard')
- outer_moment_new: float32 [2, 3086, 768], P(None, None, 'shard')
- outer_square_new: float32 [2, 3086, 768], P(None, None, 'shard')
- outer_copy: bfloat16 [2, 3086, 768], P(None, None, 'shard')
- embed_new: float32 [2043, 768], P(None, 'shard')
- embed_moment_new: float32 [2043, 768], P(None, 'shard')
- embed_square_new: float32 [2043, 768], P(None, 'shard')
- embed_copy: bfloat16 [2043, 768], P(None, 'shard')
- final_new: float32 [769, 1536], P(None, 'shard')
- final_moment_new: float32 [769, 1536], P(None, 'shard')
- final_square_new: float32 [769, 1536], P(None, 'shard')
- final_copy: bfloat16 [769, 1536], P(None, 'shard')
- head_new: float32 [769, 16], replicated
- head_moment_new: float32 [769, 16], replicated
- head_square_new: float32 [769, 16], replicated
- head_copy: bfloat16 [769, 16], replicated
The draws below stay inside these ranges and needn't reach their ends.
All inputs are finite; a program needn't handle non-finite values.
Results may differ from the reference program's by a relative error of at most 0.0045.
The reference program's roundings to bfloat16 on the way count: a program that leaves them out, or rounds other values in their place, can miss the bound.
Values may be sent and summed in bfloat16 or wider, within the bound.
A program may use at most 384 MiB of HBM per device.

```python
import math
import jax
import jax.numpy as jnp
from jax import lax

D = 768
HEADS = 12
HDIM = 64
FF = 3072
FREQ = 256
NCLASS = 1000
P_SIZE = 16
GRID = 16
LAYERS = 2
TOK = 256
LATENTS = 128


def draw_inner_weights(key, part):
    column = jnp.arange(10 * D + FF)
    scale_by = jnp.where(column < 3 * D, 1.0, jnp.where(column < 4 * D, 3.0, jnp.where(column < 4 * D + FF, 1.0, 1.5))) / math.sqrt(D)
    base = jnp.clip(jax.random.normal(key, (LAYERS, D, 10 * D + FF), jnp.float32), -4.0, 4.0)
    return base * scale_by[None, None, :]


def draw_outer_weights(key, part):
    row_ids = jnp.arange(FF + 10 + FF // D)
    scale_by = jnp.where(row_ids < FF, 1.0 / math.sqrt(FF), 0.3)
    base = jnp.clip(jax.random.normal(key, (LAYERS, FF + 10 + FF // D, D), jnp.float32), -4.0, 4.0)
    return base * scale_by[None, :, None]


def draw_embed_table(key, part):
    row_ids = jnp.arange(P_SIZE + FREQ + D + NCLASS + 3)
    scale_by = jnp.where(row_ids < P_SIZE, 1.0 / math.sqrt(P_SIZE), jnp.where(row_ids == P_SIZE, 0.3, jnp.where(row_ids < P_SIZE + 1 + FREQ, 1.0 / math.sqrt(FREQ), jnp.where(row_ids == P_SIZE + 1 + FREQ, 0.3, jnp.where(row_ids < P_SIZE + 2 + FREQ + D, 1.0 / math.sqrt(D), jnp.where(row_ids == P_SIZE + 2 + FREQ + D, 0.3, 0.5))))))
    base = jnp.clip(jax.random.normal(key, (P_SIZE + FREQ + D + NCLASS + 3, D), jnp.float32), -4.0, 4.0)
    return base * scale_by[:, None]


def draw_final_mod(key, part):
    row_ids = jnp.arange(D + 1)
    scale_by = jnp.where(row_ids < D, 1.0 / math.sqrt(D), 0.3)
    base = jnp.clip(jax.random.normal(key, (D + 1, 2 * D), jnp.float32), -4.0, 4.0)
    return base * scale_by[:, None]


def touch_ends(result, own_key, least, top_value):
    longest = result.shape.index(max(result.shape))
    spots = []
    for shift in (0, 1):
        where = [jax.random.randint(jax.random.fold_in(own_key, axis), (), 0, length) for axis, length in enumerate(result.shape)]
        where[longest] = (where[longest] + shift) % result.shape[longest]
        spots.append(tuple(where))
    return result.at[spots[0]].set(least).at[spots[1]].set(top_value)


def steps_of(key, shape, cuts, least, top_value):
    def one(dim, blocks):
        heights = jax.random.uniform(jax.random.fold_in(jax.random.fold_in(key, 6), dim), (blocks,), jnp.float32, least / len(cuts), top_value / len(cuts))
        return jnp.repeat(jnp.exp(heights), shape[dim] // blocks).reshape((-1,) + (1,) * (len(shape) - dim - 1))

    gain = one(*cuts[0])
    for cut in cuts[1:]:
        gain = gain * one(*cut)
    return gain


def scatter_about(key, dims, width, most, cuts=(), kind=jnp.bfloat16):
    array = width * jax.random.normal(key, dims, jnp.float32)
    if cuts:
        array = array * steps_of(key, dims, cuts, -0.22, 0.18)
    return jnp.clip(array, -most, most).astype(kind)


def setup_inputs(seed: int = 0) -> dict:
    seeds = jax.random.split(jax.random.key(seed), 20)
    return {
        "latents": scatter_about(seeds[0], (LATENTS, P_SIZE, TOK), 1.0, 6.0, ((0, 32),), jnp.float32),
        "target_noise": scatter_about(seeds[1], (LATENTS, P_SIZE, TOK), 1.0, 6.0, ((0, 32),), jnp.float32),
        "labels": touch_ends(jax.random.randint(seeds[2], (LATENTS,), 0, NCLASS), jax.random.fold_in(seeds[2], 1), 0, NCLASS - 1).astype(jnp.int32),
        "time_steps": touch_ends(jax.random.randint(seeds[3], (LATENTS,), 0, 1000), jax.random.fold_in(seeds[3], 1), 0, 999).astype(jnp.int32),
        "inner_weights": draw_inner_weights(jax.random.fold_in(seeds[19], 71), 0),
        "outer_weights": draw_outer_weights(jax.random.fold_in(seeds[19], 71), 0),
        "embed_table": draw_embed_table(jax.random.fold_in(seeds[19], 71), 0),
        "final_mod": draw_final_mod(jax.random.fold_in(seeds[19], 71), 0),
        "head_weights": scatter_about(seeds[8], (D + 1, P_SIZE), D ** -0.5, 0.21875, (), jnp.float32),
        "inner_moment": scatter_about(seeds[9], (LAYERS, D, 10 * D + FF), (5e-7), 3.000000106112566e-06, ((1, 8),), jnp.float32),
        "inner_square": jnp.clip(jnp.exp(math.log(9.9999998245167e-14) - 4.6051702 * jax.random.uniform(seeds[10], (LAYERS, D, 10 * D + FF), jnp.float32) ** steps_of(seeds[10], (LAYERS, D, 10 * D + FF), ((1, 8),), -0.2, 0.2)), 1.0000000036274937e-15, 9.9999998245167e-14),
        "outer_moment": scatter_about(seeds[11], (LAYERS, FF + 10 + FF // D, D), (5e-7), 3.000000106112566e-06, ((2, 8),), jnp.float32),
        "outer_square": jnp.clip(jnp.exp(math.log(9.9999998245167e-14) - 4.6051702 * jax.random.uniform(seeds[12], (LAYERS, FF + 10 + FF // D, D), jnp.float32) ** steps_of(seeds[12], (LAYERS, FF + 10 + FF // D, D), ((2, 8),), -0.2, 0.2)), 1.0000000036274937e-15, 9.9999998245167e-14),
        "embed_moment": scatter_about(seeds[13], (P_SIZE + FREQ + D + NCLASS + 3, D), (5e-7), 3.000000106112566e-06, ((1, 8),), jnp.float32),
        "embed_square": jnp.clip(jnp.exp(math.log(9.9999998245167e-14) - 4.6051702 * jax.random.uniform(seeds[14], (P_SIZE + FREQ + D + NCLASS + 3, D), jnp.float32) ** steps_of(seeds[14], (P_SIZE + FREQ + D + NCLASS + 3, D), ((1, 8),), -0.2, 0.2)), 1.0000000036274937e-15, 9.9999998245167e-14),
        "final_moment": scatter_about(seeds[15], (D + 1, 2 * D), (5e-7), 3.000000106112566e-06, ((1, 8),), jnp.float32),
        "final_square": jnp.clip(jnp.exp(math.log(9.9999998245167e-14) - 4.6051702 * jax.random.uniform(seeds[16], (D + 1, 2 * D), jnp.float32) ** steps_of(seeds[16], (D + 1, 2 * D), ((1, 8),), -0.2, 0.2)), 1.0000000036274937e-15, 9.9999998245167e-14),
        "head_moment": scatter_about(seeds[17], (D + 1, P_SIZE), (5e-7), 3.000000106112566e-06, (), jnp.float32),
        "head_square": jnp.clip(jnp.exp(jax.random.uniform(seeds[18], (D + 1, P_SIZE), jnp.float32, math.log(1.0000000036274937e-15), math.log(9.9999998245167e-14))), 1.0000000036274937e-15, 9.9999998245167e-14),
    }


@jax.custom_vjp
def low(v):
    return lax.optimization_barrier(v.astype(jnp.bfloat16)).astype(jnp.float32)

@jax.custom_vjp
def low_back(v):
    return v

def low_keep(v):
    return (low(v), None)

def low_pass(kept, grad):
    return (grad,)

def back_keep(v):
    return (v, None)

def back_low(kept, grad):
    return (low(grad),)
low.defvjp(low_keep, low_pass)
low_back.defvjp(back_keep, back_low)
norm_eps = 1e-06
clip_coef = 2.5
beta_one = 0.9
beta_two = 0.999
adam_eps = 1e-08
learn_rate = 0.01
weight_decay = 0.01
step_count = 10.0
highest = lax.Precision.HIGHEST

def noise_levels():
    beta_line = 0.0001 + (0.02 - 0.0001) * jnp.arange(1000, dtype=jnp.float32) / 999.0
    cumulative = jnp.exp(jnp.cumsum(jnp.log(1.0 - beta_line)))
    return (jnp.sqrt(cumulative), jnp.sqrt(1.0 - cumulative))

def position_table(grid_side, feature_width):
    quarter = feature_width // 4
    omega_rate = jnp.exp(-math.log(10000.0) * jnp.arange(quarter, dtype=jnp.float32) / quarter)
    cell_ids = jnp.arange(grid_side * grid_side, dtype=jnp.int32)
    across = (cell_ids % grid_side).astype(jnp.float32)[:, None] * omega_rate[None, :]
    downward = (cell_ids // grid_side).astype(jnp.float32)[:, None] * omega_rate[None, :]
    return jnp.concatenate([jnp.sin(across), jnp.cos(across), jnp.sin(downward), jnp.cos(downward)], axis=1)

def time_features(step_ids, feature_count):
    half_count = feature_count // 2
    frequency = jnp.exp(-math.log(10000.0) * jnp.arange(half_count, dtype=jnp.float32) / half_count)
    angles = step_ids.astype(jnp.float32)[:, None] * frequency[None, :]
    return jnp.concatenate([jnp.cos(angles), jnp.sin(angles)], axis=1)

def modulate(stream, shift_by, scale_by):
    center = stream - lax.optimization_barrier(jnp.mean(stream, axis=-1, keepdims=True))
    spread = lax.optimization_barrier(jnp.mean(center * center, axis=-1, keepdims=True))
    return center * lax.rsqrt(spread + norm_eps) * (1.0 + scale_by[:, None, :]) + shift_by[:, None, :]

def adam_update(weights, gradient, moment, square, factor):
    scaled = gradient * factor
    moment_new = beta_one * moment + (1.0 - beta_one) * scaled
    square_new = beta_two * square + (1.0 - beta_two) * scaled * scaled
    moment_hat = moment_new / (1.0 - beta_one ** step_count)
    square_hat = square_new / (1.0 - beta_two ** step_count)
    updated = weights - learn_rate * (moment_hat / (jnp.sqrt(square_hat) + adam_eps) + weight_decay * weights)
    return (updated, moment_new, square_new, updated.astype(jnp.bfloat16))

def split_heads(tensor):
    return tensor.reshape(tensor.shape[0], tensor.shape[1], HEADS, HDIM)

def attention(queries, keys_all, values_all):
    scores = jnp.einsum('gqhe,gkhe->ghqk', split_heads(queries), split_heads(keys_all), precision=highest) * HDIM ** (-0.5)
    scores = low_back(scores)
    highest_score = lax.optimization_barrier(jnp.max(scores, axis=-1, keepdims=True))
    exponent = jnp.exp(scores - highest_score)
    probs = low(exponent / lax.optimization_barrier(jnp.sum(exponent, axis=-1, keepdims=True)))
    mixed = jnp.einsum('ghqk,gkhe->gqhe', probs, split_heads(values_all), precision=highest)
    return mixed.reshape(queries.shape)

def forward(params, lat_group, noise_group, label_group, step_group):
    inner_all, outer_all, embed_all, final_all, head_all = [low(weights) for weights in params]
    signal_table, noise_table = noise_levels()
    signal_rate = signal_table[step_group]
    noise_rate = noise_table[step_group]
    patches = low(signal_rate[:, None, None] * lat_group + noise_rate[:, None, None] * noise_group)
    row_time = P_SIZE + 1
    row_second = P_SIZE + 2 + FREQ
    row_class = P_SIZE + 3 + FREQ + D
    stream = low_back(jnp.einsum('gpt,pd->gtd', patches, embed_all[:P_SIZE], precision=highest)) + embed_all[P_SIZE] + position_table(GRID, D)[None]
    features = low(time_features(step_group, FREQ))
    time_hidden = low_back(jnp.dot(features, embed_all[row_time:row_time + FREQ], precision=highest)) + embed_all[row_time + FREQ]
    time_act = low(jax.nn.silu(time_hidden))
    second = low_back(jnp.dot(time_act, embed_all[row_second:row_second + D], precision=highest)) + embed_all[row_second + D]
    condition = second + jnp.take(embed_all[row_class:], label_group, axis=0)
    cond_act = low(jax.nn.silu(condition))
    blocks = FF // D
    for layer_idx in range(LAYERS):
        inner_full = inner_all[layer_idx]
        outer_full = outer_all[layer_idx]
        bias_rows = outer_full[FF:]
        modul = low_back(jnp.dot(cond_act, inner_full[:, 4 * D + FF:], precision=highest)) + bias_rows[3 + blocks:9 + blocks].reshape(-1)
        shift_one, scale_one, gate_one, shift_two, scale_two, gate_two = jnp.split(modul, 6, axis=1)
        normed = low(modulate(stream, shift_one, scale_one))
        projected = jnp.einsum('gtd,de->gte', normed, inner_full[:, :3 * D], precision=highest)
        queries = low(low_back(projected[..., :D] + bias_rows[0]))
        keys_all = low(low_back(projected[..., D:2 * D]))
        values_all = low(low_back(projected[..., 2 * D:3 * D] + bias_rows[1]))
        mixed = low(low_back(attention(queries, keys_all, values_all)))
        attn_out = low_back(jnp.einsum('gtd,de->gte', mixed, inner_full[:, 3 * D:4 * D], precision=highest)) + bias_rows[2]
        middle = stream + gate_one[:, None, :] * attn_out
        normed_two = low(modulate(middle, shift_two, scale_two))
        upper = low_back(jnp.einsum('gtd,de->gte', normed_two, inner_full[:, 4 * D:4 * D + FF], precision=highest)) + bias_rows[3:3 + blocks].reshape(-1)
        activ = low(jax.nn.gelu(upper, approximate=True))
        down_out = low_back(jnp.einsum('gtf,fd->gtd', activ, outer_full[:FF], precision=highest)) + bias_rows[9 + blocks]
        stream = middle + gate_two[:, None, :] * down_out
    fin_mod = low_back(jnp.dot(cond_act, final_all[:D], precision=highest)) + final_all[D]
    fin_shift, fin_scale = jnp.split(fin_mod, 2, axis=1)
    fin_normed = low(modulate(stream, fin_shift, fin_scale))
    output = low_back(jnp.einsum('gtd,dp->gtp', fin_normed, head_all[:D], precision=highest)) + head_all[D]
    differ = output - jnp.swapaxes(noise_group, 1, 2)
    return jnp.sum(differ * differ) / (LATENTS * TOK * P_SIZE)

def reference(latents, target_noise, labels, time_steps, inner_weights, outer_weights, embed_table, final_mod, head_weights, inner_moment, inner_square, outer_moment, outer_square, embed_moment, embed_square, final_moment, final_square, head_moment, head_square):
    params = (inner_weights, outer_weights, embed_table, final_mod, head_weights)
    group_size = math.gcd(LATENTS, max(1, 4096 // TOK))
    batches = (latents.reshape(-1, group_size, P_SIZE, TOK), target_noise.reshape(-1, group_size, P_SIZE, TOK), labels.reshape(-1, group_size), time_steps.reshape(-1, group_size))

    def one_group(running, group_batch):

        def loss_of(weights):
            return forward(weights, group_batch[0], group_batch[1], group_batch[2], group_batch[3])
        loss_value, pullback = jax.vjp(loss_of, params)
        gradient = pullback(jnp.ones_like(loss_value))[0]
        return ((running[0] + loss_value, jax.tree.map(jnp.add, running[1], gradient)), None)
    initial = (jnp.zeros((), jnp.float32), jax.tree.map(jnp.zeros_like, params))
    (mean_loss, gradient), unused = lax.scan(one_group, initial, batches)
    squares = jnp.zeros((), jnp.float32)
    for part_grad in gradient:
        squares = squares + jnp.sum(part_grad * part_grad)
    grad_norm = jnp.sqrt(squares)
    limit = clip_coef * math.sqrt(D / (LATENTS * TOK * P_SIZE))
    factor = jnp.minimum(1.0, limit / grad_norm)
    moments = (inner_moment, outer_moment, embed_moment, final_moment, head_moment)
    seconds = (inner_square, outer_square, embed_square, final_square, head_square)
    results = []
    for weights, part_grad, moment, square in zip(params, gradient, moments, seconds):
        results.extend(adam_update(weights, part_grad, moment, square, factor))
    return (mean_loss, grad_norm, results[0], results[1], results[2], results[3], results[4], results[5], results[6], results[7], results[8], results[9], results[10], results[11], results[12], results[13], results[14], results[15], results[16], results[17], results[18], results[19])
```

```python
from jax.sharding import PartitionSpec as P
import functools, math
import jax, jax.numpy as jnp
from jax import lax
from jax.experimental import pallas as pl
from jax.experimental.pallas import tpu as pltpu
D=768; HEADS=12; HDIM=64; FF=3072; TOK=256
norm_eps=1e-6
bf=jnp.bfloat16; f32=jnp.float32
VLIM=60*1024*1024
def mm(a,b): return lax.dot_general(a,b,(((1,),(0,)),((),())),preferred_element_type=f32)
def mm_nt(a,b): return lax.dot_general(a,b,(((1,),(1,)),((),())),preferred_element_type=f32)
def mm_tn(a,b): return lax.dot_general(a,b,(((0,),(0,)),((),())),preferred_element_type=f32)
def ln_parts(x):
    c=x-jnp.mean(x,axis=-1,keepdims=True)
    r=lax.rsqrt(jnp.mean(c*c,axis=-1,keepdims=True)+norm_eps)
    return c*r, r
def ln_back(dy, xhat, r, sc):
    dxh=dy*(1.0+sc)
    m1=jnp.mean(dxh,axis=-1,keepdims=True); m2=jnp.mean(dxh*xhat,axis=-1,keepdims=True)
    return r*(dxh-m1-xhat*m2)
def half_masks():
    lane=lax.broadcasted_iota(jnp.int32,(1,128),1)
    lo=(lane<HDIM)
    return lo
C0=math.sqrt(2.0/math.pi); C1=0.044715

def fwd_kernel(x_ref, mod_ref, bias_ref, wa_ref, w1_ref, w2_ref,
               normed_ref, qkv_ref, lse_ref, mixed_ref, attn_ref, mid_ref, ntwo_ref, upper_ref, activ_ref, down_ref, out_ref):
    x=x_ref[...]
    mod=lambda j: mod_ref[0, j:j+1, :]
    bias=lambda j: bias_ref[j:j+1, :]
    xh,_=ln_parts(x)
    normed=(xh*(1.0+mod(1))+mod(0)).astype(bf)
    normed_ref[...]=normed
    qkv_ref[:, :D]=(mm(normed, wa_ref[0])+bias(0)).astype(bf)
    qkv_ref[:, D:2*D]=mm(normed, wa_ref[1]).astype(bf)
    qkv_ref[:, 2*D:]=(mm(normed, wa_ref[2])+bias(1)).astype(bf)
    lo=half_masks()
    for hp in range(HEADS//2):
        c=hp*128
        q=qkv_ref[:, c:c+128]; k=qkv_ref[:, D+c:D+c+128]; v=qkv_ref[:, 2*D+c:2*D+c+128]
        outs=[]
        for h in range(2):
            keep=lo if h==0 else jnp.logical_not(lo)
            qm=jnp.where(keep, q, jnp.zeros_like(q))
            s=mm_nt(qm,k)*(HDIM**-0.5)
            m=jnp.max(s,axis=-1,keepdims=True)
            e=jnp.exp(s-m)
            l=jnp.sum(e,axis=-1,keepdims=True)
            p=(e*(1.0/l)).astype(bf)
            lse_ref[:, 2*hp+h:2*hp+h+1]=m+jnp.log(l)
            outs.append(mm(p,v))
        mixed_ref[:, c:c+128]=jnp.where(lo, outs[0], outs[1]).astype(bf)
    attn=mm(mixed_ref[...], wa_ref[3])+bias(2)
    attn_ref[...]=attn
    mid=x+mod(2)*attn
    mid_ref[...]=mid
    xh2,_=ln_parts(mid)
    ntwo=(xh2*(1.0+mod(4))+mod(3)).astype(bf)
    ntwo_ref[...]=ntwo
    down=jnp.broadcast_to(bias(13),(TOK,D))
    for j in range(4):
        up=mm(ntwo, w1_ref[j])+bias(3+j)
        upper_ref[:, j*D:(j+1)*D]=up
        t=jnp.tanh(C0*(up+C1*(up*up*up)))
        act=(0.5*up*(1.0+t)).astype(bf)
        activ_ref[:, j*D:(j+1)*D]=act
        down=down+mm_nt(act, w2_ref[j])
    down_ref[...]=down
    out_ref[...]=mid_ref[...]+mod(5)*down

def full(shape):
    n=len(shape)
    return pl.BlockSpec(shape, lambda i: (0,)*n, pipeline_mode=pl.Buffered(1))
def rows(width): return pl.BlockSpec((TOK,width), lambda i:(i,0))
def layer_fwd(x, mod, bias, wa, w1, w2):
    T=x.shape[0]; n=T//TOK
    sd=jax.ShapeDtypeStruct
    widths=[(D,bf),(3*D,bf),(128,f32),(D,bf),(D,f32),(D,f32),(D,bf),(FF,f32),(FF,bf),(D,f32),(D,f32)]
    return pl.pallas_call(fwd_kernel, grid=(n,),
        in_specs=[rows(D), pl.BlockSpec((1,8,D),lambda i:(i,0,0)), full((16,D)), full((4,D,D)), full((4,D,D)), full((4,D,D))],
        out_specs=[rows(w) for w,_ in widths],
        out_shape=[sd((T,w),t) for w,t in widths],
        compiler_params=pltpu.CompilerParams(vmem_limit_bytes=VLIM),
        cost_estimate=pl.CostEstimate(flops=2*T*(9216*D+2*TOK*D), bytes_accessed=60_000_000, transcendentals=T*FF*2),
    )(x,mod,bias,wa,w1,w2)

def bwd_mlp_kernel(g_ref, mod_ref, wa3_ref, w1_ref, w2_ref, down_ref, upper_ref, mid_ref, attn_ref,
                   dlow_ref, ulow_ref, gmid_ref, alow_ref, gmix_ref, dmod_ref, db_ref):
    i=pl.program_id(0)
    mod=lambda j: mod_ref[0, j:j+1, :]
    g=g_ref[...]
    gd=g*mod(5)
    dl=gd.astype(bf)
    dlow_ref[...]=dl
    @pl.when(i==0)
    def _(): db_ref[...]=jnp.zeros_like(db_ref)
    s0=lambda v: jnp.sum(v,axis=0,keepdims=True)
    dmod_ref[0,5:6,:]=s0(g*down_ref[...])
    db_ref[13:14,:]+=s0(gd)
    gn=jnp.zeros((TOK,D),f32)
    for j in range(4):
        ga=mm(dl, w2_ref[j])
        up=upper_ref[:, j*D:(j+1)*D]
        u2=up*up
        t=jnp.tanh(C0*(up+C1*(u2*up)))
        gu=ga*(0.5*(1.0+t)+(0.5*C0)*up*(1.0-t*t)*(1.0+(3.0*C1)*u2))
        db_ref[3+j:4+j,:]+=s0(gu)
        ul=gu.astype(bf)
        ulow_ref[:, j*D:(j+1)*D]=ul
        gn=gn+mm_nt(ul, w1_ref[j])
    xh,r=ln_parts(mid_ref[...])
    dmod_ref[0,3:4,:]=s0(gn)
    dmod_ref[0,4:5,:]=s0(gn*xh)
    gm=g_ref[...]+ln_back(gn,xh,r,mod(4))
    gmid_ref[...]=gm
    ga=gm*mod(2)
    dmod_ref[0,2:3,:]=s0(gm*attn_ref[...])
    db_ref[2:3,:]+=s0(ga)
    al=ga.astype(bf)
    alow_ref[...]=al
    gmix_ref[...]=mm_nt(al, wa3_ref[0]).astype(bf)
def layer_bwd_mlp(g, mod, wa, w1, w2, down, upper, mid, attn):
    T=g.shape[0]; n=T//TOK
    sd=jax.ShapeDtypeStruct
    m3=pl.BlockSpec((1,8,D),lambda i:(i,0,0))
    return pl.pallas_call(bwd_mlp_kernel, grid=(n,),
        in_specs=[rows(D), m3, pl.BlockSpec((1,D,D),lambda i:(3,0,0),pipeline_mode=pl.Buffered(1)), full((4,D,D)), full((4,D,D)), rows(D), rows(FF), rows(D), rows(D)],
        out_specs=[rows(D),rows(FF),rows(D),rows(D),rows(D),m3,pl.BlockSpec((16,D),lambda i:(0,0))],
        out_shape=[sd((T,D),bf),sd((T,FF),bf),sd((T,D),f32),sd((T,D),bf),sd((T,D),bf),sd((n,8,D),f32),sd((16,D),f32)],
        compiler_params=pltpu.CompilerParams(vmem_limit_bytes=VLIM),
        cost_estimate=pl.CostEstimate(flops=2*T*D*(2*FF+D), bytes_accessed=50_000_000, transcendentals=T*FF),
    )(g,mod,wa,w1,w2,down,upper,mid,attn)

def bwd_attn_kernel(gmix_ref, gmid_ref, mod_ref, wa_ref, qkv_ref, lse_ref, x_ref,
                    low_ref, gin_ref, dmod_ref, db_ref):
    i=pl.program_id(0)
    mod=lambda j: mod_ref[0, j:j+1, :]
    @pl.when(i==0)
    def _(): db_ref[...]=jnp.zeros_like(db_ref)
    s0=lambda v: jnp.sum(v,axis=0,keepdims=True)
    lo=half_masks()
    zero=jnp.zeros((TOK,128),bf)
    for hp in range(HEADS//2):
        c=hp*128
        q=qkv_ref[:, c:c+128]; k=qkv_ref[:, D+c:D+c+128]; v=qkv_ref[:, 2*D+c:2*D+c+128]
        gm=gmix_ref[:, c:c+128]
        res=[]
        for h in range(2):
            keep=lo if h==0 else jnp.logical_not(lo)
            qm=jnp.where(keep,q,zero); gmm=jnp.where(keep,gm,zero)
            s=mm_nt(qm,k)*(HDIM**-0.5)
            p=jnp.exp(s-lse_ref[:, 2*hp+h:2*hp+h+1])
            dp=mm_nt(gmm,v)
            ds=p*(dp-jnp.sum(p*dp,axis=-1,keepdims=True))
            dsl=ds.astype(bf)
            res.append((mm(dsl,k), mm_tn(dsl,q), mm_tn(p.astype(bf),gm)))
        for j in range(3):
            o=jnp.where(lo,res[0][j],res[1][j])
            if j<2: o=o*(HDIM**-0.5)
            ol=o.astype(bf)
            low_ref[:, j*D+c:j*D+c+128]=ol
            if j!=1:
                row=0 if j==0 else 1
                db_ref[row:row+1, c:c+128]+=s0(ol.astype(f32))
    gn=mm_nt(low_ref[:, :D], wa_ref[0])+mm_nt(low_ref[:, D:2*D], wa_ref[1])+mm_nt(low_ref[:, 2*D:], wa_ref[2])
    xh,r=ln_parts(x_ref[...])
    dmod_ref[...]=jnp.zeros_like(dmod_ref)
    dmod_ref[0,0:1,:]=s0(gn)
    dmod_ref[0,1:2,:]=s0(gn*xh)
    gin_ref[...]=gmid_ref[...]+ln_back(gn,xh,r,mod(1))
def layer_bwd_attn(gmix, gmid, mod, wa, qkv, lse, x):
    T=gmix.shape[0]; n=T//TOK
    sd=jax.ShapeDtypeStruct
    m3=pl.BlockSpec((1,8,D),lambda i:(i,0,0))
    return pl.pallas_call(bwd_attn_kernel, grid=(n,),
        in_specs=[rows(D),rows(D),m3,full((3,D,D)),rows(3*D),rows(128),rows(D)],
        out_specs=[rows(3*D),rows(D),m3,pl.BlockSpec((8,D),lambda i:(0,0))],
        out_shape=[sd((T,3*D),bf),sd((T,D),f32),sd((n,8,D),f32),sd((8,D),f32)],
        compiler_params=pltpu.CompilerParams(vmem_limit_bytes=VLIM),
        cost_estimate=pl.CostEstimate(flops=2*T*D*(3*D+5*TOK), bytes_accessed=25_000_000, transcendentals=T*TOK*HEADS),
    )(gmix,gmid,mod,wa,qkv,lse,x)

def dw_kernel(x_ref, dy_ref, o_ref, xt_ref):
    @pl.when(pl.program_id(0)==0)
    def _(): xt_ref[...]=x_ref[...].T
    o_ref[...]=mm(xt_ref[...], dy_ref[...])
def dw(x, dy):
    T=x.shape[0]; C=dy.shape[1]; W=384
    return pl.pallas_call(dw_kernel, grid=(C//W,),
        in_specs=[pl.BlockSpec((T,D),lambda i:(0,0)), pl.BlockSpec((T,W),lambda i:(0,i))],
        out_specs=pl.BlockSpec((D,W),lambda i:(0,i)),
        out_shape=jax.ShapeDtypeStruct((D,C),f32),
        scratch_shapes=[pltpu.VMEM((D,T),bf)],
        compiler_params=pltpu.CompilerParams(vmem_limit_bytes=VLIM),
    )(x,dy)
def gather_kernel(R, nz, U, w_ref, out_ref, zs, zr, xs, xr, cs, cr, ls):
    rep=lax.axis_index("rep"); shard=lax.axis_index("shard")
    z=shard//2; c=lax.rem(shard,2)
    dev=lambda r,zz,cc: (r, 2*zz+cc)
    MESH=pl.DeviceIdType.MESH
    bar=pltpu.get_barrier_semaphore()
    peers=[dev(rep, lax.rem(z+k,nz), c) for k in range(1,nz)]+[dev(jnp.bitwise_xor(rep,j), z, c) for j in range(1,R)]+[dev(rep,z,1-c)]
    for p in peers: pl.semaphore_signal(bar, inc=1, device_id=p, device_id_type=MESH)
    pl.semaphore_wait(bar, len(peers))
    def zcopy(u,k):
        return pltpu.make_async_remote_copy(src_ref=w_ref.at[u,rep], dst_ref=out_ref.at[u,rep,z,c], send_sem=zs.at[u,k-1], recv_sem=zr.at[u,k-1],
            device_id=dev(rep,lax.rem(z+k,nz),c), device_id_type=MESH)
    def xcopy(u,j,k):
        o=lax.rem(z-k+nz,nz)
        return pltpu.make_async_remote_copy(src_ref=out_ref.at[u,rep,o,c], dst_ref=out_ref.at[u,rep,o,c], send_sem=xs.at[u,j-1,k-1], recv_sem=xr.at[u,j-1,k-1],
            device_id=dev(jnp.bitwise_xor(rep,j),z,c), device_id_type=MESH)
    def ccopy(u,j):
        r=jnp.bitwise_xor(rep,j)
        return pltpu.make_async_remote_copy(src_ref=out_ref.at[u,r,:,c], dst_ref=out_ref.at[u,r,:,c], send_sem=cs.at[u,j], recv_sem=cr.at[u,j],
            device_id=dev(rep,z,1-c), device_id_type=MESH)
    locs=[pltpu.make_async_copy(w_ref.at[u], out_ref.at[u,:,z,c], ls.at[u]) for u in range(U)]
    for u in range(U):
        for k in range(1,nz): zcopy(u,k).start()
    for u in range(U): locs[u].start()
    for u in range(U):
        for k in range(1,nz):
            zcopy(u,k).wait_recv()
            for j in range(1,R): xcopy(u,j,k).start()
        locs[u].wait()
        ccopy(u,0).start()
    for u in range(U):
        for j in range(1,R):
            for k in range(1,nz): xcopy(u,j,k).wait_recv()
            ccopy(u,j).start()
    for u in range(U):
        for j in range(R): ccopy(u,j).wait()
        for k in range(1,nz): zcopy(u,k).wait_send()
        for j in range(1,R):
            for k in range(1,nz): xcopy(u,j,k).wait_send()

def gather_layer(w, R, S, cid):
    U,_,rows_,W=w.shape
    nz=S//2
    dma=pltpu.SemaphoreType.DMA
    any_=pl.BlockSpec(memory_space=pl.ANY)
    out=pl.pallas_call(functools.partial(gather_kernel,R,nz,U),
        in_specs=[any_], out_specs=any_, out_shape=jax.ShapeDtypeStruct((U,R,nz,2,rows_,W),bf),
        scratch_shapes=[dma((U,nz-1)),dma((U,nz-1)),dma((U,R-1,nz-1)),dma((U,R-1,nz-1)),dma((U,R)),dma((U,R)),dma((U,))],
        compiler_params=pltpu.CompilerParams(collective_id=cid, has_side_effects=True, vmem_limit_bytes=4*1024*1024),
    )(w)
    out=out.reshape(U,R,D,W)
    if R==4: return [out[u] for u in range(U)]
    m=R//4
    return [out[u].reshape(4,m,D,W).transpose(0,2,1,3).reshape(4,D,D) for u in range(U)]
P_SIZE=16; GRID=16; LAYERS=2; LAT_DEV=4; FREQ=256; NCLASS=1000
clip_coef=2.5; beta_one=0.9; beta_two=0.999; adam_eps=1e-8; learn_rate=0.01; weight_decay=0.01; step_count=10.0
BIAS=14
def position_table(grid_side, feature_width):
    quarter=feature_width//4
    omega=jnp.exp(-math.log(10000.0)*jnp.arange(quarter,dtype=f32)/quarter)
    ids=jnp.arange(grid_side*grid_side,dtype=jnp.int32)
    a=(ids%grid_side).astype(f32)[:,None]*omega[None,:]
    d=(ids//grid_side).astype(f32)[:,None]*omega[None,:]
    return jnp.concatenate([jnp.sin(a),jnp.cos(a),jnp.sin(d),jnp.cos(d)],axis=1)
def time_features(steps, count):
    half=count//2
    freq=jnp.exp(-math.log(10000.0)*jnp.arange(half,dtype=f32)/half)
    ang=steps.astype(f32)[:,None]*freq[None,:]
    return jnp.concatenate([jnp.cos(ang),jnp.sin(ang)],axis=1)
def modulate(x, sh, sc):
    c=x-jnp.mean(x,axis=-1,keepdims=True)
    v=jnp.mean(c*c,axis=-1,keepdims=True)
    return c*lax.rsqrt(v+norm_eps)*(1.0+sc[:,None,:])+sh[:,None,:]
def adam_update(w,g,m,v,factor):
    s=g*factor
    m2=beta_one*m+(1.0-beta_one)*s
    v2=beta_two*v+(1.0-beta_two)*s*s
    mh=m2/(1.0-beta_one**step_count)
    vh=v2/(1.0-beta_two**step_count)
    w2=w-learn_rate*(mh/(jnp.sqrt(vh)+adam_eps)+weight_decay*w)
    return (w2,m2,v2,w2.astype(bf))
def dot32(pattern,a,b): return jnp.einsum(pattern,a,b,preferred_element_type=f32)
def silu_back(v,g): return jax.vjp(jax.nn.silu,v)[1](g)[0]
ALL=("rep","shard")

def per_device(latents,target_noise,labels,time_steps,inner_weights,outer_weights,embed_table,final_mod,head_weights,
               inner_moment,inner_square,outer_moment,outer_square,embed_moment,embed_square,final_moment,final_square,head_moment,head_square):
    R=lax.axis_size("rep"); S=lax.axis_size("shard")
    rep=lax.axis_index("rep"); shard=lax.axis_index("shard")
    own=D//S; W=4*D//R; N=LAT_DEV*R*S; G=LAT_DEV*S
    count=N*TOK*P_SIZE
    inner_low=inner_weights.astype(bf); outer_low=outer_weights.astype(bf)
    gathered=[]
    for l in range(LAYERS):
        slab=jnp.stack([inner_low[l,:,:4*D],inner_low[l,:,4*D:8*D],outer_low[l,:FF].T])
        slab=slab.reshape(3,own,R,W).transpose(0,2,1,3)
        gathered.append(gather_layer(slab,R,S,l))
    embed_low=embed_table.astype(bf); final_low=final_mod.astype(bf); head_low=head_weights.astype(bf)
    small=jnp.concatenate([outer_low[:,FF:].reshape(LAYERS*BIAS,own),embed_low[:P_SIZE+1]],axis=0)
    small=lax.all_gather(small,"shard",axis=1,tiled=True)
    biases=small[:LAYERS*BIAS].reshape(LAYERS,BIAS,D).astype(f32)
    patch_w=small[LAYERS*BIAS:LAYERS*BIAS+P_SIZE]; patch_b=small[LAYERS*BIAS+P_SIZE].astype(f32)
    ids=lax.all_gather(jnp.stack([time_steps,labels],axis=1),ALL,axis=0,tiled=True)
    steps_all=ids[:,0]; labels_all=ids[:,1]
    r1=P_SIZE+1; r2=P_SIZE+2+FREQ; r3=P_SIZE+3+FREQ+D
    features=time_features(steps_all,FREQ).astype(bf)
    hidden=dot32("nf,fd->nd",features,embed_low[r1:r1+FREQ])+embed_low[r1+FREQ].astype(f32)
    act_own=jax.nn.silu(hidden).astype(bf)
    time_act=lax.all_gather(act_own,"shard",axis=1,tiled=True)
    hot=labels_all[:,None]==jnp.arange(NCLASS,dtype=jnp.int32)[None,:]
    condition=dot32("nd,de->ne",time_act,embed_low[r2:r2+D])+embed_low[r2+D].astype(f32)+dot32("nc,ce->ne",hot.astype(bf),embed_low[r3:])
    cond_own=jax.nn.silu(condition).astype(bf)
    cond_all=lax.all_gather(cond_own,"shard",axis=1,tiled=True)
    cond_group=lax.dynamic_slice_in_dim(cond_own,rep*G,G,0)
    ada_own=inner_low[:,:,4*D+FF:]
    part=dot32("gd,lde->gle",cond_group,ada_own)
    modul=lax.psum_scatter(part,"shard",scatter_dimension=0,tiled=True)
    modul=modul.reshape(LAT_DEV,LAYERS,6,D)+biases[:,7:13].reshape(1,LAYERS,6,D)
    modul=jnp.pad(modul.transpose(1,0,2,3),((0,0),(0,0),(0,2),(0,0)))
    fin_cols=2*D//S
    fin_part=dot32("gd,de->ge",lax.dynamic_slice_in_dim(cond_all,rep*G,G,0),final_low[:D])+final_low[D].astype(f32)
    fin_mod=lax.all_to_all(fin_part.reshape(S,LAT_DEV,fin_cols),"shard",0,0,tiled=True)
    fin_mod=fin_mod.reshape(S,LAT_DEV,fin_cols).transpose(1,0,2).reshape(LAT_DEV,2*D)
    ramp=0.0001+(0.02-0.0001)*jnp.arange(1000,dtype=f32)/999.0
    upto=jnp.arange(1000,dtype=jnp.int32)[None,:]<=time_steps[:,None]
    abar=jnp.exp(jnp.sum(jnp.where(upto,jnp.log(1.0-ramp)[None,:],0.0),axis=1))
    patches=(jnp.sqrt(abar)[:,None,None]*latents+jnp.sqrt(1.0-abar)[:,None,None]*target_noise).astype(bf)
    stream=dot32("gpt,pd->gtd",patches,patch_w)+patch_b+position_table(GRID,D)[None]
    stream=stream.reshape(LAT_DEV*TOK,D)
    saved=[]
    for l in range(LAYERS):
        wa,w1,w2=gathered[l]
        bias=jnp.pad(biases[l],((0,2),(0,0)))
        o=layer_fwd(stream,modul[l],bias,wa,w1,w2)
        saved.append((stream,)+tuple(o))
        stream=o[-1]
    stream3=stream.reshape(LAT_DEV,TOK,D)
    fin_shift,fin_scale=jnp.split(fin_mod,2,axis=1)
    fin_normed=modulate(stream3,fin_shift,fin_scale).astype(bf)
    output=dot32("gtd,dp->gtp",fin_normed,head_low[:D])+head_low[D].astype(f32)
    differ=output-jnp.swapaxes(target_noise,1,2)
    loss_part=jnp.sum(differ*differ)/count
    grad_output=2.0*(differ*(1.0/count))
    head_bias=jnp.sum(grad_output,axis=(0,1))
    output_low=grad_output.astype(bf)
    head_grad=jnp.concatenate([dot32("gtd,gtp->dp",fin_normed,output_low),head_bias[None]],axis=0)
    grad_fin_normed=dot32("gtp,dp->gtd",output_low,head_low[:D])
    grad_stream,g_shift,g_scale=jax.vjp(modulate,stream3,fin_shift,fin_scale)[1](grad_fin_normed)
    grad_stream=grad_stream.reshape(LAT_DEV*TOK,D)
    grad_fin=jnp.concatenate([g_shift,g_scale],axis=1)
    fin_rows=lax.all_gather(grad_fin.astype(bf),ALL,axis=0,tiled=True)
    fin_mine=lax.dynamic_slice_in_dim(fin_rows,shard*fin_cols,fin_cols,1)
    final_main=dot32("nd,ne->de",cond_all,fin_mine)
    grad_cond=lax.psum_scatter(dot32("ne,de->nd",fin_mine,final_low[:D]),"shard",scatter_dimension=1,tiled=True)
    unit_parts=[None]*LAYERS; ada_parts=[None]*LAYERS; bias_grads=[None]*LAYERS
    for l in range(LAYERS-1,-1,-1):
        wa,w1,w2=gathered[l]
        x,normed,qkv,lse,mixed,attn,mid,ntwo,upper,activ,down,_=saved[l]
        dlow,ulow,gmid,alow,gmix,dm1,db1=layer_bwd_mlp(grad_stream,modul[l],wa,w1,w2,down,upper,mid,attn)
        low,grad_stream,dm2,db2=layer_bwd_attn(gmix,gmid,modul[l],wa,qkv,lse,x)
        units=[jnp.concatenate([dot32("td,te->de",normed,low),dot32("td,te->de",mixed,alow)],axis=1),dw(ntwo,ulow),dw(dlow,activ)]
        units=[lax.psum_scatter(u.astype(bf),"shard",scatter_dimension=0,tiled=True) for u in units]
        unit_parts[l]=[lax.psum(u.astype(f32),"rep") for u in units]
        dmod=jnp.concatenate([dm2[:,:2],dm1[:,2:6]],axis=1)
        rows_all=lax.all_gather(dmod.astype(bf).reshape(LAT_DEV,6*D),ALL,axis=0,tiled=True)
        ada_parts[l]=dot32("nd,ne->de",cond_own,rows_all)
        grad_cond=grad_cond+dot32("ne,de->nd",rows_all,ada_own[l])
        bias_grads[l]=jnp.concatenate([db2[0:2],db1[2:7],jnp.sum(dmod,axis=0),db1[13:14]],axis=0)
    gs=grad_stream.reshape(LAT_DEV,TOK,D)
    patch_grad=dot32("gpt,gtd->pd",patches,gs.astype(bf))
    patch_bias=jnp.sum(grad_stream,axis=0)
    fin_bias=jnp.sum(grad_fin,axis=0).reshape(2,D)
    tail=jnp.zeros((1,D),f32).at[0,0].set(loss_part)
    head_flat=head_grad.reshape(-1)
    head_rows=-(-head_flat.shape[0]//D)
    head_flat=jnp.pad(head_flat,(0,head_rows*D-head_flat.shape[0])).reshape(head_rows,D)
    sums=lax.psum(jnp.concatenate(bias_grads+[patch_grad,patch_bias[None],fin_bias,head_flat,tail],axis=0),ALL)
    o1=LAYERS*BIAS; o2=o1+P_SIZE+1; o3=o2+2; o4=o3+head_rows
    mean_loss=sums[o4,0]
    head_total=sums[o3:o4].reshape(-1)[:(D+1)*P_SIZE].reshape(D+1,P_SIZE)
    fin_bias_own=lax.dynamic_slice_in_dim(sums[o2:o3].reshape(2*D),shard*fin_cols,fin_cols,0)
    mine=lax.dynamic_slice_in_dim(sums[:o2],shard*own,own,1)
    grad_condition=silu_back(condition,grad_cond)
    b2=jnp.sum(grad_condition,axis=0)
    clow=grad_condition.astype(bf)
    second=dot32("nd,ne->de",time_act,clow)
    class_grad=jnp.einsum("nc,nd->cd",hot.astype(f32),grad_condition,precision=lax.Precision.HIGHEST)
    grad_time_act=lax.psum_scatter(dot32("ne,de->nd",clow,embed_low[r2:r2+D]),"shard",scatter_dimension=1,tiled=True)
    grad_time=silu_back(hidden,grad_time_act)
    first=dot32("nf,nd->fd",features,grad_time.astype(bf))
    embed_grad=jnp.concatenate([mine[o1:o2],first,jnp.sum(grad_time,axis=0)[None],second,b2[None],class_grad],axis=0)
    final_grad=jnp.concatenate([final_main,fin_bias_own[None]],axis=0)
    inner_grad=jnp.stack([jnp.concatenate([unit_parts[l][0],unit_parts[l][1],ada_parts[l]],axis=1) for l in range(LAYERS)])
    outer_grad=jnp.stack([jnp.concatenate([unit_parts[l][2].T,mine[l*BIAS:(l+1)*BIAS]],axis=0) for l in range(LAYERS)])
    sq=lambda a: jnp.sum(a*a)
    square=lax.psum(sq(inner_grad)+sq(outer_grad)+sq(embed_grad)+sq(final_grad),"shard")
    grad_norm=jnp.sqrt(square+sq(head_total))
    factor=jnp.minimum(1.0,clip_coef*math.sqrt(D/count)/grad_norm)
    out=[mean_loss,grad_norm]
    for w,g,m,v in ((inner_weights,inner_grad,inner_moment,inner_square),(outer_weights,outer_grad,outer_moment,outer_square),
                    (embed_table,embed_grad,embed_moment,embed_square),(final_mod,final_grad,final_moment,final_square),
                    (head_weights,head_total,head_moment,head_square)):
        out.extend(adam_update(w,g,m,v,factor))
    return tuple(out)

def solution(mesh):
    lat=P(ALL,None,None); one=P(ALL); inn=P(None,"shard",None); oute=P(None,None,"shard"); col=P(None,"shard")
    in_specs=(lat,lat,one,one,inn,oute,col,col,P(),inn,inn,oute,oute,col,col,col,col,P(),P())
    out_specs=(P(),P())+(inn,)*4+(oute,)*4+(col,)*8+(P(),)*4
    return jax.shard_map(per_device,mesh=mesh,in_specs=in_specs,out_specs=out_specs,check_vma=False)
```

```python
from jax.sharding import PartitionSpec as P
import functools, math
import jax, jax.numpy as jnp
from jax import lax
from jax.experimental import pallas as pl
from jax.experimental.pallas import tpu as pltpu
D=768; HEADS=12; HDIM=64; FF=3072; TOK=256
norm_eps=1e-6
bf=jnp.bfloat16; f32=jnp.float32
VLIM=60*1024*1024
def mm(a,b): return lax.dot_general(a,b,(((1,),(0,)),((),())),preferred_element_type=f32)
def mm_nt(a,b): return lax.dot_general(a,b,(((1,),(1,)),((),())),preferred_element_type=f32)
def mm_tn(a,b): return lax.dot_general(a,b,(((0,),(0,)),((),())),preferred_element_type=f32)
def ln_parts(x):
    c=x-jnp.mean(x,axis=-1,keepdims=True)
    r=lax.rsqrt(jnp.mean(c*c,axis=-1,keepdims=True)+norm_eps)
    return c*r, r
def ln_back(dy, xhat, r, sc):
    dxh=dy*(1.0+sc)
    m1=jnp.mean(dxh,axis=-1,keepdims=True); m2=jnp.mean(dxh*xhat,axis=-1,keepdims=True)
    return r*(dxh-m1-xhat*m2)
def half_masks():
    lane=lax.broadcasted_iota(jnp.int32,(1,128),1)
    lo=(lane<HDIM)
    return lo
C0=math.sqrt(2.0/math.pi); C1=0.044715

def fwd_kernel(x_ref, mod_ref, bias_ref, wa_ref, w1_ref, w2_ref,
               normed_ref, qkv_ref, lse_ref, mixed_ref, attn_ref, mid_ref, ntwo_ref, upper_ref, activ_ref, down_ref, out_ref):
    x=x_ref[...]
    mod=lambda j: mod_ref[0, j:j+1, :]
    bias=lambda j: bias_ref[j:j+1, :]
    xh,_=ln_parts(x)
    normed=(xh*(1.0+mod(1))+mod(0)).astype(bf)
    normed_ref[...]=normed
    qkv_ref[:, :D]=(mm(normed, wa_ref[0])+bias(0)).astype(bf)
    qkv_ref[:, D:2*D]=mm(normed, wa_ref[1]).astype(bf)
    qkv_ref[:, 2*D:]=(mm(normed, wa_ref[2])+bias(1)).astype(bf)
    lo=half_masks()
    for hp in range(HEADS//2):
        c=hp*128
        q=qkv_ref[:, c:c+128]; k=qkv_ref[:, D+c:D+c+128]; v=qkv_ref[:, 2*D+c:2*D+c+128]
        outs=[]
        for h in range(2):
            keep=lo if h==0 else jnp.logical_not(lo)
            qm=jnp.where(keep, q, jnp.zeros_like(q))
            s=mm_nt(qm,k)*(HDIM**-0.5)
            m=jnp.max(s,axis=-1,keepdims=True)
            e=jnp.exp(s-m)
            l=jnp.sum(e,axis=-1,keepdims=True)
            p=(e*(1.0/l)).astype(bf)
            lse_ref[:, 2*hp+h:2*hp+h+1]=m+jnp.log(l)
            outs.append(mm(p,v))
        mixed_ref[:, c:c+128]=jnp.where(lo, outs[0], outs[1]).astype(bf)
    attn=mm(mixed_ref[...], wa_ref[3])+bias(2)
    attn_ref[...]=attn
    mid=x+mod(2)*attn
    mid_ref[...]=mid
    xh2,_=ln_parts(mid)
    ntwo=(xh2*(1.0+mod(4))+mod(3)).astype(bf)
    ntwo_ref[...]=ntwo
    down=jnp.broadcast_to(bias(13),(TOK,D))
    for j in range(4):
        up=mm(ntwo, w1_ref[j])+bias(3+j)
        upper_ref[:, j*D:(j+1)*D]=up
        t=jnp.tanh(C0*(up+C1*(up*up*up)))
        act=(0.5*up*(1.0+t)).astype(bf)
        activ_ref[:, j*D:(j+1)*D]=act
        down=down+mm_nt(act, w2_ref[j])
    down_ref[...]=down
    out_ref[...]=mid_ref[...]+mod(5)*down

def full(shape):
    n=len(shape)
    return pl.BlockSpec(shape, lambda i: (0,)*n, pipeline_mode=pl.Buffered(1))
def rows(width): return pl.BlockSpec((TOK,width), lambda i:(i,0))
def layer_fwd(x, mod, bias, wa, w1, w2):
    T=x.shape[0]; n=T//TOK
    sd=jax.ShapeDtypeStruct
    widths=[(D,bf),(3*D,bf),(128,f32),(D,bf),(D,f32),(D,f32),(D,bf),(FF,f32),(FF,bf),(D,f32),(D,f32)]
    return pl.pallas_call(fwd_kernel, grid=(n,),
        in_specs=[rows(D), pl.BlockSpec((1,8,D),lambda i:(i,0,0)), full((16,D)), full((4,D,D)), full((4,D,D)), full((4,D,D))],
        out_specs=[rows(w) for w,_ in widths],
        out_shape=[sd((T,w),t) for w,t in widths],
        compiler_params=pltpu.CompilerParams(vmem_limit_bytes=VLIM),
        cost_estimate=pl.CostEstimate(flops=2*T*(9216*D+2*TOK*D), bytes_accessed=60_000_000, transcendentals=T*FF*2),
    )(x,mod,bias,wa,w1,w2)

def bwd_mlp_kernel(g_ref, mod_ref, wa3_ref, w1_ref, w2_ref, down_ref, upper_ref, mid_ref, attn_ref,
                   dlow_ref, ulow_ref, gmid_ref, alow_ref, gmix_ref, dmod_ref, db_ref):
    i=pl.program_id(0)
    mod=lambda j: mod_ref[0, j:j+1, :]
    g=g_ref[...]
    gd=g*mod(5)
    dl=gd.astype(bf)
    dlow_ref[...]=dl
    @pl.when(i==0)
    def _(): db_ref[...]=jnp.zeros_like(db_ref)
    s0=lambda v: jnp.sum(v,axis=0,keepdims=True)
    dmod_ref[0,5:6,:]=s0(g*down_ref[...])
    db_ref[13:14,:]+=s0(gd)
    gn=jnp.zeros((TOK,D),f32)
    for j in range(4):
        ga=mm(dl, w2_ref[j])
        up=upper_ref[:, j*D:(j+1)*D]
        u2=up*up
        t=jnp.tanh(C0*(up+C1*(u2*up)))
        gu=ga*(0.5*(1.0+t)+(0.5*C0)*up*(1.0-t*t)*(1.0+(3.0*C1)*u2))
        db_ref[3+j:4+j,:]+=s0(gu)
        ul=gu.astype(bf)
        ulow_ref[:, j*D:(j+1)*D]=ul
        gn=gn+mm_nt(ul, w1_ref[j])
    xh,r=ln_parts(mid_ref[...])
    dmod_ref[0,3:4,:]=s0(gn)
    dmod_ref[0,4:5,:]=s0(gn*xh)
    gm=g_ref[...]+ln_back(gn,xh,r,mod(4))
    gmid_ref[...]=gm
    ga=gm*mod(2)
    dmod_ref[0,2:3,:]=s0(gm*attn_ref[...])
    db_ref[2:3,:]+=s0(ga)
    al=ga.astype(bf)
    alow_ref[...]=al
    gmix_ref[...]=mm_nt(al, wa3_ref[0]).astype(bf)
def layer_bwd_mlp(g, mod, wa, w1, w2, down, upper, mid, attn):
    T=g.shape[0]; n=T//TOK
    sd=jax.ShapeDtypeStruct
    m3=pl.BlockSpec((1,8,D),lambda i:(i,0,0))
    return pl.pallas_call(bwd_mlp_kernel, grid=(n,),
        in_specs=[rows(D), m3, pl.BlockSpec((1,D,D),lambda i:(3,0,0),pipeline_mode=pl.Buffered(1)), full((4,D,D)), full((4,D,D)), rows(D), rows(FF), rows(D), rows(D)],
        out_specs=[rows(D),rows(FF),rows(D),rows(D),rows(D),m3,pl.BlockSpec((16,D),lambda i:(0,0))],
        out_shape=[sd((T,D),bf),sd((T,FF),bf),sd((T,D),f32),sd((T,D),bf),sd((T,D),bf),sd((n,8,D),f32),sd((16,D),f32)],
        compiler_params=pltpu.CompilerParams(vmem_limit_bytes=VLIM),
        cost_estimate=pl.CostEstimate(flops=2*T*D*(2*FF+D), bytes_accessed=50_000_000, transcendentals=T*FF),
    )(g,mod,wa,w1,w2,down,upper,mid,attn)

def bwd_attn_kernel(gmix_ref, alow_ref, gmid_ref, mod_ref, wa_ref, qkv_ref, lse_ref, x_ref,
                    low_ref, gin_ref, dmod_ref, db_ref):
    i=pl.program_id(0)
    mod=lambda j: mod_ref[0, j:j+1, :]
    @pl.when(i==0)
    def _(): db_ref[...]=jnp.zeros_like(db_ref)
    s0=lambda v: jnp.sum(v,axis=0,keepdims=True)
    low_ref[:, 3*D:]=alow_ref[...]
    lo=half_masks()
    zero=jnp.zeros((TOK,128),bf)
    for hp in range(HEADS//2):
        c=hp*128
        q=qkv_ref[:, c:c+128]; k=qkv_ref[:, D+c:D+c+128]; v=qkv_ref[:, 2*D+c:2*D+c+128]
        gm=gmix_ref[:, c:c+128]
        res=[]
        for h in range(2):
            keep=lo if h==0 else jnp.logical_not(lo)
            qm=jnp.where(keep,q,zero); gmm=jnp.where(keep,gm,zero)
            s=mm_nt(qm,k)*(HDIM**-0.5)
            p=jnp.exp(s-lse_ref[:, 2*hp+h:2*hp+h+1])
            dp=mm_nt(gmm,v)
            ds=p*(dp-jnp.sum(p*dp,axis=-1,keepdims=True))
            dsl=ds.astype(bf)
            res.append((mm(dsl,k), mm_tn(dsl,q), mm_tn(p.astype(bf),gm)))
        for j in range(3):
            o=jnp.where(lo,res[0][j],res[1][j])
            if j<2: o=o*(HDIM**-0.5)
            ol=o.astype(bf)
            low_ref[:, j*D+c:j*D+c+128]=ol
            if j!=1:
                row=0 if j==0 else 1
                db_ref[row:row+1, c:c+128]+=s0(ol.astype(f32))
    gn=mm_nt(low_ref[:, :D], wa_ref[0])+mm_nt(low_ref[:, D:2*D], wa_ref[1])+mm_nt(low_ref[:, 2*D:3*D], wa_ref[2])
    xh,r=ln_parts(x_ref[...])
    dmod_ref[...]=jnp.zeros_like(dmod_ref)
    dmod_ref[0,0:1,:]=s0(gn)
    dmod_ref[0,1:2,:]=s0(gn*xh)
    gin_ref[...]=gmid_ref[...]+ln_back(gn,xh,r,mod(1))
def layer_bwd_attn(gmix, alow, gmid, mod, wa, qkv, lse, x):
    T=gmix.shape[0]; n=T//TOK
    sd=jax.ShapeDtypeStruct
    m3=pl.BlockSpec((1,8,D),lambda i:(i,0,0))
    return pl.pallas_call(bwd_attn_kernel, grid=(n,),
        in_specs=[rows(D),rows(D),rows(D),m3,full((3,D,D)),rows(3*D),rows(128),rows(D)],
        out_specs=[rows(4*D),rows(D),m3,pl.BlockSpec((8,D),lambda i:(0,0))],
        out_shape=[sd((T,4*D),bf),sd((T,D),f32),sd((n,8,D),f32),sd((8,D),f32)],
        compiler_params=pltpu.CompilerParams(vmem_limit_bytes=VLIM),
        cost_estimate=pl.CostEstimate(flops=2*T*D*(3*D+5*TOK), bytes_accessed=25_000_000, transcendentals=T*TOK*HEADS),
    )(gmix,alow,gmid,mod,wa,qkv,lse,x)

def gather_kernel(R, nz, U, w_ref, out_ref, zs, zr, xs, xr, cs, cr, ls):
    rep=lax.axis_index("rep"); shard=lax.axis_index("shard")
    z=shard//2; c=lax.rem(shard,2)
    dev=lambda r,zz,cc: (r, 2*zz+cc)
    MESH=pl.DeviceIdType.MESH
    bar=pltpu.get_barrier_semaphore()
    peers=[dev(rep, lax.rem(z+k,nz), c) for k in range(1,nz)]+[dev(jnp.bitwise_xor(rep,j), z, c) for j in range(1,R)]+[dev(rep,z,1-c)]
    for p in peers: pl.semaphore_signal(bar, inc=1, device_id=p, device_id_type=MESH)
    pl.semaphore_wait(bar, len(peers))
    def zcopy(u,k):
        return pltpu.make_async_remote_copy(src_ref=w_ref.at[u,rep], dst_ref=out_ref.at[u,rep,z,c], send_sem=zs.at[u,k-1], recv_sem=zr.at[u,k-1],
            device_id=dev(rep,lax.rem(z+k,nz),c), device_id_type=MESH)
    def xcopy(u,j,k):
        o=lax.rem(z-k+nz,nz)
        return pltpu.make_async_remote_copy(src_ref=out_ref.at[u,rep,o,c], dst_ref=out_ref.at[u,rep,o,c], send_sem=xs.at[u,j-1,k-1], recv_sem=xr.at[u,j-1,k-1],
            device_id=dev(jnp.bitwise_xor(rep,j),z,c), device_id_type=MESH)
    def ccopy(u,j):
        r=jnp.bitwise_xor(rep,j)
        return pltpu.make_async_remote_copy(src_ref=out_ref.at[u,r,:,c], dst_ref=out_ref.at[u,r,:,c], send_sem=cs.at[u,j], recv_sem=cr.at[u,j],
            device_id=dev(rep,z,1-c), device_id_type=MESH)
    locs=[pltpu.make_async_copy(w_ref.at[u], out_ref.at[u,:,z,c], ls.at[u]) for u in range(U)]
    for u in range(U):
        for k in range(1,nz): zcopy(u,k).start()
    for u in range(U): locs[u].start()
    for u in range(U):
        for k in range(1,nz):
            zcopy(u,k).wait_recv()
            for j in range(1,R): xcopy(u,j,k).start()
        locs[u].wait()
        ccopy(u,0).start()
    for u in range(U):
        for j in range(1,R):
            for k in range(1,nz): xcopy(u,j,k).wait_recv()
            ccopy(u,j).start()
    for u in range(U):
        for j in range(R): ccopy(u,j).wait()
        for k in range(1,nz): zcopy(u,k).wait_send()
        for j in range(1,R):
            for k in range(1,nz): xcopy(u,j,k).wait_send()

def gather_layer(w, R, S, cid):
    U,_,rows_,W=w.shape
    nz=S//2
    dma=pltpu.SemaphoreType.DMA
    any_=pl.BlockSpec(memory_space=pl.ANY)
    out=pl.pallas_call(functools.partial(gather_kernel,R,nz,U),
        in_specs=[any_], out_specs=any_, out_shape=jax.ShapeDtypeStruct((U,R,nz,2,rows_,W),bf),
        scratch_shapes=[dma((U,nz-1)),dma((U,nz-1)),dma((U,R-1,nz-1)),dma((U,R-1,nz-1)),dma((U,R)),dma((U,R)),dma((U,))],
        compiler_params=pltpu.CompilerParams(collective_id=cid, has_side_effects=True, vmem_limit_bytes=4*1024*1024),
    )(w)
    out=out.reshape(U,R,D,W)
    if R==4: return [out[u] for u in range(U)]
    m=R//4
    return [out[u].reshape(4,m,D,W).transpose(0,2,1,3).reshape(4,D,D) for u in range(U)]
CW=384; NCH=8
def bit_orders(R):
    bits=[1<<i for i in range(R.bit_length()-1)]
    return [bits[g%len(bits):]+bits[:g%len(bits)] if bits else [] for g in range(NCH//R)]
def grad_plan(R):
    orders=bit_orders(R); G=NCH//R; n=len(orders[0])
    def stage(g,m): return next(i for i,b in enumerate(orders[g]) if m&b)
    pos=[]
    for i in range(n+1):
        ms=[[m for m in range(R) if (m==0 and i==n) or (m and stage(g,m)==i)] for g in range(G)]
        if i<n: ms=[sorted(v,key=lambda m,g=g:(-bin(m).count("1"),m)) for g,v in enumerate(ms)]
        for a in range(len(ms[0])):
            for g in range(G): pos.append((g,ms[g][a],i))
    send={}; keep={}; recv={}
    for g,m,i in pos:
        if m: send[g,m]=len(send)
        if i>0 or m==0: keep[g,m]=len(keep)
    for i in range(n):
        for g in range(G):
            for m in range(R):
                if not any(m&b for b in orders[g][:i+1]): recv[g,i,m]=len(recv)
    return orders,n,pos,send,keep,recv

def grad_kernel(R,nz,own,T, xa,xb,xc,xd, da,db,dc, out_ref, xin,xt,dy,sbuf,obuf,rbuf,sb,rb,kf,zs,zr,az,
                xsem,dsem,csend,crecv,ssem,rsem,zss,zrs,ass,ars,als):
    orders,n,pos,send,keep,recv=grad_plan(R)
    G=NCH//R
    MESH=pl.DeviceIdType.MESH
    rep=lax.axis_index("rep"); shard=lax.axis_index("shard")
    z=shard//2; c=lax.rem(shard,2)
    xor=lambda m: jnp.bitwise_xor(rep,m)
    mate=(rep,2*z+1-c)
    zdev=lambda k: (rep, 2*lax.rem(z+k,nz)+c)
    rdev=lambda m: (xor(m), shard)
    bar=pltpu.get_barrier_semaphore()
    peers=[mate]+[zdev(k) for k in range(1,nz)]+[rdev(m) for m in range(1,R)]
    for p in peers: pl.semaphore_signal(bar,inc=1,device_id=p,device_id_type=MESH)
    xs=(xa,xb,xc,xd)
    xcopy=lambda i: pltpu.make_async_copy(xs[i],xin.at[i%2],xsem.at[i%2])
    chunk=lambda k: pos[k][0]*R+xor(pos[k][1])
    def dstart(u,k):
        for i,ref in enumerate((da,db,dc)):
            @pl.when(u==i)
            def _(): pltpu.make_async_copy(ref.at[:,pl.ds(pl.multiple_of(chunk(k)*CW,128),CW)],dy.at[k%4],dsem.at[k%4]).start()
    def dwait(k): pltpu.make_async_copy(da.at[:,pl.ds(0,CW)],dy.at[k%4],dsem.at[k%4]).wait()
    ccopy=lambda k: pltpu.make_async_remote_copy(src_ref=sbuf.at[k%2],dst_ref=rbuf.at[k%4],send_sem=csend.at[k%2],recv_sem=crecv.at[k%4],device_id=mate,device_id_type=MESH)
    def scopy(u,g,m):
        i=next(i for i,b in enumerate(orders[g]) if m&b); b=orders[g][i]
        a=send[g,m]; d=recv[g,i,m^b]
        return pltpu.make_async_remote_copy(src_ref=sb.at[u,a],dst_ref=rb.at[u,d],send_sem=ssem.at[u,a],recv_sem=rsem.at[u,d],device_id=rdev(b),device_id_type=MESH)
    def rwait(u,g,i,m):
        d=recv[g,i,m]
        pltpu.make_async_remote_copy(src_ref=sb.at[u,0],dst_ref=rb.at[u,d],send_sem=ssem.at[u,0],recv_sem=rsem.at[u,d],device_id=rdev(1),device_id_type=MESH).wait_recv()
    zcopy=lambda u,g,k: pltpu.make_async_remote_copy(src_ref=zs.at[u,g,lax.rem(z+k,nz)],dst_ref=zr.at[u,g,k-1],send_sem=zss.at[u,g,k-1],recv_sem=zrs.at[u,g,k-1],device_id=zdev(k),device_id_type=MESH)
    def acopy(u,g,m): return pltpu.make_async_remote_copy(src_ref=az.at[u,g],dst_ref=out_ref.at[u,g*R+rep],send_sem=ass.at[u,g,m-1],recv_sem=ars.at[u,g,m-1],device_id=rdev(m),device_id_type=MESH)
    alocal=lambda u,g: pltpu.make_async_copy(az.at[u,g],out_ref.at[u,g*R+rep],als.at[u,g])
    def arecv(u,g,m):
        return pltpu.make_async_remote_copy(src_ref=az.at[u,g],dst_ref=out_ref.at[u,g*R+xor(m)],send_sem=ass.at[u,g,m-1],recv_sem=ars.at[u,g,m-1],device_id=rdev(m),device_id_type=MESH)
    xcopy(0).start(); xcopy(1).start(); dstart(0,0); dstart(0,1)
    for i in range(4):
        xcopy(i).wait()
        xt[i]=xin[i%2].T
        if i+2<4: xcopy(i+2).start()
    pl.semaphore_wait(bar,len(peers))
    def consume(u,k):
        g,m,i=pos[k]
        ccopy(k).wait_recv()
        total=obuf[k%2]+rbuf[k%4]
        if i==0 and m:
            sb[u,send[g,m]]=total.astype(bf)
            scopy(u,g,m).start()
        else: kf[u,keep[g,m]]=total.reshape(nz,own,CW)
    def products(u):
        for k in range(NCH):
            if k+2<NCH: dstart(u,k+2)
            else:
                @pl.when(u<2)
                def _(): dstart(u+1,k+2-NCH)
            dwait(k)
            xi=u+(u//2)*(chunk(k)//6)
            p=mm(xt[xi],dy[k%4]).reshape(nz,2,own,CW)
            even=p[:,0].reshape(nz*own,CW); odd=p[:,1].reshape(nz*own,CW)
            if k>=2: ccopy(k).wait_send()
            else:
                @pl.when(u>0)
                def _(): ccopy(k).wait_send()
            sbuf[k%2]=jnp.where(c==0,odd,even)
            obuf[k%2]=jnp.where(c==0,even,odd)
            ccopy(k).start()
            if k>0: consume(u,k-1)
            else:
                @pl.when(u>0)
                def _(): consume(u-1,NCH-1)
    def middle(u,i):
        for g,m,j in pos:
            if m and j==i:
                v=kf[u,keep[g,m]].reshape(nz*own,CW)
                for i2 in range(i):
                    rwait(u,g,i2,m); v=v+rb[u,recv[g,i2,m]].astype(f32)
                sb[u,send[g,m]]=v.astype(bf)
                scopy(u,g,m).start()
    def along(u):
        for g in range(G):
            v=kf[u,keep[g,0]]
            for i2 in range(n):
                rwait(u,g,i2,0); v=v+rb[u,recv[g,i2,0]].astype(f32).reshape(nz,own,CW)
            kf[u,keep[g,0]]=v
            zs[u,g]=v.astype(bf)
            for k in range(1,nz): zcopy(u,g,k).start()
    def spread(u):
        for g in range(G):
            v=kf[u,keep[g,0],z]
            for k in range(1,nz):
                zcopy(u,g,k).wait_recv(); v=v+zr[u,g,k-1].astype(f32)
            az[u,g]=v
            alocal(u,g).start()
            for m in range(1,R): acopy(u,g,m).start()
    depth=max(n-1,0)
    def step(t,_):
        @pl.when(t<3)
        def _(): products(t)
        @pl.when(t==3)
        def _(): consume(2,NCH-1)
        for i in range(1,n):
            @pl.when(jnp.logical_and(t>=i,t<3+i))
            def _(): middle(t-i,i)
        @pl.when(jnp.logical_and(t>=1+depth,t<4+depth))
        def _(): along(t-1-depth)
        @pl.when(jnp.logical_and(t>=2+depth,t<5+depth))
        def _(): spread(t-2-depth)
        return 0
    lax.fori_loop(0,5+depth,step,0)
    def finish(u,_):
        for g in range(G):
            alocal(u,g).wait()
            for m in range(1,R): arecv(u,g,m).wait_recv(); acopy(u,g,m).wait_send()
            for k in range(1,nz): zcopy(u,g,k).wait_send()
            for m in range(1,R): scopy(u,g,m).wait_send()
        return 0
    lax.fori_loop(0,3,finish,0)
    ccopy(NCH-2).wait_send(); ccopy(NCH-1).wait_send()

def layer_grads(R,S,cid,xs,dys):
    T=xs[0].shape[0]; nz=S//2; own=D//S; G=NCH//R
    orders,n,pos,send,keep,recv=grad_plan(R)
    dma=pltpu.SemaphoreType.DMA; V=pltpu.VMEM
    any_=pl.BlockSpec(memory_space=pl.ANY)
    ns,nk,nr=max(len(send),1),len(keep),max(len(recv),1)
    return pl.pallas_call(functools.partial(grad_kernel,R,nz,own,T),
        in_specs=[any_]*7, out_specs=any_, out_shape=jax.ShapeDtypeStruct((3,NCH,own,CW),f32),
        scratch_shapes=[V((2,T,D),bf),V((4,D,T),bf),V((4,T,CW),bf),V((2,D//2,CW),f32),V((2,D//2,CW),f32),V((4,D//2,CW),f32),
            V((3,ns,D//2,CW),bf),V((3,nr,D//2,CW),bf),V((3,nk,nz,own,CW),f32),V((3,G,nz,own,CW),bf),V((3,G,nz-1,own,CW),bf),V((3,G,own,CW),f32),
            dma((2,)),dma((4,)),dma((2,)),dma((4,)),dma((3,ns)),dma((3,nr)),dma((3,G,nz-1)),dma((3,G,nz-1)),dma((3,G,R-1)),dma((3,G,R-1)),dma((3,G))],
        compiler_params=pltpu.CompilerParams(collective_id=cid,has_side_effects=True,vmem_limit_bytes=VLIM),
        cost_estimate=pl.CostEstimate(flops=2*T*D*9216,bytes_accessed=40_000_000,transcendentals=0),
    )(*xs,*dys)
LAYERS=2
beta_one=0.9; beta_two=0.999; adam_eps=1e-8; learn_rate=0.01; weight_decay=0.01; step_count=10.0
def adam_update(w,g,m,v,factor):
    s=g*factor
    m2=beta_one*m+(1.0-beta_one)*s
    v2=beta_two*v+(1.0-beta_two)*s*s
    mh=m2/(1.0-beta_one**step_count)
    vh=v2/(1.0-beta_two**step_count)
    w2=w-learn_rate*(mh/(jnp.sqrt(vh)+adam_eps)+weight_decay*w)
    return (w2,m2,v2,w2.astype(bf))
def inner_adam_kernel(f_ref,g0_ref,g1_ref,ada_ref,w_ref,m_ref,v_ref,*outs):
    factor=f_ref[0]; l=pl.program_id(0); j=pl.program_id(1)
    def put(sl,g):
        for o,val in zip(outs,adam_update(w_ref[0,:,sl],g,m_ref[0,:,sl],v_ref[0,:,sl],factor)): o[0,:,sl]=val
    for a in range(2):
        sl=slice(a*CW,(a+1)*CW)
        for layer,ref in enumerate((g0_ref,g1_ref)):
            @pl.when(jnp.logical_and(j<8,l==layer))
            def _(): put(sl,ref[0,a])
        @pl.when(j>=8)
        def _(): put(sl,ada_ref[0,:,sl])
def inner_adam(factor,g0,g1,ada,w,m,v):
    own=w.shape[1]; C=w.shape[2]; W=2*CW
    blk=pl.BlockSpec((1,own,W),lambda l,j:(l,0,j))
    def gmap(layer):
        def index(l,j):
            jj=jnp.minimum(j,7); on=jnp.where(l==layer,jj,7*(l>layer))
            return (2-on//4, on%4, 0, 0)
        return pl.BlockSpec((1,2,own,CW),index)
    sd=jax.ShapeDtypeStruct
    return pl.pallas_call(inner_adam_kernel,grid=(LAYERS,C//W),
        in_specs=[pl.BlockSpec(memory_space=pltpu.SMEM),gmap(0),gmap(1),pl.BlockSpec((1,own,W),lambda l,j:(l,0,jnp.maximum(j-8,0))),blk,blk,blk],
        out_specs=[blk]*4,out_shape=[sd(w.shape,f32)]*3+[sd(w.shape,bf)],
        compiler_params=pltpu.CompilerParams(vmem_limit_bytes=VLIM))(factor,g0,g1,ada,w,m,v)
def outer_adam_kernel(f_ref,g0_ref,g1_ref,b_ref,w_ref,m_ref,v_ref,*outs):
    factor=f_ref[0]; l=pl.program_id(0); j=pl.program_id(1)
    def put(sl,g):
        for o,val in zip(outs,adam_update(w_ref[0,sl],g,m_ref[0,sl],v_ref[0,sl],factor)): o[0,sl]=val
    for a in range(2):
        sl=slice(a*CW,(a+1)*CW)
        for layer,ref in enumerate((g0_ref,g1_ref)):
            @pl.when(jnp.logical_and(j<4,l==layer))
            def _(): put(sl,ref[0,a].T)
    @pl.when(j==4)
    def _(): put(slice(0,16),b_ref[0])
def outer_adam(factor,g0,g1,b,w,m,v):
    own=w.shape[2]; W=2*CW
    blk=pl.BlockSpec((1,W,own),lambda l,j:(l,j,0))
    def gmap(layer):
        def index(l,j):
            jj=jnp.minimum(j,3); on=jnp.where(l==layer,jj,3*(l>layer))
            return (0, on, 0, 0)
        return pl.BlockSpec((1,2,own,CW),index)
    sd=jax.ShapeDtypeStruct
    return pl.pallas_call(outer_adam_kernel,grid=(LAYERS,5),
        in_specs=[pl.BlockSpec(memory_space=pltpu.SMEM),gmap(0),gmap(1),pl.BlockSpec((1,16,own),lambda l,j:(l,0,0)),blk,blk,blk],
        out_specs=[blk]*4,out_shape=[sd(w.shape,f32)]*3+[sd(w.shape,bf)],
        compiler_params=pltpu.CompilerParams(vmem_limit_bytes=VLIM))(factor,g0,g1,b,w,m,v)
P_SIZE=16; GRID=16; LAYERS=2; LAT_DEV=4; FREQ=256; NCLASS=1000
clip_coef=2.5
BIAS=14
def position_table(grid_side, feature_width):
    quarter=feature_width//4
    omega=jnp.exp(-math.log(10000.0)*jnp.arange(quarter,dtype=f32)/quarter)
    ids=jnp.arange(grid_side*grid_side,dtype=jnp.int32)
    a=(ids%grid_side).astype(f32)[:,None]*omega[None,:]
    d=(ids//grid_side).astype(f32)[:,None]*omega[None,:]
    return jnp.concatenate([jnp.sin(a),jnp.cos(a),jnp.sin(d),jnp.cos(d)],axis=1)
def time_features(steps, count):
    half=count//2
    freq=jnp.exp(-math.log(10000.0)*jnp.arange(half,dtype=f32)/half)
    ang=steps.astype(f32)[:,None]*freq[None,:]
    return jnp.concatenate([jnp.cos(ang),jnp.sin(ang)],axis=1)
def modulate(x, sh, sc):
    c=x-jnp.mean(x,axis=-1,keepdims=True)
    v=jnp.mean(c*c,axis=-1,keepdims=True)
    return c*lax.rsqrt(v+norm_eps)*(1.0+sc[:,None,:])+sh[:,None,:]
def dot32(pattern,a,b): return jnp.einsum(pattern,a,b,preferred_element_type=f32)
def silu_back(v,g): return jax.vjp(jax.nn.silu,v)[1](g)[0]
ALL=("rep","shard")

def per_device(latents,target_noise,labels,time_steps,inner_weights,outer_weights,embed_table,final_mod,head_weights,
               inner_moment,inner_square,outer_moment,outer_square,embed_moment,embed_square,final_moment,final_square,head_moment,head_square):
    R=lax.axis_size("rep"); S=lax.axis_size("shard")
    rep=lax.axis_index("rep"); shard=lax.axis_index("shard")
    own=D//S; W=4*D//R; N=LAT_DEV*R*S; G=LAT_DEV*S
    count=N*TOK*P_SIZE
    inner_low=inner_weights.astype(bf); outer_low=outer_weights.astype(bf)
    gathered=[]
    for l in range(LAYERS):
        slab=jnp.stack([inner_low[l,:,:4*D],inner_low[l,:,4*D:8*D],outer_low[l,:FF].T])
        slab=slab.reshape(3,own,R,W).transpose(0,2,1,3)
        gathered.append(gather_layer(slab,R,S,l))
    embed_low=embed_table.astype(bf); final_low=final_mod.astype(bf); head_low=head_weights.astype(bf)
    small=jnp.concatenate([outer_low[:,FF:].reshape(LAYERS*BIAS,own),embed_low[:P_SIZE+1]],axis=0)
    small=lax.all_gather(small,"shard",axis=1,tiled=True)
    biases=small[:LAYERS*BIAS].reshape(LAYERS,BIAS,D).astype(f32)
    patch_w=small[LAYERS*BIAS:LAYERS*BIAS+P_SIZE]; patch_b=small[LAYERS*BIAS+P_SIZE].astype(f32)
    ids=lax.all_gather(jnp.stack([time_steps,labels],axis=1),ALL,axis=0,tiled=True)
    steps_all=ids[:,0]; labels_all=ids[:,1]
    r1=P_SIZE+1; r2=P_SIZE+2+FREQ; r3=P_SIZE+3+FREQ+D
    features=time_features(steps_all,FREQ).astype(bf)
    hidden=dot32("nf,fd->nd",features,embed_low[r1:r1+FREQ])+embed_low[r1+FREQ].astype(f32)
    act_own=jax.nn.silu(hidden).astype(bf)
    time_act=lax.all_gather(act_own,"shard",axis=1,tiled=True)
    hot=labels_all[:,None]==jnp.arange(NCLASS,dtype=jnp.int32)[None,:]
    condition=dot32("nd,de->ne",time_act,embed_low[r2:r2+D])+embed_low[r2+D].astype(f32)+dot32("nc,ce->ne",hot.astype(bf),embed_low[r3:])
    cond_own=jax.nn.silu(condition).astype(bf)
    cond_all=lax.all_gather(cond_own,"shard",axis=1,tiled=True)
    cond_group=lax.dynamic_slice_in_dim(cond_own,rep*G,G,0)
    ada_own=inner_low[:,:,4*D+FF:]
    part=dot32("gd,lde->gle",cond_group,ada_own)
    modul=lax.psum_scatter(part,"shard",scatter_dimension=0,tiled=True)
    modul=modul.reshape(LAT_DEV,LAYERS,6,D)+biases[:,7:13].reshape(1,LAYERS,6,D)
    modul=jnp.pad(modul.transpose(1,0,2,3),((0,0),(0,0),(0,2),(0,0)))
    fin_cols=2*D//S
    fin_part=dot32("gd,de->ge",lax.dynamic_slice_in_dim(cond_all,rep*G,G,0),final_low[:D])+final_low[D].astype(f32)
    fin_mod=lax.all_to_all(fin_part.reshape(S,LAT_DEV,fin_cols),"shard",0,0,tiled=True)
    fin_mod=fin_mod.reshape(S,LAT_DEV,fin_cols).transpose(1,0,2).reshape(LAT_DEV,2*D)
    ramp=0.0001+(0.02-0.0001)*jnp.arange(1000,dtype=f32)/999.0
    upto=jnp.arange(1000,dtype=jnp.int32)[None,:]<=time_steps[:,None]
    abar=jnp.exp(jnp.sum(jnp.where(upto,jnp.log(1.0-ramp)[None,:],0.0),axis=1))
    patches=(jnp.sqrt(abar)[:,None,None]*latents+jnp.sqrt(1.0-abar)[:,None,None]*target_noise).astype(bf)
    stream=dot32("gpt,pd->gtd",patches,patch_w)+patch_b+position_table(GRID,D)[None]
    stream=stream.reshape(LAT_DEV*TOK,D)
    saved=[]
    for l in range(LAYERS):
        wa,w1,w2=gathered[l]
        bias=jnp.pad(biases[l],((0,2),(0,0)))
        o=layer_fwd(stream,modul[l],bias,wa,w1,w2)
        saved.append((stream,)+tuple(o))
        stream=o[-1]
    stream3=stream.reshape(LAT_DEV,TOK,D)
    fin_shift,fin_scale=jnp.split(fin_mod,2,axis=1)
    fin_normed=modulate(stream3,fin_shift,fin_scale).astype(bf)
    output=dot32("gtd,dp->gtp",fin_normed,head_low[:D])+head_low[D].astype(f32)
    differ=output-jnp.swapaxes(target_noise,1,2)
    loss_part=jnp.sum(differ*differ)/count
    grad_output=2.0*(differ*(1.0/count))
    head_bias=jnp.sum(grad_output,axis=(0,1))
    output_low=grad_output.astype(bf)
    head_grad=jnp.concatenate([dot32("gtd,gtp->dp",fin_normed,output_low),head_bias[None]],axis=0)
    grad_fin_normed=dot32("gtp,dp->gtd",output_low,head_low[:D])
    grad_stream,g_shift,g_scale=jax.vjp(modulate,stream3,fin_shift,fin_scale)[1](grad_fin_normed)
    grad_stream=grad_stream.reshape(LAT_DEV*TOK,D)
    grad_fin=jnp.concatenate([g_shift,g_scale],axis=1)
    fin_rows=lax.all_gather(grad_fin.astype(bf),ALL,axis=0,tiled=True)
    fin_mine=lax.dynamic_slice_in_dim(fin_rows,shard*fin_cols,fin_cols,1)
    final_main=dot32("nd,ne->de",cond_all,fin_mine)
    grad_cond=lax.psum_scatter(dot32("ne,de->nd",fin_mine,final_low[:D]),"shard",scatter_dimension=1,tiled=True)
    ada_parts=[None]*LAYERS; bias_grads=[None]*LAYERS; operands=[None]*LAYERS
    for l in range(LAYERS-1,-1,-1):
        wa,w1,w2=gathered[l]
        x,normed,qkv,lse,mixed,attn,mid,ntwo,upper,activ,down,_=saved[l]
        dlow,ulow,gmid,alow,gmix,dm1,db1=layer_bwd_mlp(grad_stream,modul[l],wa,w1,w2,down,upper,mid,attn)
        low,grad_stream,dm2,db2=layer_bwd_attn(gmix,alow,gmid,modul[l],wa,qkv,lse,x)
        operands[l]=((dlow,ntwo,normed,mixed),(activ,ulow,low))
        dmod=jnp.concatenate([dm2[:,:2],dm1[:,2:6]],axis=1)
        rows_all=lax.all_gather(dmod.astype(bf).reshape(LAT_DEV,6*D),ALL,axis=0,tiled=True)
        ada_parts[l]=dot32("nd,ne->de",cond_own,rows_all)
        grad_cond=grad_cond+dot32("ne,de->nd",rows_all,ada_own[l])
        bias_grads[l]=jnp.concatenate([db2[0:2],db1[2:7],jnp.sum(dmod,axis=0),db1[13:14]],axis=0)
    ops1,grad_stream=lax.optimization_barrier((operands[1],grad_stream))
    grads1=layer_grads(R,S,LAYERS+1,*ops1)
    gs=grad_stream.reshape(LAT_DEV,TOK,D)
    patch_grad=dot32("gpt,gtd->pd",patches,gs.astype(bf))
    patch_bias=jnp.sum(grad_stream,axis=0)
    fin_bias=jnp.sum(grad_fin,axis=0).reshape(2,D)
    tail=jnp.zeros((1,D),f32).at[0,0].set(loss_part)
    head_flat=head_grad.reshape(-1)
    head_rows=-(-head_flat.shape[0]//D)
    head_flat=jnp.pad(head_flat,(0,head_rows*D-head_flat.shape[0])).reshape(head_rows,D)
    sums=lax.psum(jnp.concatenate(bias_grads+[patch_grad,patch_bias[None],fin_bias,head_flat,tail],axis=0),ALL)
    o1=LAYERS*BIAS; o2=o1+P_SIZE+1; o3=o2+2; o4=o3+head_rows
    mean_loss=sums[o4,0]
    head_total=sums[o3:o4].reshape(-1)[:(D+1)*P_SIZE].reshape(D+1,P_SIZE)
    fin_bias_own=lax.dynamic_slice_in_dim(sums[o2:o3].reshape(2*D),shard*fin_cols,fin_cols,0)
    mine=lax.dynamic_slice_in_dim(sums[:o2],shard*own,own,1)
    grad_cond,grads1=lax.optimization_barrier((grad_cond,grads1))
    grad_condition=silu_back(condition,grad_cond)
    b2=jnp.sum(grad_condition,axis=0)
    clow=grad_condition.astype(bf)
    second=dot32("nd,ne->de",time_act,clow)
    class_grad=jnp.einsum("nc,nd->cd",hot.astype(f32),grad_condition,precision=lax.Precision.HIGHEST)
    time_part=dot32("ne,de->nd",clow,embed_low[r2:r2+D])
    time_part,ops0=lax.optimization_barrier((time_part,operands[0]))
    grad_time_act=lax.psum_scatter(time_part,"shard",scatter_dimension=1,tiled=True)
    grads0=layer_grads(R,S,LAYERS,*ops0)
    grads0,grad_time_act=lax.optimization_barrier((grads0,grad_time_act))
    grad_time=silu_back(hidden,grad_time_act)
    first=dot32("nf,nd->fd",features,grad_time.astype(bf))
    embed_grad=jnp.concatenate([mine[o1:o2],first,jnp.sum(grad_time,axis=0)[None],second,b2[None],class_grad],axis=0)
    final_grad=jnp.concatenate([final_main,fin_bias_own[None]],axis=0)
    ada_grad=jnp.stack(ada_parts)
    bias_grad=jnp.pad(mine[:o1].reshape(LAYERS,BIAS,own),((0,0),(0,2),(0,0)))
    sq=lambda a: jnp.sum(a*a)
    square=lax.psum(sq(grads0)+sq(grads1)+sq(ada_grad)+sq(bias_grad)+sq(embed_grad)+sq(final_grad),"shard")
    grad_norm=jnp.sqrt(square+sq(head_total))
    factor=jnp.minimum(1.0,clip_coef*math.sqrt(D/count)/grad_norm)
    out=[mean_loss,grad_norm]
    out.extend(inner_adam(factor.reshape(1),grads0,grads1,ada_grad,inner_weights,inner_moment,inner_square))
    out.extend(outer_adam(factor.reshape(1),grads0,grads1,bias_grad,outer_weights,outer_moment,outer_square))
    for w,g,m,v in ((embed_table,embed_grad,embed_moment,embed_square),(final_mod,final_grad,final_moment,final_square),
                    (head_weights,head_total,head_moment,head_square)):
        out.extend(adam_update(w,g,m,v,factor))
    return tuple(out)

def solution(mesh):
    lat=P(ALL,None,None); one=P(ALL); inn=P(None,"shard",None); oute=P(None,None,"shard"); col=P(None,"shard")
    in_specs=(lat,lat,one,one,inn,oute,col,col,P(),inn,inn,oute,oute,col,col,col,col,P(),P())
    out_specs=(P(),P())+(inn,)*4+(oute,)*4+(col,)*8+(P(),)*4
    return jax.shard_map(per_device,mesh=mesh,in_specs=in_specs,out_specs=out_specs,check_vma=False)
```

```python
from jax.sharding import PartitionSpec as P
import functools, math
import jax, jax.numpy as jnp
from jax import lax
from jax.experimental import pallas as pl
from jax.experimental.pallas import tpu as pltpu
D=768; HEADS=12; HDIM=64; FF=3072; TOK=256
norm_eps=1e-6
bf=jnp.bfloat16; f32=jnp.float32
VLIM=60*1024*1024
def mm(a,b): return lax.dot_general(a,b,(((1,),(0,)),((),())),preferred_element_type=f32)
def mm_nt(a,b): return lax.dot_general(a,b,(((1,),(1,)),((),())),preferred_element_type=f32)
def mm_tn(a,b): return lax.dot_general(a,b,(((0,),(0,)),((),())),preferred_element_type=f32)
def ln_parts(x):
    c=x-jnp.mean(x,axis=-1,keepdims=True)
    r=lax.rsqrt(jnp.mean(c*c,axis=-1,keepdims=True)+norm_eps)
    return c*r, r
def ln_back(dy, xhat, r, sc):
    dxh=dy*(1.0+sc)
    m1=jnp.mean(dxh,axis=-1,keepdims=True); m2=jnp.mean(dxh*xhat,axis=-1,keepdims=True)
    return r*(dxh-m1-xhat*m2)
def half_masks():
    lane=lax.broadcasted_iota(jnp.int32,(1,128),1)
    lo=(lane<HDIM)
    return lo
C0=math.sqrt(2.0/math.pi); C1=0.044715

def fwd_kernel(x_ref, mod_ref, bias_ref, wa_ref, w1_ref, w2_ref,
               normed_ref, qkv_ref, lse_ref, mixed_ref, attn_ref, mid_ref, ntwo_ref, upper_ref, activ_ref, down_ref, out_ref, hook=lambda p: None):
    hook(0)
    x=x_ref[...]
    mod=lambda j: mod_ref[0, j:j+1, :]
    bias=lambda j: bias_ref[j:j+1, :]
    xh,_=ln_parts(x)
    normed=(xh*(1.0+mod(1))+mod(0)).astype(bf)
    normed_ref[...]=normed
    qkv_ref[:, :D]=(mm(normed, wa_ref[0])+bias(0)).astype(bf)
    qkv_ref[:, D:2*D]=mm(normed, wa_ref[1]).astype(bf)
    qkv_ref[:, 2*D:]=(mm(normed, wa_ref[2])+bias(1)).astype(bf)
    lo=half_masks()
    for hp in range(HEADS//2):
        hook(1+hp)
        c=hp*128
        q=qkv_ref[:, c:c+128]; k=qkv_ref[:, D+c:D+c+128]; v=qkv_ref[:, 2*D+c:2*D+c+128]
        outs=[]
        for h in range(2):
            keep=lo if h==0 else jnp.logical_not(lo)
            qm=jnp.where(keep, q, jnp.zeros_like(q))
            s=mm_nt(qm,k)*(HDIM**-0.5)
            m=jnp.max(s,axis=-1,keepdims=True)
            e=jnp.exp(s-m)
            l=jnp.sum(e,axis=-1,keepdims=True)
            p=(e*(1.0/l)).astype(bf)
            lse_ref[:, 2*hp+h:2*hp+h+1]=m+jnp.log(l)
            outs.append(mm(p,v))
        mixed_ref[:, c:c+128]=jnp.where(lo, outs[0], outs[1]).astype(bf)
    hook(7)
    attn=mm(mixed_ref[...], wa_ref[3])+bias(2)
    attn_ref[...]=attn
    mid=x+mod(2)*attn
    mid_ref[...]=mid
    xh2,_=ln_parts(mid)
    ntwo=(xh2*(1.0+mod(4))+mod(3)).astype(bf)
    ntwo_ref[...]=ntwo
    down=jnp.broadcast_to(bias(13),(TOK,D))
    for j in range(4):
        hook(8+j)
        up=mm(ntwo, w1_ref[j])+bias(3+j)
        upper_ref[:, j*D:(j+1)*D]=up
        t=jnp.tanh(C0*(up+C1*(up*up*up)))
        act=(0.5*up*(1.0+t)).astype(bf)
        activ_ref[:, j*D:(j+1)*D]=act
        down=down+mm_nt(act, w2_ref[j])
    down_ref[...]=down
    out_ref[...]=mid_ref[...]+mod(5)*down

def full(shape):
    n=len(shape)
    return pl.BlockSpec(shape, lambda i: (0,)*n, pipeline_mode=pl.Buffered(1))
def rows(width): return pl.BlockSpec((TOK,width), lambda i:(i,0))
def layer_fwd(x, mod, bias, wa, w1, w2):
    T=x.shape[0]; n=T//TOK
    sd=jax.ShapeDtypeStruct
    widths=[(D,bf),(3*D,bf),(128,f32),(D,bf),(D,f32),(D,f32),(D,bf),(FF,f32),(FF,bf),(D,f32),(D,f32)]
    return pl.pallas_call(fwd_kernel, grid=(n,),
        in_specs=[rows(D), pl.BlockSpec((1,8,D),lambda i:(i,0,0)), full((16,D)), full((4,D,D)), full((4,D,D)), full((4,D,D))],
        out_specs=[rows(w) for w,_ in widths],
        out_shape=[sd((T,w),t) for w,t in widths],
        compiler_params=pltpu.CompilerParams(vmem_limit_bytes=VLIM),
        cost_estimate=pl.CostEstimate(flops=2*T*(9216*D+2*TOK*D), bytes_accessed=60_000_000, transcendentals=T*FF*2),
    )(x,mod,bias,wa,w1,w2)

def bwd_mlp_kernel(g_ref, mod_ref, wa3_ref, w1_ref, w2_ref, down_ref, upper_ref, mid_ref, attn_ref,
                   dlow_ref, ulow_ref, gmid_ref, alow_ref, gmix_ref, dmod_ref, db_ref):
    i=pl.program_id(0)
    mod=lambda j: mod_ref[0, j:j+1, :]
    g=g_ref[...]
    gd=g*mod(5)
    dl=gd.astype(bf)
    dlow_ref[...]=dl
    @pl.when(i==0)
    def _(): db_ref[...]=jnp.zeros_like(db_ref)
    s0=lambda v: jnp.sum(v,axis=0,keepdims=True)
    dmod_ref[0,5:6,:]=s0(g*down_ref[...])
    db_ref[13:14,:]+=s0(gd)
    gn=jnp.zeros((TOK,D),f32)
    for j in range(4):
        ga=mm(dl, w2_ref[j])
        up=upper_ref[:, j*D:(j+1)*D]
        u2=up*up
        t=jnp.tanh(C0*(up+C1*(u2*up)))
        gu=ga*(0.5*(1.0+t)+(0.5*C0)*up*(1.0-t*t)*(1.0+(3.0*C1)*u2))
        db_ref[3+j:4+j,:]+=s0(gu)
        ul=gu.astype(bf)
        ulow_ref[:, j*D:(j+1)*D]=ul
        gn=gn+mm_nt(ul, w1_ref[j])
    xh,r=ln_parts(mid_ref[...])
    dmod_ref[0,3:4,:]=s0(gn)
    dmod_ref[0,4:5,:]=s0(gn*xh)
    gm=g_ref[...]+ln_back(gn,xh,r,mod(4))
    gmid_ref[...]=gm
    ga=gm*mod(2)
    dmod_ref[0,2:3,:]=s0(gm*attn_ref[...])
    db_ref[2:3,:]+=s0(ga)
    al=ga.astype(bf)
    alow_ref[...]=al
    gmix_ref[...]=mm_nt(al, wa3_ref[0]).astype(bf)
def layer_bwd_mlp(g, mod, wa, w1, w2, down, upper, mid, attn):
    T=g.shape[0]; n=T//TOK
    sd=jax.ShapeDtypeStruct
    m3=pl.BlockSpec((1,8,D),lambda i:(i,0,0))
    return pl.pallas_call(bwd_mlp_kernel, grid=(n,),
        in_specs=[rows(D), m3, pl.BlockSpec((1,D,D),lambda i:(3,0,0),pipeline_mode=pl.Buffered(1)), full((4,D,D)), full((4,D,D)), rows(D), rows(FF), rows(D), rows(D)],
        out_specs=[rows(D),rows(FF),rows(D),rows(D),rows(D),m3,pl.BlockSpec((16,D),lambda i:(0,0))],
        out_shape=[sd((T,D),bf),sd((T,FF),bf),sd((T,D),f32),sd((T,D),bf),sd((T,D),bf),sd((n,8,D),f32),sd((16,D),f32)],
        compiler_params=pltpu.CompilerParams(vmem_limit_bytes=VLIM),
        cost_estimate=pl.CostEstimate(flops=2*T*D*(2*FF+D), bytes_accessed=50_000_000, transcendentals=T*FF),
    )(g,mod,wa,w1,w2,down,upper,mid,attn)

def bwd_attn_kernel(gmix_ref, alow_ref, gmid_ref, mod_ref, wa_ref, qkv_ref, lse_ref, x_ref,
                    low_ref, gin_ref, dmod_ref, db_ref):
    i=pl.program_id(0)
    mod=lambda j: mod_ref[0, j:j+1, :]
    @pl.when(i==0)
    def _(): db_ref[...]=jnp.zeros_like(db_ref)
    s0=lambda v: jnp.sum(v,axis=0,keepdims=True)
    low_ref[:, 3*D:]=alow_ref[...]
    lo=half_masks()
    zero=jnp.zeros((TOK,128),bf)
    for hp in range(HEADS//2):
        c=hp*128
        q=qkv_ref[:, c:c+128]; k=qkv_ref[:, D+c:D+c+128]; v=qkv_ref[:, 2*D+c:2*D+c+128]
        gm=gmix_ref[:, c:c+128]
        res=[]
        for h in range(2):
            keep=lo if h==0 else jnp.logical_not(lo)
            qm=jnp.where(keep,q,zero); gmm=jnp.where(keep,gm,zero)
            s=mm_nt(qm,k)*(HDIM**-0.5)
            p=jnp.exp(s-lse_ref[:, 2*hp+h:2*hp+h+1])
            dp=mm_nt(gmm,v)
            ds=p*(dp-jnp.sum(p*dp,axis=-1,keepdims=True))
            dsl=ds.astype(bf)
            res.append((mm(dsl,k), mm_tn(dsl,q), mm_tn(p.astype(bf),gm)))
        for j in range(3):
            o=jnp.where(lo,res[0][j],res[1][j])
            if j<2: o=o*(HDIM**-0.5)
            ol=o.astype(bf)
            low_ref[:, j*D+c:j*D+c+128]=ol
            if j!=1:
                row=0 if j==0 else 1
                db_ref[row:row+1, c:c+128]+=s0(ol.astype(f32))
    gn=mm_nt(low_ref[:, :D], wa_ref[0])+mm_nt(low_ref[:, D:2*D], wa_ref[1])+mm_nt(low_ref[:, 2*D:3*D], wa_ref[2])
    xh,r=ln_parts(x_ref[...])
    dmod_ref[...]=jnp.zeros_like(dmod_ref)
    dmod_ref[0,0:1,:]=s0(gn)
    dmod_ref[0,1:2,:]=s0(gn*xh)
    gin_ref[...]=gmid_ref[...]+ln_back(gn,xh,r,mod(1))
def layer_bwd_attn(gmix, alow, gmid, mod, wa, qkv, lse, x):
    T=gmix.shape[0]; n=T//TOK
    sd=jax.ShapeDtypeStruct
    m3=pl.BlockSpec((1,8,D),lambda i:(i,0,0))
    return pl.pallas_call(bwd_attn_kernel, grid=(n,),
        in_specs=[rows(D),rows(D),rows(D),m3,full((3,D,D)),rows(3*D),rows(128),rows(D)],
        out_specs=[rows(4*D),rows(D),m3,pl.BlockSpec((8,D),lambda i:(0,0))],
        out_shape=[sd((T,4*D),bf),sd((T,D),f32),sd((n,8,D),f32),sd((8,D),f32)],
        compiler_params=pltpu.CompilerParams(vmem_limit_bytes=VLIM),
        cost_estimate=pl.CostEstimate(flops=2*T*D*(3*D+5*TOK), bytes_accessed=25_000_000, transcendentals=T*TOK*HEADS),
    )(gmix,alow,gmid,mod,wa,qkv,lse,x)

MESH=pl.DeviceIdType.MESH
class Gather:
    def __init__(self,R,nz,U,w_ref,out_ref,zs,zr,xs,xr,cs,cr,ls):
        self.R,self.nz,self.U=R,nz,U
        self.w,self.out=w_ref,out_ref
        self.zs,self.zr,self.xs,self.xr,self.cs,self.cr,self.ls=zs,zr,xs,xr,cs,cr,ls
        self.rep=lax.axis_index("rep"); self.shard=lax.axis_index("shard")
        self.z=self.shard//2; self.c=lax.rem(self.shard,2)
        self.relay=R==4
    def at(self,m,z,other=False): return (jnp.bitwise_xor(self.rep,m), 2*z+(1-self.c if other else self.c))
    def peers(self):
        return [self.at(0,lax.rem(self.z+k,self.nz)) for k in range(1,self.nz)]+[self.at(m,self.z) for m in range(1,self.R)]+[self.at(0,self.z,True)]
    def copy(self,src,dst,s,r,dev): return pltpu.make_async_remote_copy(src_ref=src,dst_ref=dst,send_sem=s,recv_sem=r,device_id=dev,device_id_type=MESH)
    def along(self,u,o,up):
        b=self.out.at[u,self.rep,o,self.c]
        return self.copy(b,b,self.zs.at[u,o,1 if up else 0],self.zr.at[u,o],self.at(0,self.z+(1 if up else -1)))
    def own(self,u,up):
        return self.copy(self.w.at[u,self.rep],self.out.at[u,self.rep,self.z,self.c],self.zs.at[u,self.z,1 if up else 0],self.zr.at[u,self.z],self.at(0,self.z+(1 if up else -1)))
    def across(self,u,o,m,q,to):
        b=self.out.at[u,jnp.bitwise_xor(self.rep,q),o,self.c]
        return self.copy(b,b,self.xs.at[u,m-1,o],self.xr.at[u,m-1,o],self.at(to,self.z))
    def swap(self,u,m):
        b=self.out.at[u,jnp.bitwise_xor(self.rep,m),:,self.c]
        return self.copy(b,b,self.cs.at[u,m],self.cr.at[u,m],self.at(0,self.z,True))
    def local(self,u): return pltpu.make_async_copy(self.w.at[u],self.out.at[u,:,self.z,self.c],self.ls.at[u])
    def start(self):
        for u in range(self.U):
            @pl.when(self.z<self.nz-1)
            def _(): self.own(u,True).start()
            @pl.when(self.z>0)
            def _(): self.own(u,False).start()
        for u in range(self.U): self.local(u).start()
    def sides(self,h):
        z,nz=self.z,self.nz
        return ((z>=h,z-h,True,z<nz-1),(z+h<nz,z+h,False,z>0))
    def arrive(self,h,u):
        for there,o,up,more in self.sides(h):
            @pl.when(there)
            def _():
                self.along(u,o,up).wait_recv()
                @pl.when(more)
                def _(): self.along(u,o,up).start()
                for m in range(1,self.R):
                    if not (self.relay and m==3): self.across(u,o,m,0,m).start()
    def pass_on(self,h,u):
        if not self.relay: return
        for there,o,up,more in self.sides(h):
            for par,(q,to) in enumerate(((1,2),(2,1))):
                @pl.when(jnp.logical_and(there,lax.rem(u+o+self.nz,2)==par))
                def _():
                    self.across(u,o,q,0,q).wait_recv()
                    self.across(u,o,3,q,to).start()
    def swap_own(self,u):
        self.local(u).wait(); self.swap(u,0).start()
    def swap_block(self,u,m):
        for o in range(self.nz):
            seen=self.relay and m<3
            cond=o!=self.z
            if seen: cond=jnp.logical_and(cond,(u+o+self.nz)%2!=m-1)
            if seen and (u+o+self.nz)%2==m-1: continue
            @pl.when(o!=self.z)
            def _(): self.across(u,o,m,0,m).wait_recv()
        self.swap(u,m).start()
    def ticks(self):
        U,nz=self.U,self.nz
        order=[(h,u) for h in range(1,nz) for u in range(U)]
        out=[]
        for i in range(len(order)+U):
            if i<len(order): out.append(functools.partial(self.arrive,*order[i]))
            if i>=U: out.append(functools.partial(self.pass_on,*order[i-U]))
            if i>=len(order): out.append(functools.partial(self.swap_own,i-len(order)))
        for u in range(U):
            for m in range(1,self.R): out.append(functools.partial(self.swap_block,u,m))
        return out
    def finish(self):
        for u in range(self.U):
            for m in range(self.R): self.swap(u,m).wait()
            @pl.when(self.z<self.nz-1)
            def _(): self.own(u,True).wait_send()
            @pl.when(self.z>0)
            def _(): self.own(u,False).wait_send()
            for h in range(1,self.nz):
                for there,o,up,more in self.sides(h):
                    @pl.when(there)
                    def _():
                        @pl.when(more)
                        def _(): self.along(u,o,up).wait_send()
                        for m in range(1,self.R): self.across(u,o,m,0,m).wait_send()
def gather_sems(R,nz,U):
    dma=pltpu.SemaphoreType.DMA
    return [dma((U,nz,2)),dma((U,nz)),dma((U,R-1,nz)),dma((U,R-1,nz)),dma((U,R)),dma((U,R)),dma((U,))]
def unit_blocks(out,R):
    U=out.shape[0]; W=out.shape[-1]
    out=out.reshape(U,R,D,W)
    if R==4: return [out[u] for u in range(U)]
    m=R//4
    return [out[u].reshape(4,m,D,W).transpose(0,2,1,3).reshape(4,D,D) for u in range(U)]
def meet(peers):
    bar=pltpu.get_barrier_semaphore()
    for p in peers: pl.semaphore_signal(bar,inc=1,device_id=p,device_id_type=MESH)
    pl.semaphore_wait(bar,len(peers))

def first_kernel(R,nz,U,own, w_ref,fo_ref,sm_ref,t1_ref,t2_ref,cls_ref,tb_ref,ada_ref,fin_ref,finb_ref,
                 out_ref,f_ref,sg_ref,hid_ref,act_ref,con_ref,call_ref,mod_ref,fm_ref,
                 cgs,pm,mr,ps,zrv,fps, fs1,fr1,fs2,fr2,ss,sr,as_,ar,cs_,cr_,ms,mrs,pz,pzr,vs,vr, *gsems):
    S=2*nz; NP=S*R*8
    ga=Gather(R,nz,U,w_ref,out_ref,*gsems)
    rep=lax.axis_index("rep"); shard=lax.axis_index("shard"); z=shard//2; c=lax.rem(shard,2)
    rpeer=lambda m: (jnp.bitwise_xor(rep,m),shard)
    speer=lambda k: (rep,lax.rem(shard+k,S))
    mate=(rep,2*z+1-c)
    peers=[rpeer(m) for m in range(1,R)]+[speer(k) for k in range(1,S)]
    def send(src,dst,s,r,dev): return pltpu.make_async_remote_copy(src_ref=src,dst_ref=dst,send_sem=s,recv_sem=r,device_id=dev,device_id_type=MESH)
    meet(peers)
    f1=lambda m: send(fo_ref,f_ref.at[shard,rep],fs1.at[m-1],fr1.at[m-1],rpeer(m))
    for m in range(1,R): f1(m).start()
    smc=lambda k: send(sm_ref,sg_ref.at[shard],ss.at[k-1],sr.at[k-1],speer(k))
    ga.start(); ticks=ga.ticks()
    f_ref[shard,rep]=fo_ref[...]
    sg_ref[shard]=sm_ref[...]
    for m in range(1,R): f1(m).wait_recv()
    f2=lambda k: send(f_ref.at[shard],f_ref.at[shard],fs2.at[k-1],fr2.at[k-1],speer(k))
    for k in range(1,S): f2(k).start()
    for k in range(1,S): smc(k).start()
    for t in ticks[:U]: t()
    for k in range(1,S): f2(k).wait_recv()
    feats=f_ref[...].reshape(NP,384)
    hidden=mm_nt(feats[:,:256].astype(bf),t1_ref[...])+tb_ref[0:1,:]
    hid_ref[...]=hidden
    act_ref[shard]=(hidden/(1.0+jnp.exp(-hidden))).astype(bf)
    ac=lambda k: send(act_ref.at[shard],act_ref.at[shard],as_.at[k-1],ar.at[k-1],speer(k))
    for k in range(1,S): ac(k).start()
    hot=(feats[:,256:257].astype(jnp.int32)==lax.broadcasted_iota(jnp.int32,(1,cls_ref.shape[1]),1))
    con=mm_nt(jnp.where(hot,1.0,0.0).astype(bf),cls_ref[...])
    for t in ticks[U:2*U]: t()
    for k in range(1,S): ac(k).wait_recv()
    sec=mm_nt(act_ref[0],t2_ref[0])
    for s in range(1,S): sec=sec+mm_nt(act_ref[s],t2_ref[s])
    con=(sec+tb_ref[1:2,:])+con
    con_ref[...]=con
    cond=con/(1.0+jnp.exp(-con))
    call_ref[shard]=cond.astype(bf)
    cc=lambda k: send(call_ref.at[shard],call_ref.at[shard],cs_.at[k-1],cr_.at[k-1],speer(k))
    for k in range(1,S): cc(k).start()
    cgs[...]=cond.reshape(S,R,8,own)
    cg=cgs[:,rep].reshape(S*8,own).astype(bf)
    first=lax.rem(lax.broadcasted_iota(jnp.int32,(S*8,1),0),8)<4
    for b in range(6):
        sl=slice(b*D,(b+1)*D)
        v=jnp.where(first,mm(cg,ada_ref[0,:,sl]),mm(cg,ada_ref[1,:,sl]))
        pm[:,:,:,sl]=v.reshape(nz,2,8,D)
    mc=send(pm.at[:,1-c],mr,ms,mrs,mate)
    mc.start()
    for t in ticks[2*U:4*U]: t()
    mc.wait_recv()
    ps[...]=pm[:,c]+mr[...]
    zc=lambda k: send(ps.at[lax.rem(z+k,nz)],zrv.at[k-1],pz.at[k-1],pzr.at[k-1],(rep,2*lax.rem(z+k,nz)+c))
    for k in range(1,nz): zc(k).start()
    for k in range(1,S): cc(k).wait_recv()
    fp=mm(call_ref[0],fin_ref[0])
    for s in range(1,S): fp=fp+mm(call_ref[s],fin_ref[s])
    fps[...]=(fp+finb_ref[0:1,:]).reshape(S,R,8,fin_ref.shape[2])
    vc=lambda k: send(fps.at[lax.rem(shard+k,S),rep],fm_ref.at[shard],vs.at[k-1],vr.at[k-1],speer(k))
    for k in range(1,S): vc(k).start()
    fm_ref[shard]=fps[shard,rep]
    for t in ticks[4*U:]: t()
    total=ps[z]
    for k in range(1,nz): zc(k).wait_recv(); total=total+zrv[k-1]
    mod_ref[...]=total
    for k in range(1,S): vc(k).wait_recv(); smc(k).wait_recv()
    for m in range(1,R): f1(m).wait_send()
    for k in range(1,S):
        for cp in (f2,smc,ac,cc,vc): cp(k).wait_send()
    mc.wait_send()
    for k in range(1,nz): zc(k).wait_send()
    ga.finish()

def first_call(w,fo,sm,t1,t2,cls,tb,ada,fin,finb,R,S,cid):
    U,_,own,W=w.shape; nz=S//2; NP=S*R*8; FC=fin.shape[2]
    dma=pltpu.SemaphoreType.DMA; V=pltpu.VMEM; sd=jax.ShapeDtypeStruct
    any_=pl.BlockSpec(memory_space=pl.ANY); vm=pl.BlockSpec(memory_space=pltpu.VMEM)
    return pl.pallas_call(functools.partial(first_kernel,R,nz,U,own),
        in_specs=[vm]*10, out_specs=[any_]+[vm]*8,
        out_shape=[sd((U,R,nz,2,own,W),bf),sd((S,R,8,384),f32),sd((S,)+sm.shape,bf),sd((NP,own),f32),sd((S,NP,own),bf),sd((NP,own),f32),sd((S,NP,own),bf),sd((8,6*D),f32),sd((S,8,FC),f32)],
        scratch_shapes=[V((S,R,8,own),f32),V((nz,2,8,6*D),f32),V((nz,8,6*D),f32),V((nz,8,6*D),f32),V((max(nz-1,1),8,6*D),f32),V((S,R,8,FC),f32),
            dma((R-1,)),dma((R-1,))]+[dma((S-1,))]*8+[dma(()),dma(()),dma((nz-1,)),dma((nz-1,)),dma((S-1,)),dma((S-1,))]+gather_sems(R,nz,U),
        compiler_params=pltpu.CompilerParams(collective_id=cid,has_side_effects=True,vmem_limit_bytes=VLIM),
    )(w,fo,sm,t1,t2,cls,tb,ada,fin,finb)

def fwd_gather_kernel(R,nz,U,x_ref,mod_ref,bias_ref,wa_ref,w1_ref,w2_ref,w_ref,*rest):
    outs=rest[:11]; out_ref=rest[11]; gsems=rest[12:]
    i=pl.program_id(0); last=pl.num_programs(0)-1
    ga=Gather(R,nz,U,w_ref,out_ref,*gsems)
    @pl.when(i==0)
    def _():
        meet(ga.peers()); ga.start()
    ticks=ga.ticks(); used=set()
    def hook(p):
        for step in range(4):
            n=12*step+p-6
            if n>=0 and n%2==0 and n//2<len(ticks):
                used.add(n//2)
                pl.when(i==step)(ticks[n//2])
    fwd_kernel(x_ref,mod_ref,bias_ref,wa_ref,w1_ref,w2_ref,*outs,hook=hook)
    @pl.when(i==last)
    def _():
        for n,t in enumerate(ticks):
            if n not in used: t()
        ga.finish()
FWD_WIDTHS=[(D,bf),(3*D,bf),(128,f32),(D,bf),(D,f32),(D,f32),(D,bf),(FF,f32),(FF,bf),(D,f32),(D,f32)]
def layer_fwd_gather(x,mod,bias,wa,w1,w2,w,R,S,cid):
    T=x.shape[0]; n=T//TOK; U,_,own,W=w.shape; nz=S//2
    sd=jax.ShapeDtypeStruct
    any_=pl.BlockSpec(memory_space=pl.ANY)
    o=pl.pallas_call(functools.partial(fwd_gather_kernel,R,nz,U),grid=(n,),
        in_specs=[rows(D),pl.BlockSpec((1,8,D),lambda i:(i,0,0)),full((16,D)),full((4,D,D)),full((4,D,D)),full((4,D,D)),pl.BlockSpec(memory_space=pltpu.VMEM)],
        out_specs=[rows(v) for v,_ in FWD_WIDTHS]+[any_],
        out_shape=[sd((T,v),t) for v,t in FWD_WIDTHS]+[sd((U,R,nz,2,own,W),bf)],
        scratch_shapes=gather_sems(R,nz,U),
        compiler_params=pltpu.CompilerParams(collective_id=cid,has_side_effects=True,vmem_limit_bytes=VLIM),
        cost_estimate=pl.CostEstimate(flops=2*T*(9216*D+2*TOK*D),bytes_accessed=60_000_000,transcendentals=T*FF*2),
    )(x,mod,bias,wa,w1,w2,w)
    return o[:11],o[11]
CW=384; NCH=8
def bit_orders(R):
    bits=[1<<i for i in range(R.bit_length()-1)]
    return [bits[g%len(bits):]+bits[:g%len(bits)] if bits else [] for g in range(NCH//R)]
def grad_plan(R):
    orders=bit_orders(R); G=NCH//R; n=len(orders[0])
    def stage(g,m): return next(i for i,b in enumerate(orders[g]) if m&b)
    pos=[]
    for i in range(n+1):
        ms=[[m for m in range(R) if (m==0 and i==n) or (m and stage(g,m)==i)] for g in range(G)]
        if i<n: ms=[sorted(v,key=lambda m,g=g:(-bin(m).count("1"),m)) for g,v in enumerate(ms)]
        for a in range(len(ms[0])):
            for g in range(G): pos.append((g,ms[g][a],i))
    send={}; keep={}; recv={}
    for g,m,i in pos:
        if m: send[g,m]=len(send)
        if i>0 or m==0: keep[g,m]=len(keep)
    for i in range(n):
        for g in range(G):
            for m in range(R):
                if not any(m&b for b in orders[g][:i+1]): recv[g,i,m]=len(recv)
    return orders,n,pos,send,keep,recv

def grad_kernel(R,nz,own,T, xa,xb,xc,xd, da,db,dc, out_ref, xin,xt,dy,sbuf,obuf,rbuf,sb,rb,kf,zs,zr,az,
                xsem,dsem,csend,crecv,ssem,rsem,zss,zrs,ass,ars,als):
    orders,n,pos,send,keep,recv=grad_plan(R)
    G=NCH//R
    MESH=pl.DeviceIdType.MESH
    rep=lax.axis_index("rep"); shard=lax.axis_index("shard")
    z=shard//2; c=lax.rem(shard,2)
    xor=lambda m: jnp.bitwise_xor(rep,m)
    mate=(rep,2*z+1-c)
    zdev=lambda k: (rep, 2*lax.rem(z+k,nz)+c)
    rdev=lambda m: (xor(m), shard)
    bar=pltpu.get_barrier_semaphore()
    peers=[mate]+[zdev(k) for k in range(1,nz)]+[rdev(m) for m in range(1,R)]
    for p in peers: pl.semaphore_signal(bar,inc=1,device_id=p,device_id_type=MESH)
    xs=(xa,xb,xc,xd)
    xcopy=lambda i: pltpu.make_async_copy(xs[i],xin.at[i%2],xsem.at[i%2])
    chunk=lambda k: pos[k][0]*R+xor(pos[k][1])
    def dstart(u,k):
        for i,ref in enumerate((da,db,dc)):
            @pl.when(u==i)
            def _(): pltpu.make_async_copy(ref.at[:,pl.ds(pl.multiple_of(chunk(k)*CW,128),CW)],dy.at[k%4],dsem.at[k%4]).start()
    def dwait(k): pltpu.make_async_copy(da.at[:,pl.ds(0,CW)],dy.at[k%4],dsem.at[k%4]).wait()
    ccopy=lambda k: pltpu.make_async_remote_copy(src_ref=sbuf.at[k%2],dst_ref=rbuf.at[k%4],send_sem=csend.at[k%2],recv_sem=crecv.at[k%4],device_id=mate,device_id_type=MESH)
    def scopy(u,g,m):
        i=next(i for i,b in enumerate(orders[g]) if m&b); b=orders[g][i]
        a=send[g,m]; d=recv[g,i,m^b]
        return pltpu.make_async_remote_copy(src_ref=sb.at[u,a],dst_ref=rb.at[u,d],send_sem=ssem.at[u,a],recv_sem=rsem.at[u,d],device_id=rdev(b),device_id_type=MESH)
    def rwait(u,g,i,m):
        d=recv[g,i,m]
        pltpu.make_async_remote_copy(src_ref=sb.at[u,0],dst_ref=rb.at[u,d],send_sem=ssem.at[u,0],recv_sem=rsem.at[u,d],device_id=rdev(1),device_id_type=MESH).wait_recv()
    zcopy=lambda u,g,k: pltpu.make_async_remote_copy(src_ref=zs.at[u,g,lax.rem(z+k,nz)],dst_ref=zr.at[u,g,k-1],send_sem=zss.at[u,g,k-1],recv_sem=zrs.at[u,g,k-1],device_id=zdev(k),device_id_type=MESH)
    def acopy(u,g,m): return pltpu.make_async_remote_copy(src_ref=az.at[u,g],dst_ref=out_ref.at[u,g*R+rep],send_sem=ass.at[u,g,m-1],recv_sem=ars.at[u,g,m-1],device_id=rdev(m),device_id_type=MESH)
    alocal=lambda u,g: pltpu.make_async_copy(az.at[u,g],out_ref.at[u,g*R+rep],als.at[u,g])
    def arecv(u,g,m):
        return pltpu.make_async_remote_copy(src_ref=az.at[u,g],dst_ref=out_ref.at[u,g*R+xor(m)],send_sem=ass.at[u,g,m-1],recv_sem=ars.at[u,g,m-1],device_id=rdev(m),device_id_type=MESH)
    xcopy(0).start(); xcopy(1).start(); dstart(0,0); dstart(0,1)
    for i in range(4):
        xcopy(i).wait()
        xt[i]=xin[i%2].T
        if i+2<4: xcopy(i+2).start()
    pl.semaphore_wait(bar,len(peers))
    def consume(u,k):
        g,m,i=pos[k]
        ccopy(k).wait_recv()
        total=obuf[k%2]+rbuf[k%4]
        if i==0 and m:
            sb[u,send[g,m]]=total.astype(bf)
            scopy(u,g,m).start()
        else: kf[u,keep[g,m]]=total.reshape(nz,own,CW)
    def products(u):
        for k in range(NCH):
            if k+2<NCH: dstart(u,k+2)
            else:
                @pl.when(u<2)
                def _(): dstart(u+1,k+2-NCH)
            dwait(k)
            xi=u+(u//2)*(chunk(k)//6)
            p=mm(xt[xi],dy[k%4]).reshape(nz,2,own,CW)
            even=p[:,0].reshape(nz*own,CW); odd=p[:,1].reshape(nz*own,CW)
            if k>=2: ccopy(k).wait_send()
            else:
                @pl.when(u>0)
                def _(): ccopy(k).wait_send()
            sbuf[k%2]=jnp.where(c==0,odd,even)
            obuf[k%2]=jnp.where(c==0,even,odd)
            ccopy(k).start()
            if k>0: consume(u,k-1)
            else:
                @pl.when(u>0)
                def _(): consume(u-1,NCH-1)
    def middle(u,i):
        for g,m,j in pos:
            if m and j==i:
                v=kf[u,keep[g,m]].reshape(nz*own,CW)
                for i2 in range(i):
                    rwait(u,g,i2,m); v=v+rb[u,recv[g,i2,m]].astype(f32)
                sb[u,send[g,m]]=v.astype(bf)
                scopy(u,g,m).start()
    def along(u):
        for g in range(G):
            v=kf[u,keep[g,0]]
            for i2 in range(n):
                rwait(u,g,i2,0); v=v+rb[u,recv[g,i2,0]].astype(f32).reshape(nz,own,CW)
            kf[u,keep[g,0]]=v
            zs[u,g]=v.astype(bf)
            for k in range(1,nz): zcopy(u,g,k).start()
    def spread(u):
        for g in range(G):
            v=kf[u,keep[g,0],z]
            for k in range(1,nz):
                zcopy(u,g,k).wait_recv(); v=v+zr[u,g,k-1].astype(f32)
            az[u,g]=v
            alocal(u,g).start()
            for m in range(1,R): acopy(u,g,m).start()
    depth=max(n-1,0)
    def step(t,_):
        @pl.when(t<3)
        def _(): products(t)
        @pl.when(t==3)
        def _(): consume(2,NCH-1)
        for i in range(1,n):
            @pl.when(jnp.logical_and(t>=i,t<3+i))
            def _(): middle(t-i,i)
        @pl.when(jnp.logical_and(t>=1+depth,t<4+depth))
        def _(): along(t-1-depth)
        @pl.when(jnp.logical_and(t>=2+depth,t<5+depth))
        def _(): spread(t-2-depth)
        return 0
    lax.fori_loop(0,5+depth,step,0)
    def finish(u,_):
        for g in range(G):
            alocal(u,g).wait()
            for m in range(1,R): arecv(u,g,m).wait_recv(); acopy(u,g,m).wait_send()
            for k in range(1,nz): zcopy(u,g,k).wait_send()
            for m in range(1,R): scopy(u,g,m).wait_send()
        return 0
    lax.fori_loop(0,3,finish,0)
    ccopy(NCH-2).wait_send(); ccopy(NCH-1).wait_send()

def layer_grads(R,S,cid,xs,dys):
    T=xs[0].shape[0]; nz=S//2; own=D//S; G=NCH//R
    orders,n,pos,send,keep,recv=grad_plan(R)
    dma=pltpu.SemaphoreType.DMA; V=pltpu.VMEM
    any_=pl.BlockSpec(memory_space=pl.ANY)
    ns,nk,nr=max(len(send),1),len(keep),max(len(recv),1)
    return pl.pallas_call(functools.partial(grad_kernel,R,nz,own,T),
        in_specs=[any_]*7, out_specs=any_, out_shape=jax.ShapeDtypeStruct((3,NCH,own,CW),f32),
        scratch_shapes=[V((2,T,D),bf),V((4,D,T),bf),V((4,T,CW),bf),V((2,D//2,CW),f32),V((2,D//2,CW),f32),V((4,D//2,CW),f32),
            V((3,ns,D//2,CW),bf),V((3,nr,D//2,CW),bf),V((3,nk,nz,own,CW),f32),V((3,G,nz,own,CW),bf),V((3,G,nz-1,own,CW),bf),V((3,G,own,CW),f32),
            dma((2,)),dma((4,)),dma((2,)),dma((4,)),dma((3,ns)),dma((3,nr)),dma((3,G,nz-1)),dma((3,G,nz-1)),dma((3,G,R-1)),dma((3,G,R-1)),dma((3,G))],
        compiler_params=pltpu.CompilerParams(collective_id=cid,has_side_effects=True,vmem_limit_bytes=VLIM),
        cost_estimate=pl.CostEstimate(flops=2*T*D*9216,bytes_accessed=40_000_000,transcendentals=0),
    )(*xs,*dys)
LAYERS=2
beta_one=0.9; beta_two=0.999; adam_eps=1e-8; learn_rate=0.01; weight_decay=0.01; step_count=10.0
def adam_update(w,g,m,v,factor):
    s=g*factor
    m2=beta_one*m+(1.0-beta_one)*s
    v2=beta_two*v+(1.0-beta_two)*s*s
    mh=m2/(1.0-beta_one**step_count)
    vh=v2/(1.0-beta_two**step_count)
    w2=w-learn_rate*(mh/(jnp.sqrt(vh)+adam_eps)+weight_decay*w)
    return (w2,m2,v2,w2.astype(bf))
def inner_adam_kernel(f_ref,g0_ref,g1_ref,ada_ref,w_ref,m_ref,v_ref,*outs):
    factor=f_ref[0]; l=pl.program_id(0); j=pl.program_id(1)
    def put(sl,g):
        for o,val in zip(outs,adam_update(w_ref[0,:,sl],g,m_ref[0,:,sl],v_ref[0,:,sl],factor)): o[0,:,sl]=val
    for a in range(2):
        sl=slice(a*CW,(a+1)*CW)
        for layer,ref in enumerate((g0_ref,g1_ref)):
            @pl.when(jnp.logical_and(j<8,l==layer))
            def _(): put(sl,ref[0,a])
        @pl.when(j>=8)
        def _(): put(sl,ada_ref[0,:,sl])
def inner_adam(factor,g0,g1,ada,w,m,v):
    own=w.shape[1]; C=w.shape[2]; W=2*CW
    blk=pl.BlockSpec((1,own,W),lambda l,j:(l,0,j))
    def gmap(layer):
        def index(l,j):
            jj=jnp.minimum(j,7); on=jnp.where(l==layer,jj,7*(l>layer))
            return (2-on//4, on%4, 0, 0)
        return pl.BlockSpec((1,2,own,CW),index)
    sd=jax.ShapeDtypeStruct
    return pl.pallas_call(inner_adam_kernel,grid=(LAYERS,C//W),
        in_specs=[pl.BlockSpec(memory_space=pltpu.SMEM),gmap(0),gmap(1),pl.BlockSpec((1,own,W),lambda l,j:(l,0,jnp.maximum(j-8,0))),blk,blk,blk],
        out_specs=[blk]*4,out_shape=[sd(w.shape,f32)]*3+[sd(w.shape,bf)],
        compiler_params=pltpu.CompilerParams(vmem_limit_bytes=VLIM))(factor,g0,g1,ada,w,m,v)
def outer_adam_kernel(f_ref,g0_ref,g1_ref,b_ref,w_ref,m_ref,v_ref,*outs):
    factor=f_ref[0]; l=pl.program_id(0); j=pl.program_id(1)
    def put(sl,g):
        for o,val in zip(outs,adam_update(w_ref[0,:,sl],g,m_ref[0,:,sl],v_ref[0,:,sl],factor)): o[0,:,sl]=val
    for a in range(2):
        sl=slice(a*CW,(a+1)*CW)
        for layer,ref in enumerate((g0_ref,g1_ref)):
            @pl.when(jnp.logical_and(j<4,l==layer))
            def _(): put(sl,ref[0,a])
    @pl.when(j==4)
    def _(): put(slice(0,128),b_ref[0])
def outer_adam(factor,g0,g1,b,w,m,v):
    own=w.shape[1]; W=2*CW
    blk=pl.BlockSpec((1,own,W),lambda l,j:(l,0,j))
    def gmap(layer):
        def index(l,j):
            jj=jnp.minimum(j,3); on=jnp.where(l==layer,jj,3*(l>layer))
            return (0, on, 0, 0)
        return pl.BlockSpec((1,2,own,CW),index)
    sd=jax.ShapeDtypeStruct
    return pl.pallas_call(outer_adam_kernel,grid=(LAYERS,5),
        in_specs=[pl.BlockSpec(memory_space=pltpu.SMEM),gmap(0),gmap(1),pl.BlockSpec((1,own,128),lambda l,j:(l,0,0)),blk,blk,blk],
        out_specs=[blk]*4,out_shape=[sd(w.shape,f32)]*3+[sd(w.shape,bf)],
        compiler_params=pltpu.CompilerParams(vmem_limit_bytes=VLIM))(factor,g0,g1,b,w,m,v)
P_SIZE=16; GRID=16; LAYERS=2; LAT_DEV=4; FREQ=256; NCLASS=1000
clip_coef=2.5
BIAS=14
def position_table(grid_side, feature_width):
    quarter=feature_width//4
    omega=jnp.exp(-math.log(10000.0)*jnp.arange(quarter,dtype=f32)/quarter)
    ids=jnp.arange(grid_side*grid_side,dtype=jnp.int32)
    a=(ids%grid_side).astype(f32)[:,None]*omega[None,:]
    d=(ids//grid_side).astype(f32)[:,None]*omega[None,:]
    return jnp.concatenate([jnp.sin(a),jnp.cos(a),jnp.sin(d),jnp.cos(d)],axis=1)
def time_features(steps, count):
    half=count//2
    freq=jnp.exp(-math.log(10000.0)*jnp.arange(half,dtype=f32)/half)
    ang=steps.astype(f32)[:,None]*freq[None,:]
    return jnp.concatenate([jnp.cos(ang),jnp.sin(ang)],axis=1)
def modulate(x, sh, sc):
    c=x-jnp.mean(x,axis=-1,keepdims=True)
    v=jnp.mean(c*c,axis=-1,keepdims=True)
    return c*lax.rsqrt(v+norm_eps)*(1.0+sc[:,None,:])+sh[:,None,:]
def dot32(pattern,a,b): return jnp.einsum(pattern,a,b,preferred_element_type=f32)
def silu_back(v,g): return jax.vjp(jax.nn.silu,v)[1](g)[0]
ALL=("rep","shard")

def per_device(latents,target_noise,labels,time_steps,inner_weights,outer_weights,embed_table,final_mod,head_weights,
               inner_moment,inner_square,outer_moment,outer_square,embed_moment,embed_square,final_moment,final_square,head_moment,head_square):
    R=lax.axis_size("rep"); S=lax.axis_size("shard")
    rep=lax.axis_index("rep"); shard=lax.axis_index("shard")
    own=D//S; W=4*D//R; N=LAT_DEV*R*S; G=LAT_DEV*S
    count=N*TOK*P_SIZE
    inner_low=inner_weights.astype(bf)
    outer_turn=lambda a: a.transpose(0,2,1)
    outer_low=outer_turn(outer_weights).astype(bf)
    def slab(l):
        s=jnp.stack([inner_low[l,:,:4*D],inner_low[l,:,4*D:8*D],outer_low[l,:,:FF]])
        return s.reshape(3,own,R,W).transpose(0,2,1,3)
    embed_low=embed_table.T.astype(bf); final_low=final_mod.astype(bf); head_low=head_weights.astype(bf)
    r1=P_SIZE+1; r2=P_SIZE+2+FREQ; r3=P_SIZE+3+FREQ+D
    fin_cols=2*D//S
    small=jnp.concatenate([outer_low[0,:,FF:],outer_low[1,:,FF:],embed_low[:,:P_SIZE+1]],axis=1).T
    small=jnp.pad(small,((0,48-small.shape[0]),(0,0)))
    mine_rows=jnp.concatenate([time_features(time_steps,FREQ).astype(bf).astype(f32),labels.astype(f32)[:,None],jnp.zeros((LAT_DEV,127),f32)],axis=1)
    mine_rows=jnp.concatenate([mine_rows,mine_rows],axis=0)
    second_w=embed_low[:,r2:r2+D]
    table=jnp.pad(embed_low[:,r3:],((0,0),(0,1024-NCLASS)))
    biases2=jnp.pad(jnp.stack([embed_low[:,r1+FREQ],embed_low[:,r2+D]]).astype(f32),((0,6),(0,0)))
    ada_own=inner_low[:,:,4*D+FF:]
    fin_bias=jnp.pad(final_low[D:].astype(f32),((0,7),(0,0)))
    first=first_call(slab(0),mine_rows,small,embed_low[:,r1:r1+FREQ],second_w.reshape(own,S,own).transpose(1,0,2),table,biases2,ada_own,final_low[:D].reshape(S,own,fin_cols),fin_bias,R,S,0)
    gather0,rows_all,small,hidden,time_act,condition,cond_all,modul,fin_mod=first
    def latent_order(a):
        a=a.reshape(a.shape[:-2]+(S,R,8,a.shape[-1]))[...,:LAT_DEV,:]
        return jnp.swapaxes(a,-4,-3).reshape(a.shape[:-4]+(N,a.shape[-1]))
    rows_all=latent_order(rows_all.reshape(S*R*8,384))
    features=rows_all[:,:FREQ].astype(bf)
    hot=rows_all[:,FREQ:FREQ+1]==jnp.arange(NCLASS,dtype=jnp.int32).astype(f32)[None,:]
    hidden=latent_order(hidden); condition=latent_order(condition)
    wide=lambda a: latent_order(a).transpose(1,0,2).reshape(N,D)
    time_act=wide(time_act); cond_all=wide(cond_all)
    cond_own=lax.dynamic_slice_in_dim(cond_all,shard*own,own,1)
    small=small.transpose(1,0,2).reshape(48,D)
    biases=small[:LAYERS*BIAS].reshape(LAYERS,BIAS,D).astype(f32)
    patch_w=small[LAYERS*BIAS:LAYERS*BIAS+P_SIZE]; patch_b=small[LAYERS*BIAS+P_SIZE].astype(f32)
    modul=modul.reshape(LAYERS,LAT_DEV,6,D)+biases[:,None,7:13]
    modul=jnp.pad(modul,((0,0),(0,0),(0,2),(0,0)))
    fin_mod=fin_mod[:,:LAT_DEV].transpose(1,0,2).reshape(LAT_DEV,2*D)
    ramp=0.0001+(0.02-0.0001)*jnp.arange(1000,dtype=f32)/999.0
    upto=jnp.arange(1000,dtype=jnp.int32)[None,:]<=time_steps[:,None]
    abar=jnp.exp(jnp.sum(jnp.where(upto,jnp.log(1.0-ramp)[None,:],0.0),axis=1))
    patches=(jnp.sqrt(abar)[:,None,None]*latents+jnp.sqrt(1.0-abar)[:,None,None]*target_noise).astype(bf)
    stream=dot32("gpt,pd->gtd",patches,patch_w)+patch_b+position_table(GRID,D)[None]
    stream=stream.reshape(LAT_DEV*TOK,D)
    saved=[]
    gathered=[unit_blocks(gather0,R)]
    for l in range(LAYERS):
        wa,w1,w2=gathered[l]
        bias=jnp.pad(biases[l],((0,2),(0,0)))
        if l==0:
            o,gather1=layer_fwd_gather(stream,modul[l],bias,wa,w1,w2,slab(1),R,S,1)
            gathered.append(unit_blocks(gather1,R))
        else: o=layer_fwd(stream,modul[l],bias,wa,w1,w2)
        saved.append((stream,)+tuple(o))
        stream=o[-1]
    stream3=stream.reshape(LAT_DEV,TOK,D)
    fin_shift,fin_scale=jnp.split(fin_mod,2,axis=1)
    fin_normed=modulate(stream3,fin_shift,fin_scale).astype(bf)
    output=dot32("gtd,dp->gtp",fin_normed,head_low[:D])+head_low[D].astype(f32)
    differ=output-jnp.swapaxes(target_noise,1,2)
    loss_part=jnp.sum(differ*differ)/count
    grad_output=2.0*(differ*(1.0/count))
    head_bias=jnp.sum(grad_output,axis=(0,1))
    output_low=grad_output.astype(bf)
    head_grad=jnp.concatenate([dot32("gtd,gtp->dp",fin_normed,output_low),head_bias[None]],axis=0)
    grad_fin_normed=dot32("gtp,dp->gtd",output_low,head_low[:D])
    grad_stream,g_shift,g_scale=jax.vjp(modulate,stream3,fin_shift,fin_scale)[1](grad_fin_normed)
    grad_stream=grad_stream.reshape(LAT_DEV*TOK,D)
    grad_fin=jnp.concatenate([g_shift,g_scale],axis=1)
    ada_parts=[None]*LAYERS; bias_grads=[None]*LAYERS; operands=[None]*LAYERS; gathered_rows=[None]*LAYERS
    for l in range(LAYERS-1,-1,-1):
        wa,w1,w2=gathered[l]
        x,normed,qkv,lse,mixed,attn,mid,ntwo,upper,activ,down,_=saved[l]
        dlow,ulow,gmid,alow,gmix,dm1,db1=layer_bwd_mlp(grad_stream,modul[l],wa,w1,w2,down,upper,mid,attn)
        low,grad_stream,dm2,db2=layer_bwd_attn(gmix,alow,gmid,modul[l],wa,qkv,lse,x)
        operands[l]=((dlow,ntwo,normed,mixed),(activ,ulow,low))
        dmod=jnp.concatenate([dm2[:,:2],dm1[:,2:6]],axis=1)
        mod_rows=dmod.astype(bf).reshape(LAT_DEV,6*D)
        if l==LAYERS-1: mod_rows=jnp.concatenate([mod_rows,grad_fin.astype(bf)],axis=1)
        mod_rows=lax.all_gather(mod_rows,ALL,axis=0,tiled=True)
        gathered_rows[l]=mod_rows
        bias_grads[l]=jnp.concatenate([db2[0:2],db1[2:7],jnp.sum(dmod,axis=0),db1[13:14]],axis=0)
    ops1,late=lax.optimization_barrier((operands[1],gathered_rows[1]))
    fin_mine=lax.dynamic_slice_in_dim(late,6*D+shard*fin_cols,fin_cols,1)
    final_main=dot32("nd,ne->de",cond_all,fin_mine)
    fin_part=dot32("ne,de->nd",fin_mine,final_low[:D])
    fin_part,ops1=lax.optimization_barrier((fin_part,ops1))
    grad_cond=lax.psum_scatter(fin_part,"shard",scatter_dimension=1,tiled=True)
    grads1=layer_grads(R,S,LAYERS+1,*ops1)
    grads1,grad_cond,early=lax.optimization_barrier((grads1,grad_cond,gathered_rows[0]))
    for l,mod_rows in ((0,early),(1,late[:,:6*D])):
        ada_parts[l]=dot32("nd,ne->de",cond_own,mod_rows)
        grad_cond=grad_cond+dot32("ne,de->nd",mod_rows,ada_own[l])
    gs=grad_stream.reshape(LAT_DEV,TOK,D)
    patch_grad=dot32("gpt,gtd->pd",patches,gs.astype(bf))
    patch_bias=jnp.sum(grad_stream,axis=0)
    fin_bias_sum=jnp.sum(grad_fin,axis=0).reshape(2,D)
    tail=jnp.zeros((1,D),f32).at[0,0].set(loss_part)
    head_flat=head_grad.reshape(-1)
    head_rows=-(-head_flat.shape[0]//D)
    head_flat=jnp.pad(head_flat,(0,head_rows*D-head_flat.shape[0])).reshape(head_rows,D)
    local_sums=(jnp.concatenate(bias_grads+[patch_grad,patch_bias[None],fin_bias_sum,head_flat,tail],axis=0))
    grad_condition=silu_back(condition,grad_cond)
    b2=jnp.sum(grad_condition,axis=0)
    clow=grad_condition.astype(bf)
    second=dot32("nd,ne->de",time_act,clow)
    class_grad=jnp.einsum("nc,nd->cd",hot.astype(f32),grad_condition,precision=lax.Precision.HIGHEST)
    time_part=dot32("ne,ed->nd",clow,second_w)
    time_part,ops0,local_sums=lax.optimization_barrier((time_part,operands[0],local_sums))
    sums=lax.psum(local_sums,ALL)
    grad_time_act=lax.psum_scatter(time_part,"shard",scatter_dimension=1,tiled=True)
    grads0=layer_grads(R,S,LAYERS,*ops0)
    grads0,grad_time_act,sums=lax.optimization_barrier((grads0,grad_time_act,sums))
    o1=LAYERS*BIAS; o2=o1+P_SIZE+1; o3=o2+2; o4=o3+head_rows
    mean_loss=sums[o4,0]
    head_total=sums[o3:o4].reshape(-1)[:(D+1)*P_SIZE].reshape(D+1,P_SIZE)
    fin_bias_own=lax.dynamic_slice_in_dim(sums[o2:o3].reshape(2*D),shard*fin_cols,fin_cols,0)
    mine=lax.dynamic_slice_in_dim(sums[:o2],shard*own,own,1)
    grad_time=silu_back(hidden,grad_time_act)
    first=dot32("nf,nd->fd",features,grad_time.astype(bf))
    embed_grad=jnp.concatenate([mine[o1:o2],first,jnp.sum(grad_time,axis=0)[None],second,b2[None],class_grad],axis=0)
    final_grad=jnp.concatenate([final_main,fin_bias_own[None]],axis=0)
    ada_grad=jnp.stack(ada_parts)
    bias_grad=jnp.pad(mine[:o1].reshape(LAYERS,BIAS,own),((0,0),(0,2),(0,0)))
    sq=lambda a: jnp.sum(a*a)
    square=lax.psum(sq(grads0)+sq(grads1)+sq(ada_grad)+sq(bias_grad)+sq(embed_grad)+sq(final_grad),"shard")
    grad_norm=jnp.sqrt(square+sq(head_total))
    factor=jnp.minimum(1.0,clip_coef*math.sqrt(D/count)/grad_norm)
    out=[mean_loss,grad_norm]
    out.extend(inner_adam(factor.reshape(1),grads0,grads1,ada_grad,inner_weights,inner_moment,inner_square))
    bias_turn=jnp.pad(bias_grad.transpose(0,2,1),((0,0),(0,0),(0,112)))
    out.extend(outer_turn(a) for a in outer_adam(factor.reshape(1),grads0,grads1,bias_turn,outer_turn(outer_weights),outer_turn(outer_moment),outer_turn(outer_square)))
    for w,g,m,v in ((embed_table,embed_grad,embed_moment,embed_square),(final_mod,final_grad,final_moment,final_square),
                    (head_weights,head_total,head_moment,head_square)):
        out.extend(adam_update(w,g,m,v,factor))
    return tuple(out)

def solution(mesh):
    lat=P(ALL,None,None); one=P(ALL); inn=P(None,"shard",None); oute=P(None,None,"shard"); col=P(None,"shard")
    in_specs=(lat,lat,one,one,inn,oute,col,col,P(),inn,inn,oute,oute,col,col,col,col,P(),P())
    out_specs=(P(),P())+(inn,)*4+(oute,)*4+(col,)*8+(P(),)*4
    return jax.shard_map(per_device,mesh=mesh,in_specs=in_specs,out_specs=out_specs,check_vma=False)
```

```python
from jax.sharding import PartitionSpec as P
import functools, math
import jax, jax.numpy as jnp
from jax import lax
from jax.experimental import pallas as pl
from jax.experimental.pallas import tpu as pltpu
D=768; HEADS=12; HDIM=64; FF=3072; TOK=256
norm_eps=1e-6
bf=jnp.bfloat16; f32=jnp.float32
VLIM=60*1024*1024
def mm(a,b): return lax.dot_general(a,b,(((1,),(0,)),((),())),preferred_element_type=f32)
def mm_nt(a,b): return lax.dot_general(a,b,(((1,),(1,)),((),())),preferred_element_type=f32)
def mm_tn(a,b): return lax.dot_general(a,b,(((0,),(0,)),((),())),preferred_element_type=f32)
def ln_parts(x):
    c=x-jnp.mean(x,axis=-1,keepdims=True)
    r=lax.rsqrt(jnp.mean(c*c,axis=-1,keepdims=True)+norm_eps)
    return c*r, r
def ln_back(dy, xhat, r, sc):
    dxh=dy*(1.0+sc)
    m1=jnp.mean(dxh,axis=-1,keepdims=True); m2=jnp.mean(dxh*xhat,axis=-1,keepdims=True)
    return r*(dxh-m1-xhat*m2)
def half_masks():
    lane=lax.broadcasted_iota(jnp.int32,(1,128),1)
    lo=(lane<HDIM)
    return lo
C0=math.sqrt(2.0/math.pi); C1=0.044715

def fwd_kernel(x_ref, mod_ref, bias_ref, wa_ref, w1_ref, w2_ref,
               normed_ref, qkv_ref, lse_ref, mixed_ref, attn_ref, mid_ref, ntwo_ref, upper_ref, activ_ref, down_ref, out_ref, hook=lambda p: None):
    hook(0)
    x=x_ref[...]
    mod=lambda j: mod_ref[0, j:j+1, :]
    bias=lambda j: bias_ref[j:j+1, :]
    xh,_=ln_parts(x)
    normed=(xh*(1.0+mod(1))+mod(0)).astype(bf)
    normed_ref[...]=normed
    qkv_ref[:, :D]=(mm(normed, wa_ref[0,0])+bias(0)).astype(bf)
    qkv_ref[:, D:2*D]=mm(normed, wa_ref[0,1]).astype(bf)
    qkv_ref[:, 2*D:]=(mm(normed, wa_ref[0,2])+bias(1)).astype(bf)
    lo=half_masks()
    for hp in range(HEADS//2):
        hook(1+hp)
        c=hp*128
        q=qkv_ref[:, c:c+128]; k=qkv_ref[:, D+c:D+c+128]; v=qkv_ref[:, 2*D+c:2*D+c+128]
        outs=[]
        for h in range(2):
            keep=lo if h==0 else jnp.logical_not(lo)
            qm=jnp.where(keep, q, jnp.zeros_like(q))
            s=mm_nt(qm,k)*(HDIM**-0.5)
            m=jnp.max(s,axis=-1,keepdims=True)
            e=jnp.exp(s-m)
            l=jnp.sum(e,axis=-1,keepdims=True)
            p=(e*(1.0/l)).astype(bf)
            lse_ref[:, 2*hp+h:2*hp+h+1]=m+jnp.log(l)
            outs.append(mm(p,v))
        mixed_ref[:, c:c+128]=jnp.where(lo, outs[0], outs[1]).astype(bf)
    hook(7)
    attn=mm(mixed_ref[...], wa_ref[0,3])+bias(2)
    attn_ref[...]=attn
    mid=x+mod(2)*attn
    mid_ref[...]=mid
    xh2,_=ln_parts(mid)
    ntwo=(xh2*(1.0+mod(4))+mod(3)).astype(bf)
    ntwo_ref[...]=ntwo
    down=jnp.broadcast_to(bias(13),(TOK,D))
    for j in range(4):
        hook(8+j)
        up=mm(ntwo, w1_ref[0,j])+bias(3+j)
        upper_ref[:, j*D:(j+1)*D]=up
        t=jnp.tanh(C0*(up+C1*(up*up*up)))
        act=(0.5*up*(1.0+t)).astype(bf)
        activ_ref[:, j*D:(j+1)*D]=act
        down=down+mm_nt(act, w2_ref[0,j])
    down_ref[...]=down
    out_ref[...]=mid_ref[...]+mod(5)*down

def full(shape):
    n=len(shape)
    return pl.BlockSpec(shape, lambda i: (0,)*n, pipeline_mode=pl.Buffered(1))
def unit(u,n=4): return pl.BlockSpec((1,n,D,D),lambda i:(u,0,0,0),pipeline_mode=pl.Buffered(1))
def rows(width): return pl.BlockSpec((TOK,width), lambda i:(i,0))
def layer_fwd(x, mod, bias, w):
    T=x.shape[0]; n=T//TOK
    sd=jax.ShapeDtypeStruct
    widths=[(D,bf),(3*D,bf),(128,f32),(D,bf),(D,f32),(D,f32),(D,bf),(FF,f32),(FF,bf),(D,f32),(D,f32)]
    return pl.pallas_call(fwd_kernel, grid=(n,),
        in_specs=[rows(D), pl.BlockSpec((1,8,D),lambda i:(i,0,0)), full((16,D)), unit(0), unit(1), unit(2)],
        out_specs=[rows(w) for w,_ in widths],
        out_shape=[sd((T,w),t) for w,t in widths],
        compiler_params=pltpu.CompilerParams(vmem_limit_bytes=VLIM),
        cost_estimate=pl.CostEstimate(flops=2*T*(9216*D+2*TOK*D), bytes_accessed=60_000_000, transcendentals=T*FF*2),
    )(x,mod,bias,w,w,w)

def bwd_mlp_kernel(g_ref, mod_ref, wa3_ref, w1_ref, w2_ref, down_ref, upper_ref, mid_ref, attn_ref,
                   dlow_ref, ulow_ref, gmid_ref, alow_ref, gmix_ref, dmod_ref, db_ref):
    i=pl.program_id(0)
    mod=lambda j: mod_ref[0, j:j+1, :]
    g=g_ref[...]
    gd=g*mod(5)
    dl=gd.astype(bf)
    dlow_ref[...]=dl
    @pl.when(i==0)
    def _(): db_ref[...]=jnp.zeros_like(db_ref)
    s0=lambda v: jnp.sum(v,axis=0,keepdims=True)
    dmod_ref[0,5:6,:]=s0(g*down_ref[...])
    db_ref[13:14,:]+=s0(gd)
    gn=jnp.zeros((TOK,D),f32)
    for j in range(4):
        ga=mm(dl, w2_ref[0,j])
        up=upper_ref[:, j*D:(j+1)*D]
        u2=up*up
        t=jnp.tanh(C0*(up+C1*(u2*up)))
        gu=ga*(0.5*(1.0+t)+(0.5*C0)*up*(1.0-t*t)*(1.0+(3.0*C1)*u2))
        db_ref[3+j:4+j,:]+=s0(gu)
        ul=gu.astype(bf)
        ulow_ref[:, j*D:(j+1)*D]=ul
        gn=gn+mm_nt(ul, w1_ref[0,j])
    xh,r=ln_parts(mid_ref[...])
    dmod_ref[0,3:4,:]=s0(gn)
    dmod_ref[0,4:5,:]=s0(gn*xh)
    gm=g_ref[...]+ln_back(gn,xh,r,mod(4))
    gmid_ref[...]=gm
    ga=gm*mod(2)
    dmod_ref[0,2:3,:]=s0(gm*attn_ref[...])
    db_ref[2:3,:]+=s0(ga)
    al=ga.astype(bf)
    alow_ref[...]=al
    gmix_ref[...]=mm_nt(al, wa3_ref[0,0]).astype(bf)
def bwd_mlp_parts(g, mod, w, down, upper, mid, attn):
    T=g.shape[0]; n=T//TOK
    sd=jax.ShapeDtypeStruct
    m3=pl.BlockSpec((1,8,D),lambda i:(i,0,0))
    return (bwd_mlp_kernel,(g,mod,w,w,w,down,upper,mid,attn),
        [rows(D), m3, pl.BlockSpec((1,1,D,D),lambda i:(0,3,0,0),pipeline_mode=pl.Buffered(1)), unit(1), unit(2), rows(D), rows(FF), rows(D), rows(D)],
        [sd((T,D),bf),sd((T,FF),bf),sd((T,D),f32),sd((T,D),bf),sd((T,D),bf),sd((n,8,D),f32),sd((16,D),f32)],
        [rows(D),rows(FF),rows(D),rows(D),rows(D),m3,pl.BlockSpec((16,D),lambda i:(0,0))],
        pl.CostEstimate(flops=2*T*D*(2*FF+D), bytes_accessed=50_000_000, transcendentals=T*FF))
def plain(kernel,args,specs,shapes,ospecs,cost):
    return pl.pallas_call(kernel,grid=(args[0].shape[0]//TOK,),in_specs=specs,out_specs=ospecs,out_shape=shapes,
        compiler_params=pltpu.CompilerParams(vmem_limit_bytes=VLIM),cost_estimate=cost)(*args)

def bwd_attn_kernel(gmix_ref, alow_ref, gmid_ref, mod_ref, wa_ref, qkv_ref, lse_ref, x_ref,
                    low_ref, gin_ref, dmod_ref, db_ref):
    i=pl.program_id(0)
    mod=lambda j: mod_ref[0, j:j+1, :]
    @pl.when(i==0)
    def _(): db_ref[...]=jnp.zeros_like(db_ref)
    s0=lambda v: jnp.sum(v,axis=0,keepdims=True)
    low_ref[:, 3*D:]=alow_ref[...]
    lo=half_masks()
    zero=jnp.zeros((TOK,128),bf)
    for hp in range(HEADS//2):
        c=hp*128
        q=qkv_ref[:, c:c+128]; k=qkv_ref[:, D+c:D+c+128]; v=qkv_ref[:, 2*D+c:2*D+c+128]
        gm=gmix_ref[:, c:c+128]
        res=[]
        for h in range(2):
            keep=lo if h==0 else jnp.logical_not(lo)
            qm=jnp.where(keep,q,zero); gmm=jnp.where(keep,gm,zero)
            s=mm_nt(qm,k)*(HDIM**-0.5)
            p=jnp.exp(s-lse_ref[:, 2*hp+h:2*hp+h+1])
            dp=mm_nt(gmm,v)
            ds=p*(dp-jnp.sum(p*dp,axis=-1,keepdims=True))
            dsl=ds.astype(bf)
            res.append((mm(dsl,k), mm_tn(dsl,q), mm_tn(p.astype(bf),gm)))
        for j in range(3):
            o=jnp.where(lo,res[0][j],res[1][j])
            if j<2: o=o*(HDIM**-0.5)
            ol=o.astype(bf)
            low_ref[:, j*D+c:j*D+c+128]=ol
            if j!=1:
                row=0 if j==0 else 1
                db_ref[row:row+1, c:c+128]+=s0(ol.astype(f32))
    gn=mm_nt(low_ref[:, :D], wa_ref[0,0])+mm_nt(low_ref[:, D:2*D], wa_ref[0,1])+mm_nt(low_ref[:, 2*D:3*D], wa_ref[0,2])
    xh,r=ln_parts(x_ref[...])
    dmod_ref[...]=jnp.zeros_like(dmod_ref)
    dmod_ref[0,0:1,:]=s0(gn)
    dmod_ref[0,1:2,:]=s0(gn*xh)
    gin_ref[...]=gmid_ref[...]+ln_back(gn,xh,r,mod(1))
def bwd_attn_parts(gmix, alow, gmid, mod, w, qkv, lse, x):
    T=gmix.shape[0]; n=T//TOK
    sd=jax.ShapeDtypeStruct
    m3=pl.BlockSpec((1,8,D),lambda i:(i,0,0))
    return (bwd_attn_kernel,(gmix,alow,gmid,mod,w,qkv,lse,x),
        [rows(D),rows(D),rows(D),m3,unit(0,3),rows(3*D),rows(128),rows(D)],
        [sd((T,4*D),bf),sd((T,D),f32),sd((n,8,D),f32),sd((8,D),f32)],
        [rows(4*D),rows(D),m3,pl.BlockSpec((8,D),lambda i:(0,0))],
        pl.CostEstimate(flops=2*T*D*(3*D+5*TOK), bytes_accessed=25_000_000, transcendentals=T*TOK*HEADS))
MESH=pl.DeviceIdType.MESH
class Gather:
    def __init__(self,R,nz,U,w_ref,out_ref,zs,zr,xs,xr,cs,cr,ls):
        self.R,self.nz,self.U=R,nz,U
        self.w,self.out=w_ref,out_ref
        self.zs,self.zr,self.xs,self.xr,self.cs,self.cr,self.ls=zs,zr,xs,xr,cs,cr,ls
        self.rep=lax.axis_index("rep"); self.shard=lax.axis_index("shard")
        self.z=self.shard//2; self.c=lax.rem(self.shard,2)
        self.relay=R==4
    def at(self,m,z,other=False): return (jnp.bitwise_xor(self.rep,m), 2*z+(1-self.c if other else self.c))
    def peers(self):
        return [self.at(0,lax.rem(self.z+k,self.nz)) for k in range(1,self.nz)]+[self.at(m,self.z) for m in range(1,self.R)]+[self.at(0,self.z,True)]
    def copy(self,src,dst,s,r,dev): return pltpu.make_async_remote_copy(src_ref=src,dst_ref=dst,send_sem=s,recv_sem=r,device_id=dev,device_id_type=MESH)
    def along(self,u,o,up):
        b=self.out.at[u,self.rep,o,self.c]
        return self.copy(b,b,self.zs.at[u,o,1 if up else 0],self.zr.at[u,o],self.at(0,self.z+(1 if up else -1)))
    def own(self,u,up):
        return self.copy(self.w.at[u,self.rep],self.out.at[u,self.rep,self.z,self.c],self.zs.at[u,self.z,1 if up else 0],self.zr.at[u,self.z],self.at(0,self.z+(1 if up else -1)))
    def across(self,u,o,m,q,to):
        b=self.out.at[u,jnp.bitwise_xor(self.rep,q),o,self.c]
        return self.copy(b,b,self.xs.at[u,m-1,o],self.xr.at[u,m-1,o],self.at(to,self.z))
    def swap(self,u,m):
        b=self.out.at[u,jnp.bitwise_xor(self.rep,m),:,self.c]
        return self.copy(b,b,self.cs.at[u,m],self.cr.at[u,m],self.at(0,self.z,True))
    def local(self,u): return pltpu.make_async_copy(self.w.at[u],self.out.at[u,:,self.z,self.c],self.ls.at[u])
    def start(self):
        for u in range(self.U):
            @pl.when(self.z<self.nz-1)
            def _(): self.own(u,True).start()
            @pl.when(self.z>0)
            def _(): self.own(u,False).start()
        for u in range(self.U): self.local(u).start()
    def sides(self,h):
        z,nz=self.z,self.nz
        return ((z>=h,z-h,True,z<nz-1),(z+h<nz,z+h,False,z>0))
    def arrive(self,h,u):
        for there,o,up,more in self.sides(h):
            @pl.when(there)
            def _():
                self.along(u,o,up).wait_recv()
                @pl.when(more)
                def _(): self.along(u,o,up).start()
                for m in range(1,self.R):
                    if not (self.relay and m==3): self.across(u,o,m,0,m).start()
    def pass_on(self,h,u):
        if not self.relay: return
        for there,o,up,more in self.sides(h):
            for par,(q,to) in enumerate(((1,2),(2,1))):
                @pl.when(jnp.logical_and(there,lax.rem(u+o+self.nz,2)==par))
                def _():
                    self.across(u,o,q,0,q).wait_recv()
                    self.across(u,o,3,q,to).start()
    def swap_own(self,u):
        self.local(u).wait(); self.swap(u,0).start()
    def swap_block(self,u,m):
        for o in range(self.nz):
            seen=self.relay and m<3
            cond=o!=self.z
            if seen: cond=jnp.logical_and(cond,(u+o+self.nz)%2!=m-1)
            if seen and (u+o+self.nz)%2==m-1: continue
            @pl.when(o!=self.z)
            def _(): self.across(u,o,m,0,m).wait_recv()
        self.swap(u,m).start()
    def ticks(self):
        U,nz=self.U,self.nz
        order=[(h,u) for h in range(1,nz) for u in range(U)]
        out=[]
        for i in range(len(order)+U):
            if i<len(order): out.append(functools.partial(self.arrive,*order[i]))
            if i>=U: out.append(functools.partial(self.pass_on,*order[i-U]))
            if i>=len(order): out.append(functools.partial(self.swap_own,i-len(order)))
        for u in range(U):
            for m in range(1,self.R): out.append(functools.partial(self.swap_block,u,m))
        return out
    def finish(self):
        for u in range(self.U):
            for m in range(self.R): self.swap(u,m).wait()
            @pl.when(self.z<self.nz-1)
            def _(): self.own(u,True).wait_send()
            @pl.when(self.z>0)
            def _(): self.own(u,False).wait_send()
            for h in range(1,self.nz):
                for there,o,up,more in self.sides(h):
                    @pl.when(there)
                    def _():
                        @pl.when(more)
                        def _(): self.along(u,o,up).wait_send()
                        for m in range(1,self.R): self.across(u,o,m,0,m).wait_send()
def gather_sems(R,nz,U):
    dma=pltpu.SemaphoreType.DMA
    return [dma((U,nz,2)),dma((U,nz)),dma((U,R-1,nz)),dma((U,R-1,nz)),dma((U,R)),dma((U,R)),dma((U,))]
def unit_blocks(out,R):
    U=out.shape[0]; W=out.shape[-1]
    out=out.reshape(U,R,D,W)
    if R==4: return out
    m=R//4
    return out.reshape(U,4,m,D,W).transpose(0,1,3,2,4).reshape(U,4,D,D)
def meet(peers):
    bar=pltpu.get_barrier_semaphore()
    for p in peers: pl.semaphore_signal(bar,inc=1,device_id=p,device_id_type=MESH)
    pl.semaphore_wait(bar,len(peers))

def first_kernel(R,nz,U,own, w_ref,fo_ref,sm_ref,t1_ref,t2_ref,cls_ref,tb_ref,ada_ref,fin_ref,finb_ref,
                 out_ref,f_ref,sg_ref,hid_ref,act_ref,con_ref,call_ref,mod_ref,fm_ref,
                 cgs,pm,mr,ps,zrv,fps, fs1,fr1,fs2,fr2,ss,sr,as_,ar,cs_,cr_,ms,mrs,pz,pzr,vs,vr, *gsems):
    S=2*nz; NP=S*R*8
    ga=Gather(R,nz,U,w_ref,out_ref,*gsems)
    rep=lax.axis_index("rep"); shard=lax.axis_index("shard"); z=shard//2; c=lax.rem(shard,2)
    rpeer=lambda m: (jnp.bitwise_xor(rep,m),shard)
    speer=lambda k: (rep,lax.rem(shard+k,S))
    mate=(rep,2*z+1-c)
    peers=[rpeer(m) for m in range(1,R)]+[speer(k) for k in range(1,S)]
    def send(src,dst,s,r,dev): return pltpu.make_async_remote_copy(src_ref=src,dst_ref=dst,send_sem=s,recv_sem=r,device_id=dev,device_id_type=MESH)
    meet(peers)
    f1=lambda m: send(fo_ref,f_ref.at[shard,rep],fs1.at[m-1],fr1.at[m-1],rpeer(m))
    for m in range(1,R): f1(m).start()
    smc=lambda k: send(sm_ref,sg_ref.at[shard],ss.at[k-1],sr.at[k-1],speer(k))
    ga.start(); ticks=ga.ticks()
    f_ref[shard,rep]=fo_ref[...]
    sg_ref[shard]=sm_ref[...]
    for m in range(1,R): f1(m).wait_recv()
    f2=lambda k: send(f_ref.at[shard],f_ref.at[shard],fs2.at[k-1],fr2.at[k-1],speer(k))
    for k in range(1,S): f2(k).start()
    for k in range(1,S): smc(k).start()
    for t in ticks[:U]: t()
    for k in range(1,S): f2(k).wait_recv()
    feats=f_ref[...].reshape(NP,384)
    hidden=mm_nt(feats[:,:256].astype(bf),t1_ref[...])+tb_ref[0:1,:]
    hid_ref[...]=hidden
    act_ref[shard]=(hidden/(1.0+jnp.exp(-hidden))).astype(bf)
    ac=lambda k: send(act_ref.at[shard],act_ref.at[shard],as_.at[k-1],ar.at[k-1],speer(k))
    for k in range(1,S): ac(k).start()
    hot=(feats[:,256:257].astype(jnp.int32)==lax.broadcasted_iota(jnp.int32,(1,cls_ref.shape[1]),1))
    con=mm_nt(jnp.where(hot,1.0,0.0).astype(bf),cls_ref[...])
    for t in ticks[U:2*U]: t()
    for k in range(1,S): ac(k).wait_recv()
    sec=mm_nt(act_ref[0],t2_ref[0])
    for s in range(1,S): sec=sec+mm_nt(act_ref[s],t2_ref[s])
    con=(sec+tb_ref[1:2,:])+con
    con_ref[...]=con
    cond=con/(1.0+jnp.exp(-con))
    call_ref[shard]=cond.astype(bf)
    cc=lambda k: send(call_ref.at[shard],call_ref.at[shard],cs_.at[k-1],cr_.at[k-1],speer(k))
    for k in range(1,S): cc(k).start()
    cgs[...]=cond.reshape(S,R,8,own)
    cg=cgs[:,rep].reshape(S*8,own).astype(bf)
    first=lax.rem(lax.broadcasted_iota(jnp.int32,(S*8,1),0),8)<4
    for b in range(6):
        sl=slice(b*D,(b+1)*D)
        v=jnp.where(first,mm(cg,ada_ref[0,:,sl]),mm(cg,ada_ref[1,:,sl]))
        pm[:,:,:,sl]=v.reshape(nz,2,8,D)
    mc=send(pm.at[:,1-c],mr,ms,mrs,mate)
    mc.start()
    for t in ticks[2*U:4*U]: t()
    mc.wait_recv()
    ps[...]=pm[:,c]+mr[...]
    zc=lambda k: send(ps.at[lax.rem(z+k,nz)],zrv.at[k-1],pz.at[k-1],pzr.at[k-1],(rep,2*lax.rem(z+k,nz)+c))
    for k in range(1,nz): zc(k).start()
    for k in range(1,S): cc(k).wait_recv()
    fp=mm(call_ref[0],fin_ref[0])
    for s in range(1,S): fp=fp+mm(call_ref[s],fin_ref[s])
    fps[...]=(fp+finb_ref[0:1,:]).reshape(S,R,8,fin_ref.shape[2])
    vc=lambda k: send(fps.at[lax.rem(shard+k,S),rep],fm_ref.at[shard],vs.at[k-1],vr.at[k-1],speer(k))
    for k in range(1,S): vc(k).start()
    fm_ref[shard]=fps[shard,rep]
    for t in ticks[4*U:]: t()
    total=ps[z]
    for k in range(1,nz): zc(k).wait_recv(); total=total+zrv[k-1]
    mod_ref[...]=total
    for k in range(1,S): vc(k).wait_recv(); smc(k).wait_recv()
    for m in range(1,R): f1(m).wait_send()
    for k in range(1,S):
        for cp in (f2,smc,ac,cc,vc): cp(k).wait_send()
    mc.wait_send()
    for k in range(1,nz): zc(k).wait_send()
    ga.finish()

def first_call(w,fo,sm,t1,t2,cls,tb,ada,fin,finb,R,S,cid):
    U,_,own,W=w.shape; nz=S//2; NP=S*R*8; FC=fin.shape[2]
    dma=pltpu.SemaphoreType.DMA; V=pltpu.VMEM; sd=jax.ShapeDtypeStruct
    any_=pl.BlockSpec(memory_space=pl.ANY); vm=pl.BlockSpec(memory_space=pltpu.VMEM)
    return pl.pallas_call(functools.partial(first_kernel,R,nz,U,own),
        in_specs=[vm]*10, out_specs=[any_]+[vm]*8,
        out_shape=[sd((U,R,nz,2,own,W),bf),sd((S,R,8,384),f32),sd((S,)+sm.shape,bf),sd((NP,own),f32),sd((S,NP,own),bf),sd((NP,own),f32),sd((S,NP,own),bf),sd((8,6*D),f32),sd((S,8,FC),f32)],
        scratch_shapes=[V((S,R,8,own),f32),V((nz,2,8,6*D),f32),V((nz,8,6*D),f32),V((nz,8,6*D),f32),V((max(nz-1,1),8,6*D),f32),V((S,R,8,FC),f32),
            dma((R-1,)),dma((R-1,))]+[dma((S-1,))]*8+[dma(()),dma(()),dma((nz-1,)),dma((nz-1,)),dma((S-1,)),dma((S-1,))]+gather_sems(R,nz,U),
        compiler_params=pltpu.CompilerParams(collective_id=cid,has_side_effects=True,vmem_limit_bytes=VLIM),
    )(w,fo,sm,t1,t2,cls,tb,ada,fin,finb)

def fwd_gather_kernel(R,nz,U,x_ref,mod_ref,bias_ref,wa_ref,w1_ref,w2_ref,w_ref,*rest):
    outs=rest[:11]; out_ref=rest[11]; gsems=rest[12:]
    i=pl.program_id(0); last=pl.num_programs(0)-1
    ga=Gather(R,nz,U,w_ref,out_ref,*gsems)
    @pl.when(i==0)
    def _():
        meet(ga.peers()); ga.start()
    ticks=ga.ticks(); used=set()
    def hook(p):
        for step in range(4):
            n=12*step+p-6
            if n>=0 and n%2==0 and n//2<len(ticks):
                used.add(n//2)
                pl.when(i==step)(ticks[n//2])
    fwd_kernel(x_ref,mod_ref,bias_ref,wa_ref,w1_ref,w2_ref,*outs,hook=hook)
    @pl.when(i==last)
    def _():
        for n,t in enumerate(ticks):
            if n not in used: t()
        ga.finish()
FWD_WIDTHS=[(D,bf),(3*D,bf),(128,f32),(D,bf),(D,f32),(D,f32),(D,bf),(FF,f32),(FF,bf),(D,f32),(D,f32)]
def layer_fwd_gather(x,mod,bias,full_w,w,R,S,cid):
    T=x.shape[0]; n=T//TOK; U,_,own,W=w.shape; nz=S//2
    sd=jax.ShapeDtypeStruct
    any_=pl.BlockSpec(memory_space=pl.ANY)
    o=pl.pallas_call(functools.partial(fwd_gather_kernel,R,nz,U),grid=(n,),
        in_specs=[rows(D),pl.BlockSpec((1,8,D),lambda i:(i,0,0)),full((16,D)),unit(0),unit(1),unit(2),pl.BlockSpec(memory_space=pltpu.VMEM)],
        out_specs=[rows(v) for v,_ in FWD_WIDTHS]+[any_],
        out_shape=[sd((T,v),t) for v,t in FWD_WIDTHS]+[sd((U,R,nz,2,own,W),bf)],
        scratch_shapes=gather_sems(R,nz,U),
        compiler_params=pltpu.CompilerParams(collective_id=cid,has_side_effects=True,vmem_limit_bytes=VLIM),
        cost_estimate=pl.CostEstimate(flops=2*T*(9216*D+2*TOK*D),bytes_accessed=60_000_000,transcendentals=T*FF*2),
    )(x,mod,bias,full_w,full_w,full_w,w)
    return o[:11],o[11]
CW=384; NCH=8
def bit_orders(R):
    bits=[1<<i for i in range(R.bit_length()-1)]
    return [bits[g%len(bits):]+bits[:g%len(bits)] if bits else [] for g in range(NCH//R)]
def grad_plan(R):
    orders=bit_orders(R); G=NCH//R; n=len(orders[0])
    def stage(g,m): return next(i for i,b in enumerate(orders[g]) if m&b)
    pos=[]
    for i in range(n+1):
        ms=[[m for m in range(R) if (m==0 and i==n) or (m and stage(g,m)==i)] for g in range(G)]
        if i<n: ms=[sorted(v,key=lambda m,g=g:(-bin(m).count("1"),m)) for g,v in enumerate(ms)]
        for a in range(len(ms[0])):
            for g in range(G): pos.append((g,ms[g][a],i))
    send={}; keep={}; recv={}
    for g,m,i in pos:
        if m: send[g,m]=len(send)
        if i>0 or m==0: keep[g,m]=len(keep)
    for i in range(n):
        for g in range(G):
            for m in range(R):
                if not any(m&b for b in orders[g][:i+1]): recv[g,i,m]=len(recv)
    return orders,n,pos,send,keep,recv

def remote(src,dst,ssem,rsem,dev): return pltpu.make_async_remote_copy(src_ref=src,dst_ref=dst,send_sem=ssem,recv_sem=rsem,device_id=dev,device_id_type=MESH)
def everyone(R,nz):
    rep=lax.axis_index("rep"); shard=lax.axis_index("shard"); z=shard//2; c=lax.rem(shard,2)
    return [(rep,2*z+1-c)]+[(rep,2*lax.rem(z+k,nz)+c) for k in range(1,nz)]+[(jnp.bitwise_xor(rep,m),shard) for m in range(1,R)]
class Sums:
    def __init__(self,R,nz,own,nu,xi,xs,dys,out_ref,scr):
        (self.xin,self.xt,self.dy,self.sbuf,self.obuf,self.rbuf,self.sb,self.rb,self.kf,
         self.xsem,self.dsem,self.csend,self.crecv,self.ssem,self.rsem)=scr
        self.R,self.nz,self.own,self.nu,self.xi,self.xs,self.dys,self.out=R,nz,own,nu,xi,xs,dys,out_ref
        self.orders,self.n,self.pos,self.send,self.keep,self.recv=grad_plan(R)
        self.G=NCH//R
        self.rep=lax.axis_index("rep"); self.shard=lax.axis_index("shard")
        self.z=self.shard//2; self.c=lax.rem(self.shard,2)
        self.mate=(self.rep,2*self.z+1-self.c)
    def xor(self,m): return jnp.bitwise_xor(self.rep,m)
    def rdev(self,m): return (self.xor(m),self.shard)
    def chunk(self,k): return self.pos[k][0]*self.R+self.xor(self.pos[k][1])
    def xcopy(self,i): return pltpu.make_async_copy(self.xs[i],self.xin.at[i],self.xsem.at[i])
    def dstart(self,u,k):
        for i,ref in enumerate(self.dys):
            @pl.when(u==i)
            def _(): pltpu.make_async_copy(ref.at[:,pl.ds(pl.multiple_of(self.chunk(k)*CW,128),CW)],self.dy.at[k%4],self.dsem.at[k%4]).start()
    def dwait(self,k): pltpu.make_async_copy(self.dys[0].at[:,pl.ds(0,CW)],self.dy.at[k%4],self.dsem.at[k%4]).wait()
    def ccopy(self,k): return remote(self.sbuf.at[k%2],self.rbuf.at[k%4],self.csend.at[k%2],self.crecv.at[k%4],self.mate)
    def scopy(self,u,g,m):
        i=next(i for i,b in enumerate(self.orders[g]) if m&b); b=self.orders[g][i]
        a=self.send[g,m]; d=self.recv[g,i,m^b]
        return remote(self.sb.at[u,a],self.rb.at[u,d],self.ssem.at[u,a],self.rsem.at[u,d],self.rdev(b))
    def rwait(self,u,g,i,m):
        d=self.recv[g,i,m]
        remote(self.sb.at[u,0],self.rb.at[u,d],self.ssem.at[u,0],self.rsem.at[u,d],self.rdev(1)).wait_recv()
    def load(self):
        self.xcopy(0).start(); self.xcopy(1).start(); self.dstart(0,0); self.dstart(0,1)
        for i in range(2):
            self.xcopy(i).wait()
            self.xt[i]=self.xin[i].T
    def consume(self,u,k):
        g,m,i=self.pos[k]
        self.ccopy(k).wait_recv()
        total=self.obuf[k%2]+self.rbuf[k%4]
        if i==0 and m:
            self.sb[u,self.send[g,m]]=total.astype(bf)
            self.scopy(u,g,m).start()
        else: self.kf[u,self.keep[g,m]]=total.reshape(self.nz,self.own,CW)
    def products(self,u):
        nz,own=self.nz,self.own
        for k in range(NCH):
            if k+2<NCH: self.dstart(u,k+2)
            else:
                @pl.when(u<self.nu-1)
                def _(): self.dstart(u+1,k+2-NCH)
            self.dwait(k)
            p=mm(self.xt[self.xi(u,self.chunk(k))],self.dy[k%4]).reshape(nz,2,own,CW)
            even=p[:,0].reshape(nz*own,CW); odd=p[:,1].reshape(nz*own,CW)
            if k>=2: self.ccopy(k).wait_send()
            else:
                @pl.when(u>0)
                def _(): self.ccopy(k).wait_send()
            self.sbuf[k%2]=jnp.where(self.c==0,odd,even)
            self.obuf[k%2]=jnp.where(self.c==0,even,odd)
            self.ccopy(k).start()
            if k>0: self.consume(u,k-1)
            else:
                @pl.when(u>0)
                def _(): self.consume(u-1,NCH-1)
    def middle(self,u,i):
        for g,m,j in self.pos:
            if m and j==i:
                v=self.kf[u,self.keep[g,m]].reshape(self.nz*self.own,CW)
                for i2 in range(i):
                    self.rwait(u,g,i2,m); v=v+self.rb[u,self.recv[g,i2,m]].astype(f32)
                self.sb[u,self.send[g,m]]=v.astype(bf)
                self.scopy(u,g,m).start()
    def form(self):
        def one(t,_):
            self.products(t)
            if self.n>1:
                @pl.when(t>=1)
                def _(): self.middle(t-1,1)
            return 0
        lax.fori_loop(0,self.nu,one,0)
        self.consume(self.nu-1,NCH-1)
    def stage(self,i):
        if i<self.n:
            for u in range(self.nu-1 if i==1 else 0,self.nu): self.middle(u,i)
    def hold(self):
        for u in range(self.nu):
            for g in range(self.G):
                v=self.kf[u,self.keep[g,0]]
                for i2 in range(self.n):
                    self.rwait(u,g,i2,0); v=v+self.rb[u,self.recv[g,i2,0]].astype(f32).reshape(self.nz,self.own,CW)
                self.out[u,g]=v
    def finish(self):
        for u in range(self.nu):
            for g in range(self.G):
                for m in range(1,self.R): self.scopy(u,g,m).wait_send()
        self.ccopy(NCH-2).wait_send(); self.ccopy(NCH-1).wait_send()
class Tail:
    def __init__(self,R,nz,own,nu,fin,out_ref,scr):
        (self.zs,self.zr,self.az,self.zss,self.zrs,self.ass,self.ars,self.als)=scr
        self.R,self.nz,self.own,self.nu,self.fin,self.out,self.G=R,nz,own,nu,fin,out_ref,NCH//R
        self.rep=lax.axis_index("rep"); self.shard=lax.axis_index("shard")
        self.z=self.shard//2; self.c=lax.rem(self.shard,2)
    def xor(self,m): return jnp.bitwise_xor(self.rep,m)
    def zdev(self,k): return (self.rep,2*lax.rem(self.z+k,self.nz)+self.c)
    def rdev(self,m): return (self.xor(m),self.shard)
    def each(self): return [(u,g) for u in range(self.nu) for g in range(self.G)]
    def zcopy(self,u,g,k): return remote(self.zs.at[u,g,lax.rem(self.z+k,self.nz)],self.zr.at[u,g,k-1],self.zss.at[u,g,k-1],self.zrs.at[u,g,k-1],self.zdev(k))
    def acopy(self,u,g,m): return remote(self.az.at[u,g],self.out.at[u,g*self.R+self.rep],self.ass.at[u,g,m-1],self.ars.at[u,g,m-1],self.rdev(m))
    def arecv(self,u,g,m): return remote(self.az.at[u,g],self.out.at[u,g*self.R+self.xor(m)],self.ass.at[u,g,m-1],self.ars.at[u,g,m-1],self.rdev(m))
    def alocal(self,u,g): return pltpu.make_async_copy(self.az.at[u,g],self.out.at[u,g*self.R+self.rep],self.als.at[u,g])
    def along(self):
        for u,g in self.each():
            self.zs[u,g]=self.fin[u,g].astype(bf)
            for k in range(1,self.nz): self.zcopy(u,g,k).start()
    def spread(self):
        for u,g in self.each():
            v=self.fin[u,g,self.z]
            for k in range(1,self.nz):
                self.zcopy(u,g,k).wait_recv(); v=v+self.zr[u,g,k-1].astype(f32)
            self.az[u,g]=v
            self.alocal(u,g).start()
            for m in range(1,self.R): self.acopy(u,g,m).start()
    def finish(self):
        for u,g in self.each():
            self.alocal(u,g).wait()
            for m in range(1,self.R): self.arecv(u,g,m).wait_recv(); self.acopy(u,g,m).wait_send()
            for k in range(1,self.nz): self.zcopy(u,g,k).wait_send()
    def squares(self):
        v=jnp.zeros((8,128),f32)
        for u,g in self.each():
            b=self.az[u,g]; b=b*b
            for q in range(CW//128): v=v+jnp.sum(b[:,q*128:(q+1)*128].reshape(self.own//8,8,128),axis=0)
        return v
def sums_scratch(R,nz,own,T,nu):
    orders,n,pos,send,keep,recv=grad_plan(R)
    dma=pltpu.SemaphoreType.DMA; V=pltpu.VMEM
    ns,nk,nr=max(len(send),1),len(keep),max(len(recv),1)
    return [V((2,T,D),bf),V((2,D,T),bf),V((4,T,CW),bf),V((2,D//2,CW),f32),V((2,D//2,CW),f32),V((4,D//2,CW),f32),
            V((nu,ns,D//2,CW),bf),V((nu,nr,D//2,CW),bf),V((nu,nk,nz,own,CW),f32),
            dma((2,)),dma((4,)),dma((2,)),dma((4,)),dma((nu,ns)),dma((nu,nr))]
def tail_scratch(R,nz,own,nu):
    G=NCH//R; dma=pltpu.SemaphoreType.DMA; V=pltpu.VMEM
    return [V((nu,G,nz,own,CW),bf),V((nu,G,nz-1,own,CW),bf),V((nu,G,own,CW),f32),dma((nu,G,nz-1)),dma((nu,G,nz-1)),dma((nu,G,R-1)),dma((nu,G,R-1)),dma((nu,G))]
NSUM=15; NTAIL=8
def remote(src,dst,ssem,rsem,dev): return pltpu.make_async_remote_copy(src_ref=src,dst_ref=dst,send_sem=ssem,recv_sem=rsem,device_id=dev,device_id_type=MESH)
def everyone(R,nz):
    rep=lax.axis_index("rep"); shard=lax.axis_index("shard"); z=shard//2; c=lax.rem(shard,2)
    return [(rep,2*z+1-c)]+[(rep,2*lax.rem(z+k,nz)+c) for k in range(1,nz)]+[(jnp.bitwise_xor(rep,m),shard) for m in range(1,R)]
MLP_X=lambda u,ch: u
ATTN_X=lambda u,ch: ch//6
def carrier_kernel(R,nz,own,nu,xi,nt,compute,ci,co,extra,ei,eo,*refs):
    p=0; parts=[]
    t1=1 if nt else 0
    for cnt in (ci,2+nu,t1,ei,co,1,2*t1,eo,NSUM,NTAIL*t1,len(refs)): parts.append(refs[p:p+cnt]); p+=cnt
    cin,rin,tin,ein,cout,(hold_ref,),tout,eout,scr,tscr,escr=parts
    S_=Sums(R,nz,own,nu,xi,rin[:2],rin[2:],hold_ref,scr)
    T_=Tail(R,nz,own,nt,tin[0],tout[0],tscr) if nt else None
    events=extra(R,nz,ein,eout,escr) if extra else {}
    i=pl.program_id(0); last=pl.num_programs(0)-1
    @pl.when(i==0)
    def _():
        S_.load()
        meet(everyone(R,nz))
        if T_: T_.along()
        for f in events.get(0,[]): f()
        S_.form()
    for q in (1,2,3):
        @pl.when(i==q)
        def _():
            S_.stage(q)
            if T_ and q==2: T_.spread()
            for f in events.get(q,[]): f()
    compute(*cin,*cout)
    @pl.when(i==last)
    def _():
        S_.hold(); S_.finish()
        if T_:
            T_.finish(); tout[1][...]=T_.squares()
        for f in events.get(99,[]): f()
def carry(R,S,cid,xs,dys,xi,tail,compute,cargs,cspecs,coshapes,cospecs,cost,extra=None):
    T=xs[0].shape[0]; nz=S//2; own=D//S; nu=len(dys); G=NCH//R
    any_=pl.BlockSpec(memory_space=pl.ANY); sd=jax.ShapeDtypeStruct
    f,eargs,especs,eshapes,eospecs,escratch=extra or (None,[],[],[],[],[])
    nt=tail[0].shape[0] if tail else 0
    held=(nu,G,nz,own,CW)
    o=pl.pallas_call(functools.partial(carrier_kernel,R,nz,own,nu,xi,nt,compute,len(cargs),len(coshapes),f,len(eargs),len(eshapes)),grid=(T//TOK,),
        in_specs=list(cspecs)+[any_]*(2+nu)+[full(t.shape) for t in tail]+especs,
        out_specs=list(cospecs)+[full(held)]+([any_,full((8,128))] if nt else [])+eospecs,
        out_shape=list(coshapes)+[sd(held,f32)]+([sd((nt,NCH,own,CW),f32),sd((8,128),f32)] if nt else [])+eshapes,
        scratch_shapes=sums_scratch(R,nz,own,T,nu)+(tail_scratch(R,nz,own,nt) if nt else [])+escratch,
        compiler_params=pltpu.CompilerParams(collective_id=cid,has_side_effects=True,vmem_limit_bytes=VLIM),
        cost_estimate=cost)(*cargs,*xs,*dys,*tail,*eargs)
    a=len(coshapes); b=a+1+(2 if nt else 0)
    return o[:a],o[a],o[a+1:b],o[b:]
def last_kernel(R,nz,own,sums,nt,extra,ei,eo,*refs):
    k=1 if sums else 0; p=0; parts=[]
    for cnt in (3*k,k,ei,4*k,eo,NSUM*k,k,NTAIL*k,NTAIL*k,len(refs)): parts.append(refs[p:p+cnt]); p+=cnt
    rin,tin,ein,rout,eout,scr,held,t1scr,t2scr,escr=parts
    if sums:
        S_=Sums(R,nz,own,1,ATTN_X,rin[:2],rin[2:],held[0],scr)
        T1=Tail(R,nz,own,nt,tin[0],rout[0],t1scr); T2=Tail(R,nz,own,1,held[0],rout[2],t2scr)
    def squares():
        return T1.squares()+T2.squares()
    events=extra(R,nz,ein,eout,escr,squares if sums else None)
    run=lambda q: [f() for f in events.get(q,[])]
    if sums: S_.load()
    meet(everyone(R,nz))
    if sums: T1.along()
    run(0)
    if sums: S_.form(); S_.stage(1)
    run(1)
    if sums:
        for i in range(2,S_.n): S_.stage(i)
        T1.spread(); S_.hold(); T2.along()
    run(2)
    run(3)
    if sums: T2.spread()
    run(4)
    if sums:
        S_.finish(); T1.finish(); T2.finish()
        rout[1][...]=T1.squares(); rout[3][...]=T2.squares()
    run(99)
def last_call(R,S,cid,xs,dys,tail,extra):
    nz=S//2; own=D//S; sums=bool(xs); G=NCH//R
    any_=pl.BlockSpec(memory_space=pl.ANY); sd=jax.ShapeDtypeStruct; vm=pl.BlockSpec(memory_space=pltpu.VMEM)
    f,eargs,especs,eshapes,eospecs,escratch=extra
    nt=tail[0].shape[0] if sums else 0
    mine=[]
    if sums: mine=sums_scratch(R,nz,own,xs[0].shape[0],1)+[pltpu.VMEM((1,G,nz,own,CW),f32)]+tail_scratch(R,nz,own,nt)+tail_scratch(R,nz,own,1)
    return pl.pallas_call(functools.partial(last_kernel,R,nz,own,sums,nt,f,len(eargs),len(eshapes)),
        in_specs=[any_]*(len(xs)+len(dys))+[vm]*len(tail)+especs,out_specs=([any_,vm,any_,vm] if sums else [])+eospecs,
        out_shape=([sd((nt,NCH,own,CW),f32),sd((8,128),f32),sd((1,NCH,own,CW),f32),sd((8,128),f32)] if sums else [])+eshapes,
        scratch_shapes=mine+escratch,
        compiler_params=pltpu.CompilerParams(collective_id=cid,has_side_effects=True,vmem_limit_bytes=VLIM))(*xs,*dys,*tail,*eargs)
def sums_call(R,S,cid,xs,dys,tail):
    none=lambda R,nz,ins,outs,scr,squares: {}
    return last_call(R,S,cid,xs,dys,tail,(none,[],[],[],[],[]))

def rows_events(R,nz,ins,outs,scr):
    (w,),(g,)=ins,outs; rs,rr,zs,zr,cs,cr,ls=scr
    rep=lax.axis_index("rep"); shard=lax.axis_index("shard"); z=shard//2; c=lax.rem(shard,2)
    loc=lambda: pltpu.make_async_copy(w,g.at[rep,z,c],ls)
    rc=lambda m: remote(w,g.at[rep,z,c],rs.at[m-1],rr.at[m-1],(jnp.bitwise_xor(rep,m),shard))
    zc=lambda k: remote(g.at[:,z,c],g.at[:,z,c],zs.at[k-1],zr.at[k-1],(rep,2*lax.rem(z+k,nz)+c))
    cc=lambda: remote(g.at[:,:,c],g.at[:,:,c],cs,cr,(rep,2*z+1-c))
    def a():
        loc().start()
        for m in range(1,R): rc(m).start()
    def b():
        loc().wait()
        for m in range(1,R): rc(m).wait_recv()
        for k in range(1,nz): zc(k).start()
    def d():
        for k in range(1,nz): zc(k).wait_recv()
        cc().start()
    def e():
        cc().wait()
        for m in range(1,R): rc(m).wait_send()
        for k in range(1,nz): zc(k).wait_send()
    return {0:[a],1:[b],2:[d],99:[e]}
def rows_extra(w,R,S):
    nz=S//2; dma=pltpu.SemaphoreType.DMA
    return (rows_events,[w],[full(w.shape)],[jax.ShapeDtypeStruct((R,nz,2)+w.shape,bf)],[pl.BlockSpec(memory_space=pl.ANY)],
        [dma((R-1,)),dma((R-1,)),dma((nz-1,)),dma((nz-1,)),dma(()),dma(()),dma(())])

class ShardSum:
    def __init__(self,nz,x,mr,ps,zr,ms,mrs,zs,zrs):
        self.nz,self.x,self.mr,self.ps,self.zr=nz,x,mr,ps,zr
        self.ms,self.mrs,self.zs,self.zrs=ms,mrs,zs,zrs
        self.rep=lax.axis_index("rep"); shard=lax.axis_index("shard"); self.z=shard//2; self.c=lax.rem(shard,2)
    def mate(self): return remote(self.x.at[:,1-self.c],self.mr,self.ms,self.mrs,(self.rep,2*self.z+1-self.c))
    def far(self,k):
        t=lax.rem(self.z+k,self.nz)
        return remote(self.ps.at[t],self.zr.at[k-1],self.zs.at[k-1],self.zrs.at[k-1],(self.rep,2*t+self.c))
    def one(self): self.mate().start()
    def two(self):
        self.mate().wait_recv()
        self.ps[...]=self.x[:,self.c]+self.mr[...]
        for k in range(1,self.nz): self.far(k).start()
    def three(self):
        v=self.ps[self.z]
        for k in range(1,self.nz): self.far(k).wait_recv(); v=v+self.zr[k-1]
        return v
    def end(self):
        self.mate().wait_send()
        for k in range(1,self.nz): self.far(k).wait_send()
def shard_sum_scratch(nz,shape,own_input):
    V=pltpu.VMEM; dma=pltpu.SemaphoreType.DMA
    return ([V((nz,2)+shape,f32)] if own_input else [])+[V((nz,)+shape,f32),V((nz,)+shape,f32),V((nz-1,)+shape,f32),dma(()),dma(()),dma((nz-1,)),dma((nz-1,))]

def sig_back(v,g):
    t=1.0/(1.0+jnp.exp(-v))
    return g*(t*(1.0+v*(1.0-t)))
def fold(v):
    v=v*v; r,c=v.shape
    if r%8: v=jnp.concatenate([v,jnp.zeros((8-r%8,c),f32)],axis=0)
    v=jnp.sum(v.reshape(-1,8,c),axis=0)
    if c%128: v=jnp.concatenate([v,jnp.zeros((8,128-c%128),f32)],axis=1)
    t=v[:,:128]
    for q in range(1,v.shape[1]//128): t=t+v[:,q*128:(q+1)*128]
    return t
HEAD_ROWS=24
FIN_ROW=45
def cond_events(R,nz,ins,outs,scr,squares):
    (rows_ref,fin_ref,cond_ref,call_ref,act_ref,pre_ref,lab_ref,feat_ref,ada_ref,finw_ref,t2_ref,w_ref)=ins[:12]
    pieces=ins[12:-1]; sq1_ref=ins[-1]
    adag,fing,secg,clsg,firg,vec,sumo,headg,norm_ref=outs
    S=2*nz
    fx,tx,sx,asm=scr[0],scr[8],scr[16],scr[24]
    fs=ShardSum(nz,*scr[0:8]); ts=ShardSum(nz,*scr[8:16]); ss=ShardSum(nz,*scr[16:24])
    g0=scr[25]
    re=rows_events(R,nz,(w_ref,),(g0,),scr[26:33])
    tot,rr,rsem,rrs,gc_s,hs,hr,hcs,hcr,nv,n1,n2,n3,nsem,nrec=scr[33:]
    rep=lax.axis_index("rep"); shard=lax.axis_index("shard"); z=shard//2; c=lax.rem(shard,2)
    nr=sumo.shape[0]; own=sumo.shape[1]; nb=nr-HEAD_ROWS; FC=fin_ref.shape[1]
    mate=(rep,2*z+1-c); zdev=lambda k: (rep,2*lax.rem(z+k,nz)+c); rdev=lambda m: (jnp.bitwise_xor(rep,m),shard)
    rc=lambda m: remote(tot,rr.at[rep],rsem.at[m-1],rrs.at[m-1],rdev(m))
    hz=lambda k: remote(headg.at[z,c],headg.at[z,c],hs.at[k-1],hr.at[k-1],zdev(k))
    hc=lambda: remote(headg.at[:,c],headg.at[:,c],hcs,hcr,mate)
    M6=6*D
    def gather():
        asm[...]=jnp.zeros(asm.shape,f32)
        for l in range(2):
            db1,db2,dm1,dm2=pieces[4*l:4*l+4]; o=14*l
            asm[o:o+2]=db2[0:2]; asm[o+2:o+7]=db1[2:7]; asm[o+13:o+14]=db1[13:14]
            t1=jnp.sum(dm1[...],axis=0); t2=jnp.sum(dm2[...],axis=0)
            asm[o+7:o+9]=t2[0:2]; asm[o+9:o+13]=t1[2:6]
        pg,pb,gfm,hd=pieces[8:]
        asm[28:44]=pg[...]; asm[44:45]=pb[...]
        asm[FIN_ROW:FIN_ROW+2]=jnp.sum(gfm[...],axis=0)
        asm[nb:]=hd[...]
        for s in range(S):
            sx[s//2,s%2]=asm[:,s*own:(s+1)*own]
            for r in range(FC//own):
                p=s*FC+r*own; row=FIN_ROW+p//D
                sx[s//2,s%2,FIN_ROW+r:FIN_ROW+r+1,:]=asm[row:row+1,p%D:p%D+own]
        ss.one()
        fin=fin_ref[...]
        for s in range(S): fx[s//2,s%2]=mm_nt(finw_ref[s],fin)
        fs.one()
    def layer1():
        gc=jnp.zeros(gc_s.shape,f32)
        for q in range(6):
            o=slice(q*D,(q+1)*D); r=rows_ref[:,o]
            adag[1,:,o]=mm(cond_ref[...],r)
            gc=gc+mm_nt(ada_ref[1,:,o],r)
        gc_s[...]=gc
        fing[...]=mm_tn(fin_ref[...],call_ref[...])
        fs.two(); ss.two()
    def total():
        tot[...]=ss.three()
        rr[rep]=tot[...]
        for m in range(1,R): rc(m).start()
    def layer0():
        for f in re[99]: f()
        N=cond_ref.shape[1]; M=4*N; B=M6//4
        g=g0[...].reshape(M,B)
        wide=jnp.zeros((own,M),f32)
        at=lax.broadcasted_iota(jnp.int32,(1,M),1)
        n_of=lax.broadcasted_iota(jnp.int32,(N,1),0)
        for j in range(4):
            o=slice(j*B,(j+1)*B)
            spot=jnp.where(at==4*n_of+j,1.0,0.0).astype(bf)
            adag[0,:,o]=mm(mm(cond_ref[...],spot).astype(bf),g)
            wide=wide+jnp.where(at-4*(at//4)==j,mm_nt(ada_ref[0,:,o],g),0.0)
        pick=jnp.where(lax.broadcasted_iota(jnp.int32,(M,1),0)//4==lax.broadcasted_iota(jnp.int32,(1,N),1),1.0,0.0)
        gc=gc_s[...]+lax.dot_general(wide,pick,(((1,),(0,)),((),())),precision=lax.Precision.HIGHEST,preferred_element_type=f32)
        g=sig_back(pre_ref[1],gc+fs.three())
        low=g.astype(bf)
        for s in range(S): tx[s//2,s%2]=mm_tn(t2_ref[s],low)
        ts.one()
        vec[0]=jnp.broadcast_to(jnp.sum(g,axis=1,keepdims=True),vec.shape[1:])
        secg[...]=mm(low,act_ref[...])
        hot=jnp.where(lab_ref[...]==lax.broadcasted_iota(jnp.int32,(1,clsg.shape[1]),1).astype(f32),1.0,0.0)
        clsg[...]=lax.dot_general(g,hot,(((1,),(0,)),((),())),precision=lax.Precision.HIGHEST,preferred_element_type=f32)
    def time_and_sums():
        ts.two()
        for m in range(1,R): rc(m).wait_recv()
        v=rr[0]
        for r in range(1,R): v=v+rr[r]
        sumo[...]=v
        headg[z,c]=v[nb:]
        for k in range(1,nz): hz(k).start()
        first=lax.broadcasted_iota(jnp.int32,(1,128),1)<1
        p=fold(v[:nb])+fold(jnp.where(first,vec[0],0.0))
        for q in range(2): p=p+fold(adag[q])
        for ref in (fing,secg,clsg): p=p+fold(ref[...])
        g=sig_back(pre_ref[0],ts.three())
        b=jnp.broadcast_to(jnp.sum(g,axis=1,keepdims=True),vec.shape[1:])
        vec[1]=b
        f=mm(g.astype(bf),feat_ref[...])
        firg[...]=f
        p=p+fold(f)+fold(jnp.where(first,b,0.0))
        nv[...]=jnp.where(rep==0,p,0.0)
        for k in range(1,nz): hz(k).wait_recv()
        hc().start()
    def end():
        hc().wait()
        for k in range(1,nz): hz(k).wait_send()
        for m in range(1,R): rc(m).wait_send()
        fs.end(); ts.end(); ss.end()
        nv[...]=nv[...]+sq1_ref[...]+(squares() if squares else 0.0)
        cp=remote(nv,n1,nsem.at[0],nrec.at[0],mate)
        cp.start(); cp.wait()
        n2[z]=nv[...]+n1[...]
        nz_=lambda k: remote(n2.at[z],n2.at[z],nsem.at[k],nrec.at[k],zdev(k))
        for k in range(1,nz): nz_(k).start()
        for k in range(1,nz): nz_(k).wait()
        v=n2[0]
        for q in range(1,nz): v=v+n2[q]
        n3[rep]=v
        nr_=lambda m: remote(n3.at[rep],n3.at[rep],nsem.at[nz-1+m],nrec.at[nz-1+m],rdev(m))
        for m in range(1,R): nr_(m).start()
        for m in range(1,R): nr_(m).wait()
        v=n3[0]
        for r in range(1,R): v=v+n3[r]
        for s in range(S): v=v+fold(headg[s//2,s%2,:HEAD_ROWS-1])
        norm_ref[...]=v
    return {0:re[0]+[gather],1:re[1]+[layer1],2:re[2]+[total],3:[layer0],4:[time_and_sums],99:[end]}
def cond_extra(args,R,S):
    nz=S//2; own=D//S; N=args[2].shape[1]; nr=48+HEAD_ROWS; FC=args[1].shape[1]; w=args[11]
    vm=pl.BlockSpec(memory_space=pltpu.VMEM); sd=jax.ShapeDtypeStruct; dma=pltpu.SemaphoreType.DMA; V=pltpu.VMEM
    shapes=[sd((2,own,6*D),f32),sd((FC,D),f32),sd((own,D),f32),sd((own,1024),f32),sd((own,256),f32),sd((2,own,128),f32),sd((nr,own),f32),sd((nz,2,HEAD_ROWS,own),f32),sd((8,128),f32)]
    scratch=shard_sum_scratch(nz,(own,N),True)*2+shard_sum_scratch(nz,(nr,own),True)+[V((nr,D),f32),V((R,nz,2)+w.shape,bf)]
    scratch+=[dma((R-1,)),dma((R-1,)),dma((nz-1,)),dma((nz-1,)),dma(()),dma(()),dma(())]
    scratch+=[V((nr,own),f32),V((R,nr,own),f32),dma((R-1,)),dma((R-1,)),V((own,N),f32),
        dma((nz-1,)),dma((nz-1,)),dma(()),dma(()),V((8,128),f32),V((8,128),f32),V((nz,8,128),f32),V((R,8,128),f32),dma((nz+R,)),dma((nz+R,))]
    return (cond_events,list(args),[vm]*len(args),shapes,[vm]*len(shapes),scratch)

def head_kernel(inv,x_ref,fm_ref,hw_ref,hb_ref,tn_ref,gx_ref,gfm_ref,hg_ref):
    i=pl.program_id(0)
    x=x_ref[...]
    sh=fm_ref[0,0:1,:]; sc=fm_ref[0,1:2,:]
    xh,r=ln_parts(x)
    nrm=(xh*(1.0+sc)+sh).astype(bf)
    diff=mm(nrm,hw_ref[...])+hb_ref[0:1,:]-tn_ref[0].T
    g=2.0*(diff*inv)
    low=g.astype(bf)
    @pl.when(i==0)
    def _():
        hg_ref[...]=jnp.zeros_like(hg_ref)
    p=low.shape[1]
    hg_ref[:p]+=mm_tn(low,nrm)
    hg_ref[p:p+1,:p]+=jnp.sum(g,axis=0,keepdims=True)
    hg_ref[HEAD_ROWS-1:HEAD_ROWS,:p]+=jnp.sum(diff*diff,axis=0,keepdims=True)
    gn=mm_nt(low,hw_ref[...])
    gfm_ref[0,0:1,:]=jnp.sum(gn,axis=0,keepdims=True)
    gfm_ref[0,1:2,:]=jnp.sum(gn*xh,axis=0,keepdims=True)
    gx_ref[...]=ln_back(gn,xh,r,sc)
def head(x,fm,hw,hb,tn,inv):
    T=x.shape[0]; n=T//TOK; sd=jax.ShapeDtypeStruct; p=hw.shape[1]
    m2=pl.BlockSpec((1,2,D),lambda i:(i,0,0))
    fixed=lambda *s: pl.BlockSpec(s,lambda i:(0,)*len(s))
    return pl.pallas_call(functools.partial(head_kernel,inv),grid=(n,),
        in_specs=[rows(D),m2,fixed(D,p),fixed(1,p),pl.BlockSpec((1,p,TOK),lambda i:(i,0,0))],
        out_specs=[rows(D),m2,fixed(HEAD_ROWS,D)],
        out_shape=[sd((T,D),f32),sd((n,2,D),f32),sd((HEAD_ROWS,D),f32)],
        compiler_params=pltpu.CompilerParams(vmem_limit_bytes=VLIM))(x,fm,hw,hb,tn)
LAYERS=2
beta_one=0.9; beta_two=0.999; adam_eps=1e-8; learn_rate=0.01; weight_decay=0.01; step_count=10.0
def adam_update(w,g,m,v,factor):
    s=g*factor
    m2=beta_one*m+(1.0-beta_one)*s
    v2=beta_two*v+(1.0-beta_two)*s*s
    mh=m2/(1.0-beta_one**step_count)
    vh=v2/(1.0-beta_two**step_count)
    w2=w-learn_rate*(mh/(jnp.sqrt(vh)+adam_eps)+weight_decay*w)
    return (w2,m2,v2,w2.astype(bf))
def inner_adam_kernel(f_ref,a0_ref,m0_ref,a1_ref,m1_ref,ada_ref,w_ref,m_ref,v_ref,*outs):
    factor=f_ref[0]; l=pl.program_id(0); j=pl.program_id(1)
    def put(sl,g):
        for o,val in zip(outs,adam_update(w_ref[0,:,sl],g,m_ref[0,:,sl],v_ref[0,:,sl],factor)): o[0,:,sl]=val
    for a in range(2):
        sl=slice(a*CW,(a+1)*CW)
        for layer,refs in enumerate(((a0_ref,m0_ref),(a1_ref,m1_ref))):
            for part,ref in enumerate(refs):
                @pl.when(jnp.logical_and(j//4==part,l==layer))
                def _(): put(sl,ref[0,a])
        @pl.when(j>=8)
        def _(): put(sl,ada_ref[0,:,sl])
def inner_adam(factor,grads,ada,w,m,v):
    own=w.shape[1]; C=w.shape[2]; W=2*CW
    blk=pl.BlockSpec((1,own,W),lambda l,j:(l,0,j))
    def gmap(layer,part):
        def index(l,j):
            jj=jnp.clip(j-4*part,0,3); on=jnp.where(l==layer,jj,3*(l>layer))
            return (part,on,0,0)
        return pl.BlockSpec((1,2,own,CW),index)
    sd=jax.ShapeDtypeStruct
    return pl.pallas_call(inner_adam_kernel,grid=(LAYERS,C//W),
        in_specs=[pl.BlockSpec(memory_space=pltpu.SMEM)]+[gmap(l,p) for l in range(2) for p in range(2)]+[pl.BlockSpec((1,own,W),lambda l,j:(l,0,jnp.maximum(j-8,0))),blk,blk,blk],
        out_specs=[blk]*4,out_shape=[sd(w.shape,f32)]*3+[sd(w.shape,bf)],
        compiler_params=pltpu.CompilerParams(vmem_limit_bytes=VLIM))(factor,*grads,ada,w,m,v)
def outer_adam_kernel(f_ref,g0_ref,g1_ref,b_ref,w_ref,m_ref,v_ref,*outs):
    factor=f_ref[0]; l=pl.program_id(0); j=pl.program_id(1)
    def put(sl,g):
        for o,val in zip(outs,adam_update(w_ref[0,:,sl],g,m_ref[0,:,sl],v_ref[0,:,sl],factor)): o[0,:,sl]=val
    for a in range(2):
        sl=slice(a*CW,(a+1)*CW)
        for layer,ref in enumerate((g0_ref,g1_ref)):
            @pl.when(jnp.logical_and(j<4,l==layer))
            def _(): put(sl,ref[0,a])
    @pl.when(j==4)
    def _(): put(slice(0,128),b_ref[0])
def outer_adam(factor,g0,g1,b,w,m,v):
    own=w.shape[1]; W=2*CW
    blk=pl.BlockSpec((1,own,W),lambda l,j:(l,0,j))
    def gmap(layer):
        def index(l,j):
            jj=jnp.minimum(j,3); on=jnp.where(l==layer,jj,3*(l>layer))
            return (0, on, 0, 0)
        return pl.BlockSpec((1,2,own,CW),index)
    sd=jax.ShapeDtypeStruct
    return pl.pallas_call(outer_adam_kernel,grid=(LAYERS,5),
        in_specs=[pl.BlockSpec(memory_space=pltpu.SMEM),gmap(0),gmap(1),pl.BlockSpec((1,own,128),lambda l,j:(l,0,0)),blk,blk,blk],
        out_specs=[blk]*4,out_shape=[sd(w.shape,f32)]*3+[sd(w.shape,bf)],
        compiler_params=pltpu.CompilerParams(vmem_limit_bytes=VLIM))(factor,g0,g1,b,w,m,v)
P_SIZE=16; GRID=16; LAYERS=2; LAT_DEV=4; FREQ=256; NCLASS=1000
clip_coef=2.5
BIAS=14
def position_table(grid_side, feature_width):
    quarter=feature_width//4
    omega=jnp.exp(-math.log(10000.0)*jnp.arange(quarter,dtype=f32)/quarter)
    ids=jnp.arange(grid_side*grid_side,dtype=jnp.int32)
    a=(ids%grid_side).astype(f32)[:,None]*omega[None,:]
    d=(ids//grid_side).astype(f32)[:,None]*omega[None,:]
    return jnp.concatenate([jnp.sin(a),jnp.cos(a),jnp.sin(d),jnp.cos(d)],axis=1)
def time_features(steps, count):
    half=count//2
    freq=jnp.exp(-math.log(10000.0)*jnp.arange(half,dtype=f32)/half)
    ang=steps.astype(f32)[:,None]*freq[None,:]
    return jnp.concatenate([jnp.cos(ang),jnp.sin(ang)],axis=1)
def dot32(pattern,a,b): return jnp.einsum(pattern,a,b,preferred_element_type=f32)
ALL=("rep","shard")

def per_device(latents,target_noise,labels,time_steps,inner_weights,outer_weights,embed_table,final_mod,head_weights,
               inner_moment,inner_square,outer_moment,outer_square,embed_moment,embed_square,final_moment,final_square,head_moment,head_square):
    R=lax.axis_size("rep"); S=lax.axis_size("shard")
    rep=lax.axis_index("rep"); shard=lax.axis_index("shard")
    own=D//S; W=4*D//R; N=LAT_DEV*R*S; G=LAT_DEV*S
    count=N*TOK*P_SIZE
    inner_low=inner_weights.astype(bf)
    outer_turn=lambda a: a.transpose(0,2,1)
    outer_low=outer_turn(outer_weights).astype(bf)
    def slab(l):
        s=jnp.stack([inner_low[l,:,:4*D],inner_low[l,:,4*D:8*D],outer_low[l,:,:FF]])
        return s.reshape(3,own,R,W).transpose(0,2,1,3)
    embed_low=embed_table.T.astype(bf); final_low=final_mod.astype(bf); head_low=head_weights.astype(bf)
    r1=P_SIZE+1; r2=P_SIZE+2+FREQ; r3=P_SIZE+3+FREQ+D
    fin_cols=2*D//S
    small=jnp.concatenate([outer_low[0,:,FF:],outer_low[1,:,FF:],embed_low[:,:P_SIZE+1]],axis=1).T
    small=jnp.pad(small,((0,48-small.shape[0]),(0,0)))
    mine_rows=jnp.concatenate([time_features(time_steps,FREQ).astype(bf).astype(f32),labels.astype(f32)[:,None],jnp.zeros((LAT_DEV,127),f32)],axis=1)
    mine_rows=jnp.concatenate([mine_rows,mine_rows],axis=0)
    second_w=embed_low[:,r2:r2+D]
    table=jnp.pad(embed_low[:,r3:],((0,0),(0,1024-NCLASS)))
    biases2=jnp.pad(jnp.stack([embed_low[:,r1+FREQ],embed_low[:,r2+D]]).astype(f32),((0,6),(0,0)))
    ada_own=inner_low[:,:,4*D+FF:]
    fin_bias=jnp.pad(final_low[D:].astype(f32),((0,7),(0,0)))
    first=first_call(slab(0),mine_rows,small,embed_low[:,r1:r1+FREQ],second_w.reshape(own,S,own).transpose(1,0,2),table,biases2,ada_own,final_low[:D].reshape(S,own,fin_cols),fin_bias,R,S,0)
    gather0,rows_all,small,hidden,time_act,condition,cond_all,modul,fin_mod=first
    def latent_order(a):
        a=a.reshape(a.shape[:-2]+(S,R,8,a.shape[-1]))[...,:LAT_DEV,:]
        return jnp.swapaxes(a,-4,-3).reshape(a.shape[:-4]+(N,a.shape[-1]))
    rows_all=latent_order(rows_all.reshape(S*R*8,384))
    features=rows_all[:,:FREQ].astype(bf)
    label_col=rows_all[:,FREQ:FREQ+1]
    before=latent_order(jnp.stack([hidden,condition])).transpose(0,2,1)
    wide=latent_order(jnp.stack([time_act,cond_all])).transpose(0,2,1,3).reshape(2,N,D)
    time_act=wide[0]; cond_all=wide[1]
    cond_own=lax.dynamic_slice_in_dim(cond_all,shard*own,own,1).T
    small=small.transpose(1,0,2).reshape(48,D)
    biases=small[:LAYERS*BIAS].reshape(LAYERS,BIAS,D).astype(f32)
    patch_w=small[LAYERS*BIAS:LAYERS*BIAS+P_SIZE]; patch_b=small[LAYERS*BIAS+P_SIZE].astype(f32)
    modul=modul.reshape(LAYERS,LAT_DEV,6,D)+biases[:,None,7:13]
    modul=jnp.pad(modul,((0,0),(0,0),(0,2),(0,0)))
    fin_mod=fin_mod[:,:LAT_DEV].transpose(1,0,2).reshape(LAT_DEV,2,D)
    ramp=0.0001+(0.02-0.0001)*jnp.arange(1000,dtype=f32)/999.0
    upto=jnp.arange(1000,dtype=jnp.int32)[None,:]<=time_steps[:,None]
    abar=jnp.exp(jnp.sum(jnp.where(upto,jnp.log(1.0-ramp)[None,:],0.0),axis=1))
    patches=(jnp.sqrt(abar)[:,None,None]*latents+jnp.sqrt(1.0-abar)[:,None,None]*target_noise).astype(bf)
    stream=dot32("gpt,pd->gtd",patches,patch_w)+patch_b+position_table(GRID,D)[None]
    stream=stream.reshape(LAT_DEV*TOK,D)
    saved=[]
    gathered=[unit_blocks(gather0,R)]
    for l in range(LAYERS):
        full_w=gathered[l]
        bias=jnp.pad(biases[l],((0,2),(0,0)))
        if l==0:
            o,gather1=layer_fwd_gather(stream,modul[l],bias,full_w,slab(1),R,S,1)
            gathered.append(unit_blocks(gather1,R))
        else: o=layer_fwd(stream,modul[l],bias,full_w)
        saved.append((stream,)+tuple(o))
        stream=o[-1]
    grad_stream,grad_fin,head_rows=head(stream,fin_mod,head_low[:D],head_low[D:].astype(f32),target_noise,1.0/count)
    def mlp_parts(l,g):
        x,normed,qkv,lse,mixed,attn,mid,ntwo,upper,activ,down,_=saved[l]
        return bwd_mlp_parts(g,modul[l],gathered[l],down,upper,mid,attn)
    def attn_parts(l,gmix,alow,gmid):
        x,normed,qkv,lse,mixed,attn,mid,ntwo,upper,activ,down,_=saved[l]
        return bwd_attn_parts(gmix,alow,gmid,modul[l],gathered[l],qkv,lse,x)
    mod_grad=lambda dm1,dm2: jnp.concatenate([dm2[:,:2],dm1[:,2:6]],axis=1).astype(bf).reshape(LAT_DEV,6*D)
    def mlp_sums(l,dlow,ulow): return (dlow,saved[l][7]),(saved[l][9],ulow)
    def attn_sums(l,low): return (saved[l][1],saved[l][4]),(low,)
    dlow,ulow,gmid,alow,gmix,dm1_1,db1_1=plain(*mlp_parts(1,grad_stream))
    (low,grad_stream,dm2_1,db2_1),held,_,_=carry(R,S,2,*mlp_sums(1,dlow,ulow),MLP_X,(),*attn_parts(1,gmix,alow,gmid))
    late=jnp.concatenate([mod_grad(dm1_1,dm2_1),grad_fin.astype(bf).reshape(LAT_DEV,2*D)],axis=1)
    (dlow,ulow,gmid,alow,gmix,dm1_0,db1_0),held,(mlp1,sq_a),(late,)=carry(R,S,3,*attn_sums(1,low),ATTN_X,(held,),*mlp_parts(0,grad_stream),
        extra=rows_extra(late.reshape(16,8*D*LAT_DEV//16),R,S))
    (low,grad_stream,dm2_0,db2_0),held,(attn1,sq_b),_=carry(R,S,4,*mlp_sums(0,dlow,ulow),MLP_X,(held,),*attn_parts(0,gmix,alow,gmid))
    late=late.reshape(N,8*D)
    fin_mine=lax.dynamic_slice_in_dim(late,6*D+shard*fin_cols,fin_cols,1)
    gs=grad_stream.reshape(LAT_DEV,TOK,D)
    patch_grad=dot32("gpt,gtd->pd",patches,gs.astype(bf))
    patch_bias=jnp.sum(grad_stream,axis=0)[None]
    o1=LAYERS*BIAS; o2=o1+P_SIZE+1
    cond_back=lambda squares: cond_extra((late,fin_mine,cond_own,cond_all,time_act,before,label_col,features,ada_own,final_low[:D].reshape(S,own,fin_cols),
        second_w.reshape(own,S,own).transpose(1,0,2),mod_grad(dm1_0,dm2_0).reshape(16,6*D*LAT_DEV//16),
        db1_0,db2_0,dm1_0,dm2_0,db1_1,db2_1,dm1_1,dm2_1,patch_grad,patch_bias,grad_fin,head_rows,squares),R,S)
    squares=sq_a+sq_b
    if N<=256: mlp0,_,attn0,_,*rest=last_call(R,S,5,*attn_sums(0,low),(held,),cond_back(squares))
    else:
        mlp0,sq_c,attn0,sq_d=sums_call(R,S,5,*attn_sums(0,low),(held,))
        rest=last_call(R,S,6,(),(),(),cond_back(squares+sq_c+sq_d))
    ada_grad,final_turn,second,class_grad,first_grad,vectors,mine,head_total,norm_parts=rest
    head_total=head_total.transpose(2,0,1,3).reshape(HEAD_ROWS,D)
    mean_loss=jnp.sum(head_total[HEAD_ROWS-1,:P_SIZE])/count
    head_total=jnp.concatenate([head_total[:P_SIZE],head_total[P_SIZE,:P_SIZE][:,None]],axis=1).T
    embed_grad=jnp.concatenate([mine[o1:o2].T,first_grad,vectors[1,:,:1],second,vectors[0,:,:1],class_grad[:,:NCLASS]],axis=1)
    final_turn=jnp.concatenate([final_turn,mine[o2:o2+fin_cols//own].reshape(fin_cols)[:,None]],axis=1)
    bias_grad=mine[:o1].reshape(LAYERS,BIAS,own)
    grad_norm=jnp.sqrt(jnp.sum(norm_parts))
    factor=jnp.minimum(1.0,clip_coef*math.sqrt(D/count)/grad_norm)
    out=[mean_loss,grad_norm]
    out.extend(inner_adam(factor.reshape(1),(attn0,mlp0,attn1,mlp1),ada_grad,inner_weights,inner_moment,inner_square))
    bias_turn=jnp.pad(bias_grad.transpose(0,2,1),((0,0),(0,0),(0,128-BIAS)))
    out.extend(outer_turn(a) for a in outer_adam(factor.reshape(1),mlp0,mlp1,bias_turn,outer_turn(outer_weights),outer_turn(outer_moment),outer_turn(outer_square)))
    for w,g,m,v in ((embed_table,embed_grad.T,embed_moment,embed_square),(final_mod,final_turn.T,final_moment,final_square),
                    (head_weights,head_total,head_moment,head_square)):
        out.extend(adam_update(w,g,m,v,factor))
    return tuple(out)

def solution(mesh):
    lat=P(ALL,None,None); one=P(ALL); inn=P(None,"shard",None); oute=P(None,None,"shard"); col=P(None,"shard")
    in_specs=(lat,lat,one,one,inn,oute,col,col,P(),inn,inn,oute,oute,col,col,col,col,P(),P())
    out_specs=(P(),P())+(inn,)*4+(oute,)*4+(col,)*8+(P(),)*4
    return jax.shard_map(per_device,mesh=mesh,in_specs=in_specs,out_specs=out_specs,check_vma=False)
```

```python
from jax.sharding import PartitionSpec as P
import functools, math
import jax, jax.numpy as jnp
from jax import lax
from jax.experimental import pallas as pl
from jax.experimental.pallas import tpu as pltpu
D=768; HEADS=12; HDIM=64; FF=3072; TOK=256
norm_eps=1e-6
bf=jnp.bfloat16; f32=jnp.float32
VLIM=60*1024*1024
def mm(a,b): return lax.dot_general(a,b,(((1,),(0,)),((),())),preferred_element_type=f32)
def mm_nt(a,b): return lax.dot_general(a,b,(((1,),(1,)),((),())),preferred_element_type=f32)
def mm_tn(a,b): return lax.dot_general(a,b,(((0,),(0,)),((),())),preferred_element_type=f32)
def ln_parts(x):
    c=x-jnp.mean(x,axis=-1,keepdims=True)
    r=lax.rsqrt(jnp.mean(c*c,axis=-1,keepdims=True)+norm_eps)
    return c*r, r
def ln_back(dy, xhat, r, sc):
    dxh=dy*(1.0+sc)
    m1=jnp.mean(dxh,axis=-1,keepdims=True); m2=jnp.mean(dxh*xhat,axis=-1,keepdims=True)
    return r*(dxh-m1-xhat*m2)
def half_masks():
    lane=lax.broadcasted_iota(jnp.int32,(1,128),1)
    lo=(lane<HDIM)
    return lo
C0=math.sqrt(2.0/math.pi); C1=0.044715

def fwd_kernel(x_ref, mod_ref, bias_ref, wa_ref, w1_ref, w2_ref,
               normed_ref, qkv_ref, lse_ref, mixed_ref, attn_ref, mid_ref, ntwo_ref, upper_ref, activ_ref, down_ref, out_ref, hook=lambda p: None):
    hook(0)
    x=x_ref[...]
    mod=lambda j: mod_ref[0, j:j+1, :]
    bias=lambda j: bias_ref[j:j+1, :]
    xh,_=ln_parts(x)
    normed=(xh*(1.0+mod(1))+mod(0)).astype(bf)
    normed_ref[...]=normed
    qkv_ref[:, :D]=(mm(normed, wa_ref[0,0])+bias(0)).astype(bf)
    qkv_ref[:, D:2*D]=mm(normed, wa_ref[0,1]).astype(bf)
    qkv_ref[:, 2*D:]=(mm(normed, wa_ref[0,2])+bias(1)).astype(bf)
    lo=half_masks()
    for hp in range(HEADS//2):
        hook(1+hp)
        c=hp*128
        q=qkv_ref[:, c:c+128]; k=qkv_ref[:, D+c:D+c+128]; v=qkv_ref[:, 2*D+c:2*D+c+128]
        outs=[]
        for h in range(2):
            keep=lo if h==0 else jnp.logical_not(lo)
            qm=jnp.where(keep, q, jnp.zeros_like(q))
            s=mm_nt(qm,k)*(HDIM**-0.5)
            m=jnp.max(s,axis=-1,keepdims=True)
            e=jnp.exp(s-m)
            l=jnp.sum(e,axis=-1,keepdims=True)
            p=(e*(1.0/l)).astype(bf)
            lse_ref[:, 2*hp+h:2*hp+h+1]=m+jnp.log(l)
            outs.append(mm(p,v))
        mixed_ref[:, c:c+128]=jnp.where(lo, outs[0], outs[1]).astype(bf)
    hook(7)
    attn=mm(mixed_ref[...], wa_ref[0,3])+bias(2)
    attn_ref[...]=attn
    mid=x+mod(2)*attn
    mid_ref[...]=mid
    xh2,_=ln_parts(mid)
    ntwo=(xh2*(1.0+mod(4))+mod(3)).astype(bf)
    ntwo_ref[...]=ntwo
    down=jnp.broadcast_to(bias(13),(TOK,D))
    for j in range(4):
        hook(8+j)
        up=mm(ntwo, w1_ref[0,j])+bias(3+j)
        upper_ref[:, j*D:(j+1)*D]=up
        t=jnp.tanh(C0*(up+C1*(up*up*up)))
        act=(0.5*up*(1.0+t)).astype(bf)
        activ_ref[:, j*D:(j+1)*D]=act
        down=down+mm_nt(act, w2_ref[0,j])
    down_ref[...]=down
    out_ref[...]=mid_ref[...]+mod(5)*down

def full(shape):
    n=len(shape)
    return pl.BlockSpec(shape, lambda i: (0,)*n, pipeline_mode=pl.Buffered(1))
def unit(u,n=4): return pl.BlockSpec((1,n,D,D),lambda i:(u,0,0,0),pipeline_mode=pl.Buffered(1))
def rows(width): return pl.BlockSpec((TOK,width), lambda i:(i,0))
def layer_fwd(x, mod, bias, w):
    T=x.shape[0]; n=T//TOK
    sd=jax.ShapeDtypeStruct
    widths=[(D,bf),(3*D,bf),(128,f32),(D,bf),(D,f32),(D,f32),(D,bf),(FF,f32),(FF,bf),(D,f32),(D,f32)]
    return pl.pallas_call(fwd_kernel, grid=(n,),
        in_specs=[rows(D), pl.BlockSpec((1,8,D),lambda i:(i,0,0)), full((16,D)), unit(0), unit(1), unit(2)],
        out_specs=[rows(w) for w,_ in widths],
        out_shape=[sd((T,w),t) for w,t in widths],
        compiler_params=pltpu.CompilerParams(vmem_limit_bytes=VLIM),
        cost_estimate=pl.CostEstimate(flops=2*T*(9216*D+2*TOK*D), bytes_accessed=60_000_000, transcendentals=T*FF*2),
    )(x,mod,bias,w,w,w)

def bwd_mlp_kernel(g_ref, mod_ref, wa3_ref, w1_ref, w2_ref, down_ref, upper_ref, mid_ref, attn_ref,
                   dlow_ref, ulow_ref, gmid_ref, alow_ref, gmix_ref, dmod_ref, db_ref):
    i=pl.program_id(0)
    mod=lambda j: mod_ref[0, j:j+1, :]
    g=g_ref[...]
    gd=g*mod(5)
    dl=gd.astype(bf)
    dlow_ref[...]=dl
    @pl.when(i==0)
    def _(): db_ref[...]=jnp.zeros_like(db_ref)
    s0=lambda v: jnp.sum(v,axis=0,keepdims=True)
    dmod_ref[0,5:6,:]=s0(g*down_ref[...])
    db_ref[13:14,:]+=s0(gd)
    gn=jnp.zeros((TOK,D),f32)
    for j in range(4):
        ga=mm(dl, w2_ref[0,j])
        up=upper_ref[:, j*D:(j+1)*D]
        u2=up*up
        t=jnp.tanh(C0*(up+C1*(u2*up)))
        gu=ga*(0.5*(1.0+t)+(0.5*C0)*up*(1.0-t*t)*(1.0+(3.0*C1)*u2))
        db_ref[3+j:4+j,:]+=s0(gu)
        ul=gu.astype(bf)
        ulow_ref[:, j*D:(j+1)*D]=ul
        gn=gn+mm_nt(ul, w1_ref[0,j])
    xh,r=ln_parts(mid_ref[...])
    dmod_ref[0,3:4,:]=s0(gn)
    dmod_ref[0,4:5,:]=s0(gn*xh)
    gm=g_ref[...]+ln_back(gn,xh,r,mod(4))
    gmid_ref[...]=gm
    ga=gm*mod(2)
    dmod_ref[0,2:3,:]=s0(gm*attn_ref[...])
    db_ref[2:3,:]+=s0(ga)
    al=ga.astype(bf)
    alow_ref[...]=al
    gmix_ref[...]=mm_nt(al, wa3_ref[0,0]).astype(bf)
def bwd_mlp_parts(g, mod, w, down, upper, mid, attn):
    T=g.shape[0]; n=T//TOK
    sd=jax.ShapeDtypeStruct
    m3=pl.BlockSpec((1,8,D),lambda i:(i,0,0))
    return (bwd_mlp_kernel,(g,mod,w,w,w,down,upper,mid,attn),
        [rows(D), m3, pl.BlockSpec((1,1,D,D),lambda i:(0,3,0,0),pipeline_mode=pl.Buffered(1)), unit(1), unit(2), rows(D), rows(FF), rows(D), rows(D)],
        [sd((T,D),bf),sd((T,FF),bf),sd((T,D),f32),sd((T,D),bf),sd((T,D),bf),sd((n,8,D),f32),sd((16,D),f32)],
        [rows(D),rows(FF),rows(D),rows(D),rows(D),m3,pl.BlockSpec((16,D),lambda i:(0,0))],
        pl.CostEstimate(flops=2*T*D*(2*FF+D), bytes_accessed=50_000_000, transcendentals=T*FF))
def plain(kernel,args,specs,shapes,ospecs,cost):
    return pl.pallas_call(kernel,grid=(args[0].shape[0]//TOK,),in_specs=specs,out_specs=ospecs,out_shape=shapes,
        compiler_params=pltpu.CompilerParams(vmem_limit_bytes=VLIM),cost_estimate=cost)(*args)

def bwd_attn_kernel(gmix_ref, alow_ref, gmid_ref, mod_ref, wa_ref, qkv_ref, lse_ref, x_ref,
                    low_ref, gin_ref, dmod_ref, db_ref):
    i=pl.program_id(0)
    mod=lambda j: mod_ref[0, j:j+1, :]
    @pl.when(i==0)
    def _(): db_ref[...]=jnp.zeros_like(db_ref)
    s0=lambda v: jnp.sum(v,axis=0,keepdims=True)
    low_ref[:, 3*D:]=alow_ref[...]
    lo=half_masks()
    zero=jnp.zeros((TOK,128),bf)
    for hp in range(HEADS//2):
        c=hp*128
        q=qkv_ref[:, c:c+128]; k=qkv_ref[:, D+c:D+c+128]; v=qkv_ref[:, 2*D+c:2*D+c+128]
        gm=gmix_ref[:, c:c+128]
        res=[]
        for h in range(2):
            keep=lo if h==0 else jnp.logical_not(lo)
            qm=jnp.where(keep,q,zero); gmm=jnp.where(keep,gm,zero)
            s=mm_nt(qm,k)*(HDIM**-0.5)
            p=jnp.exp(s-lse_ref[:, 2*hp+h:2*hp+h+1])
            dp=mm_nt(gmm,v)
            ds=p*(dp-jnp.sum(p*dp,axis=-1,keepdims=True))
            dsl=ds.astype(bf)
            res.append((mm(dsl,k), mm_tn(dsl,q), mm_tn(p.astype(bf),gm)))
        for j in range(3):
            o=jnp.where(lo,res[0][j],res[1][j])
            if j<2: o=o*(HDIM**-0.5)
            ol=o.astype(bf)
            low_ref[:, j*D+c:j*D+c+128]=ol
            if j!=1:
                row=0 if j==0 else 1
                db_ref[row:row+1, c:c+128]+=s0(ol.astype(f32))
    gn=mm_nt(low_ref[:, :D], wa_ref[0,0])+mm_nt(low_ref[:, D:2*D], wa_ref[0,1])+mm_nt(low_ref[:, 2*D:3*D], wa_ref[0,2])
    xh,r=ln_parts(x_ref[...])
    dmod_ref[...]=jnp.zeros_like(dmod_ref)
    dmod_ref[0,0:1,:]=s0(gn)
    dmod_ref[0,1:2,:]=s0(gn*xh)
    gin_ref[...]=gmid_ref[...]+ln_back(gn,xh,r,mod(1))
def bwd_attn_parts(gmix, alow, gmid, mod, w, qkv, lse, x):
    T=gmix.shape[0]; n=T//TOK
    sd=jax.ShapeDtypeStruct
    m3=pl.BlockSpec((1,8,D),lambda i:(i,0,0))
    return (bwd_attn_kernel,(gmix,alow,gmid,mod,w,qkv,lse,x),
        [rows(D),rows(D),rows(D),m3,unit(0,3),rows(3*D),rows(128),rows(D)],
        [sd((T,4*D),bf),sd((T,D),f32),sd((n,8,D),f32),sd((8,D),f32)],
        [rows(4*D),rows(D),m3,pl.BlockSpec((8,D),lambda i:(0,0))],
        pl.CostEstimate(flops=2*T*D*(3*D+5*TOK), bytes_accessed=25_000_000, transcendentals=T*TOK*HEADS))
MESH=pl.DeviceIdType.MESH
class Gather:
    def __init__(self,R,nz,U,w_ref,out_ref,zs,zr,xs,xr,cs,cr,ls):
        self.R,self.nz,self.U=R,nz,U
        self.w,self.out=w_ref,out_ref
        self.zs,self.zr,self.xs,self.xr,self.cs,self.cr,self.ls=zs,zr,xs,xr,cs,cr,ls
        self.rep=lax.axis_index("rep"); self.shard=lax.axis_index("shard")
        self.z=self.shard//2; self.c=lax.rem(self.shard,2)
        self.relay=R==4
    def at(self,m,z,other=False): return (jnp.bitwise_xor(self.rep,m), 2*z+(1-self.c if other else self.c))
    def peers(self):
        return [self.at(0,lax.rem(self.z+k,self.nz)) for k in range(1,self.nz)]+[self.at(m,self.z) for m in range(1,self.R)]+[self.at(0,self.z,True)]
    def copy(self,src,dst,s,r,dev): return pltpu.make_async_remote_copy(src_ref=src,dst_ref=dst,send_sem=s,recv_sem=r,device_id=dev,device_id_type=MESH)
    def along(self,u,o,up):
        b=self.out.at[u,self.rep,o,self.c]
        return self.copy(b,b,self.zs.at[u,o,1 if up else 0],self.zr.at[u,o],self.at(0,self.z+(1 if up else -1)))
    def own(self,u,up):
        return self.copy(self.w.at[u,self.rep],self.out.at[u,self.rep,self.z,self.c],self.zs.at[u,self.z,1 if up else 0],self.zr.at[u,self.z],self.at(0,self.z+(1 if up else -1)))
    def across(self,u,o,m,q,to):
        b=self.out.at[u,jnp.bitwise_xor(self.rep,q),o,self.c]
        return self.copy(b,b,self.xs.at[u,m-1,o],self.xr.at[u,m-1,o],self.at(to,self.z))
    def swap(self,u,m):
        b=self.out.at[u,jnp.bitwise_xor(self.rep,m),:,self.c]
        return self.copy(b,b,self.cs.at[u,m],self.cr.at[u,m],self.at(0,self.z,True))
    def local(self,u): return pltpu.make_async_copy(self.w.at[u],self.out.at[u,:,self.z,self.c],self.ls.at[u])
    def start(self):
        for u in range(self.U):
            @pl.when(self.z<self.nz-1)
            def _(): self.own(u,True).start()
            @pl.when(self.z>0)
            def _(): self.own(u,False).start()
        for u in range(self.U): self.local(u).start()
    def sides(self,h):
        z,nz=self.z,self.nz
        return ((z>=h,z-h,True,z<nz-1),(z+h<nz,z+h,False,z>0))
    def arrive(self,h,u):
        for there,o,up,more in self.sides(h):
            @pl.when(there)
            def _():
                self.along(u,o,up).wait_recv()
                @pl.when(more)
                def _(): self.along(u,o,up).start()
                for m in range(1,self.R):
                    if not (self.relay and m==3): self.across(u,o,m,0,m).start()
    def pass_on(self,h,u):
        if not self.relay: return
        for there,o,up,more in self.sides(h):
            for par,(q,to) in enumerate(((1,2),(2,1))):
                @pl.when(jnp.logical_and(there,lax.rem(u+o+self.nz,2)==par))
                def _():
                    self.across(u,o,q,0,q).wait_recv()
                    self.across(u,o,3,q,to).start()
    def swap_own(self,u):
        self.local(u).wait(); self.swap(u,0).start()
    def swap_block(self,u,m):
        for o in range(self.nz):
            seen=self.relay and m<3
            cond=o!=self.z
            if seen: cond=jnp.logical_and(cond,(u+o+self.nz)%2!=m-1)
            if seen and (u+o+self.nz)%2==m-1: continue
            @pl.when(o!=self.z)
            def _(): self.across(u,o,m,0,m).wait_recv()
        self.swap(u,m).start()
    def ticks(self):
        U,nz=self.U,self.nz
        order=[(h,u) for h in range(1,nz) for u in range(U)]
        out=[]
        for i in range(len(order)+U):
            if i<len(order): out.append(functools.partial(self.arrive,*order[i]))
            if i>=U: out.append(functools.partial(self.pass_on,*order[i-U]))
            if i>=len(order): out.append(functools.partial(self.swap_own,i-len(order)))
        for u in range(U):
            for m in range(1,self.R): out.append(functools.partial(self.swap_block,u,m))
        return out
    def finish(self):
        for u in range(self.U):
            for m in range(self.R): self.swap(u,m).wait()
            @pl.when(self.z<self.nz-1)
            def _(): self.own(u,True).wait_send()
            @pl.when(self.z>0)
            def _(): self.own(u,False).wait_send()
            for h in range(1,self.nz):
                for there,o,up,more in self.sides(h):
                    @pl.when(there)
                    def _():
                        @pl.when(more)
                        def _(): self.along(u,o,up).wait_send()
                        for m in range(1,self.R): self.across(u,o,m,0,m).wait_send()
def gather_sems(R,nz,U):
    dma=pltpu.SemaphoreType.DMA
    return [dma((U,nz,2)),dma((U,nz)),dma((U,R-1,nz)),dma((U,R-1,nz)),dma((U,R)),dma((U,R)),dma((U,))]
def unit_blocks(out,R):
    U=out.shape[0]; W=out.shape[-1]
    out=out.reshape(U,R,D,W)
    if R==4: return out
    m=R//4
    return out.reshape(U,4,m,D,W).transpose(0,1,3,2,4).reshape(U,4,D,D)
def meet(peers):
    bar=pltpu.get_barrier_semaphore()
    for p in peers: pl.semaphore_signal(bar,inc=1,device_id=p,device_id_type=MESH)
    pl.semaphore_wait(bar,len(peers))

def first_kernel(R,nz,U,own, w_ref,fo_ref,sm_ref,t1_ref,t2_ref,cls_ref,tb_ref,ada_ref,fin_ref,finb_ref,
                 out_ref,f_ref,sg_ref,hid_ref,act_ref,con_ref,call_ref,mod_ref,fm_ref,
                 cgs,pm,mr,ps,zrv,fps, fs1,fr1,ms,mrs,pz,pzr,vs,vr, sz,szr,sc_,scr, *gsems):
    S=2*nz; N=S*R*4
    ga=Gather(R,nz,U,w_ref,out_ref,*gsems)
    rep=lax.axis_index("rep"); shard=lax.axis_index("shard"); z=shard//2; c=lax.rem(shard,2)
    rpeer=lambda m: (jnp.bitwise_xor(rep,m),shard)
    speer=lambda k: (rep,lax.rem(shard+k,S))
    zpeer=lambda k: (rep,2*lax.rem(z+k,nz)+c)
    mate=(rep,2*z+1-c)
    peers=[rpeer(m) for m in range(1,R)]+[speer(k) for k in range(1,S)]
    def send(src,dst,s,r,dev): return pltpu.make_async_remote_copy(src_ref=src,dst_ref=dst,send_sem=s,recv_sem=r,device_id=dev,device_id_type=MESH)
    def far(n,ref,k): return send(ref.at[z,c],ref.at[z,c],sz.at[n,k-1],szr.at[n,k-1],zpeer(k))
    def near(n,ref): return send(ref.at[:,c],ref.at[:,c],sc_.at[n],scr.at[n],mate)
    def go(n,ref):
        for k in range(1,nz): far(n,ref,k).start()
    def turn(n,ref):
        for k in range(1,nz): far(n,ref,k).wait_recv()
        near(n,ref).start()
    def got(n,ref): near(n,ref).wait_recv()
    small=((0,f_ref),(1,sg_ref),(2,act_ref),(3,call_ref))
    meet(peers)
    f1=lambda m: send(fo_ref,f_ref.at[z,c,rep],fs1.at[m-1],fr1.at[m-1],rpeer(m))
    for m in range(1,R): f1(m).start()
    f_ref[z,c,rep]=fo_ref[...]
    sg_ref[z,c]=sm_ref[...]
    for m in range(1,R): f1(m).wait_recv()
    go(*small[0]); go(*small[1])
    ga.start(); ticks=ga.ticks()
    turn(*small[0]); turn(*small[1])
    got(*small[0])
    feats=jnp.concatenate([f_ref[s//2,s%2,r,:4] for s in range(S) for r in range(R)],axis=0)
    hidden=mm_nt(feats[:,:256].astype(bf),t1_ref[...])+tb_ref[0:1,:]
    hid_ref[...]=hidden
    act_ref[z,c]=(hidden/(1.0+jnp.exp(-hidden))).astype(bf)
    go(*small[2])
    for t in ticks[:U]: t()
    hot=(feats[:,256:257].astype(jnp.int32)==lax.broadcasted_iota(jnp.int32,(1,cls_ref.shape[1]),1))
    con=mm_nt(jnp.where(hot,1.0,0.0).astype(bf),cls_ref[...])
    turn(*small[2]); got(*small[2])
    sec=mm_nt(act_ref[0,0],t2_ref[0])
    for s in range(1,S): sec=sec+mm_nt(act_ref[s//2,s%2],t2_ref[s])
    con=(sec+tb_ref[1:2,:])+con
    con_ref[...]=con
    cond=con/(1.0+jnp.exp(-con))
    call_ref[z,c]=cond.astype(bf)
    go(*small[3])
    cgs[...]=cond.reshape(S,R,4,own)
    cg=jnp.concatenate([v for s in range(S) for v in (cgs[s,rep],)*2],axis=0).astype(bf)
    first=lax.rem(lax.broadcasted_iota(jnp.int32,(S*8,1),0),8)<4
    for b in range(6):
        sl=slice(b*D,(b+1)*D)
        v=jnp.where(first,mm(cg,ada_ref[0,:,sl]),mm(cg,ada_ref[1,:,sl]))
        pm[:,:,:,sl]=v.reshape(nz,2,8,D)
    mc=send(pm.at[:,1-c],mr,ms,mrs,mate)
    mc.start()
    for t in ticks[U:U+2]: t()
    mc.wait_recv()
    ps[...]=pm[:,c]+mr[...]
    zc=lambda k: send(ps.at[lax.rem(z+k,nz)],zrv.at[k-1],pz.at[k-1],pzr.at[k-1],zpeer(k))
    for k in range(1,nz): zc(k).start()
    for t in ticks[U+2:3*U]: t()
    turn(*small[3]); got(*small[3])
    fp=mm(call_ref[0,0],fin_ref[0])
    for s in range(1,S): fp=fp+mm(call_ref[s//2,s%2],fin_ref[s])
    fps[...]=(fp+finb_ref[0:1,:]).reshape(S,R,4,fin_ref.shape[2])
    vc=lambda k: send(fps.at[lax.rem(shard+k,S),rep],fm_ref.at[shard],vs.at[k-1],vr.at[k-1],speer(k))
    for k in range(1,S): vc(k).start()
    fm_ref[shard]=fps[shard,rep]
    for t in ticks[3*U:]: t()
    total=ps[z]
    for k in range(1,nz): zc(k).wait_recv(); total=total+zrv[k-1]
    mod_ref[...]=total
    got(*small[1])
    for k in range(1,S): vc(k).wait_recv(); vc(k).wait_send()
    for m in range(1,R): f1(m).wait_send()
    for n,ref in small:
        near(n,ref).wait_send()
        for k in range(1,nz): far(n,ref,k).wait_send()
    mc.wait_send()
    for k in range(1,nz): zc(k).wait_send()
    ga.finish()

def first_call(w,fo,sm,t1,t2,cls,tb,ada,fin,finb,R,S,cid):
    U,_,own,W=w.shape; nz=S//2; N=S*R*4; FC=fin.shape[2]
    dma=pltpu.SemaphoreType.DMA; V=pltpu.VMEM; sd=jax.ShapeDtypeStruct
    any_=pl.BlockSpec(memory_space=pl.ANY); vm=pl.BlockSpec(memory_space=pltpu.VMEM)
    return pl.pallas_call(functools.partial(first_kernel,R,nz,U,own),
        in_specs=[vm]*10, out_specs=[any_]+[vm]*8,
        out_shape=[sd((U,R,nz,2,own,W),bf),sd((nz,2,R,8,384),f32),sd((nz,2)+sm.shape,bf),sd((N,own),f32),sd((nz,2,N,own),bf),sd((N,own),f32),sd((nz,2,N,own),bf),sd((8,6*D),f32),sd((S,4,FC),f32)],
        scratch_shapes=[V((S,R,4,own),f32),V((nz,2,8,6*D),f32),V((nz,8,6*D),f32),V((nz,8,6*D),f32),V((max(nz-1,1),8,6*D),f32),V((S,R,4,FC),f32),
            dma((R-1,)),dma((R-1,)),dma(()),dma(()),dma((nz-1,)),dma((nz-1,)),dma((S-1,)),dma((S-1,)),dma((4,nz-1)),dma((4,nz-1)),dma((4,)),dma((4,))]+gather_sems(R,nz,U),
        compiler_params=pltpu.CompilerParams(collective_id=cid,has_side_effects=True,vmem_limit_bytes=VLIM),
    )(w,fo,sm,t1,t2,cls,tb,ada,fin,finb)

def fwd_gather_kernel(R,nz,U,x_ref,mod_ref,bias_ref,wa_ref,w1_ref,w2_ref,w_ref,*rest):
    outs=rest[:11]; out_ref=rest[11]; gsems=rest[12:]
    i=pl.program_id(0); last=pl.num_programs(0)-1
    ga=Gather(R,nz,U,w_ref,out_ref,*gsems)
    @pl.when(i==0)
    def _():
        meet(ga.peers()); ga.start()
    ticks=ga.ticks(); used=set()
    def hook(p):
        for step in range(4):
            n=12*step+p-6
            if n>=0 and n%2==0 and n//2<len(ticks):
                used.add(n//2)
                pl.when(i==step)(ticks[n//2])
    fwd_kernel(x_ref,mod_ref,bias_ref,wa_ref,w1_ref,w2_ref,*outs,hook=hook)
    @pl.when(i==last)
    def _():
        for n,t in enumerate(ticks):
            if n not in used: t()
        ga.finish()
FWD_WIDTHS=[(D,bf),(3*D,bf),(128,f32),(D,bf),(D,f32),(D,f32),(D,bf),(FF,f32),(FF,bf),(D,f32),(D,f32)]
def layer_fwd_gather(x,mod,bias,full_w,w,R,S,cid):
    T=x.shape[0]; n=T//TOK; U,_,own,W=w.shape; nz=S//2
    sd=jax.ShapeDtypeStruct
    any_=pl.BlockSpec(memory_space=pl.ANY)
    o=pl.pallas_call(functools.partial(fwd_gather_kernel,R,nz,U),grid=(n,),
        in_specs=[rows(D),pl.BlockSpec((1,8,D),lambda i:(i,0,0)),full((16,D)),unit(0),unit(1),unit(2),pl.BlockSpec(memory_space=pltpu.VMEM)],
        out_specs=[rows(v) for v,_ in FWD_WIDTHS]+[any_],
        out_shape=[sd((T,v),t) for v,t in FWD_WIDTHS]+[sd((U,R,nz,2,own,W),bf)],
        scratch_shapes=gather_sems(R,nz,U),
        compiler_params=pltpu.CompilerParams(collective_id=cid,has_side_effects=True,vmem_limit_bytes=VLIM),
        cost_estimate=pl.CostEstimate(flops=2*T*(9216*D+2*TOK*D),bytes_accessed=60_000_000,transcendentals=T*FF*2),
    )(x,mod,bias,full_w,full_w,full_w,w)
    return o[:11],o[11]
CW=384; NCH=8
def bit_orders(R):
    bits=[1<<i for i in range(R.bit_length()-1)]
    return [bits[g%len(bits):]+bits[:g%len(bits)] if bits else [] for g in range(NCH//R)]
def grad_plan(R):
    orders=bit_orders(R); G=NCH//R; n=len(orders[0])
    def stage(g,m): return next(i for i,b in enumerate(orders[g]) if m&b)
    pos=[]
    for i in range(n+1):
        ms=[[m for m in range(R) if (m==0 and i==n) or (m and stage(g,m)==i)] for g in range(G)]
        if i<n: ms=[sorted(v,key=lambda m,g=g:(-bin(m).count("1"),m)) for g,v in enumerate(ms)]
        for a in range(len(ms[0])):
            for g in range(G): pos.append((g,ms[g][a],i))
    send={}; keep={}; recv={}
    for g,m,i in pos:
        if m: send[g,m]=len(send)
        if i>0 or m==0: keep[g,m]=len(keep)
    for i in range(n):
        for g in range(G):
            for m in range(R):
                if not any(m&b for b in orders[g][:i+1]): recv[g,i,m]=len(recv)
    return orders,n,pos,send,keep,recv

def remote(src,dst,ssem,rsem,dev): return pltpu.make_async_remote_copy(src_ref=src,dst_ref=dst,send_sem=ssem,recv_sem=rsem,device_id=dev,device_id_type=MESH)
def everyone(R,nz):
    rep=lax.axis_index("rep"); shard=lax.axis_index("shard"); z=shard//2; c=lax.rem(shard,2)
    return [(rep,2*z+1-c)]+[(rep,2*lax.rem(z+k,nz)+c) for k in range(1,nz)]+[(jnp.bitwise_xor(rep,m),shard) for m in range(1,R)]
class Sums:
    def __init__(self,R,nz,own,nu,xi,xs,dys,out_ref,scr):
        (self.xin,self.xt,self.dy,self.sbuf,self.obuf,self.rbuf,self.sb,self.rb,self.kf,
         self.xsem,self.dsem,self.csend,self.crecv,self.ssem,self.rsem)=scr
        self.R,self.nz,self.own,self.nu,self.xi,self.xs,self.dys,self.out=R,nz,own,nu,xi,xs,dys,out_ref
        self.orders,self.n,self.pos,self.send,self.keep,self.recv=grad_plan(R)
        self.G=NCH//R
        self.rep=lax.axis_index("rep"); self.shard=lax.axis_index("shard")
        self.z=self.shard//2; self.c=lax.rem(self.shard,2)
        self.mate=(self.rep,2*self.z+1-self.c)
    def xor(self,m): return jnp.bitwise_xor(self.rep,m)
    def rdev(self,m): return (self.xor(m),self.shard)
    def chunk(self,k): return self.pos[k][0]*self.R+self.xor(self.pos[k][1])
    def xcopy(self,i): return pltpu.make_async_copy(self.xs[i],self.xin.at[i],self.xsem.at[i])
    def dstart(self,u,k):
        for i,ref in enumerate(self.dys):
            @pl.when(u==i)
            def _(): pltpu.make_async_copy(ref.at[:,pl.ds(pl.multiple_of(self.chunk(k)*CW,128),CW)],self.dy.at[k%4],self.dsem.at[k%4]).start()
    def dwait(self,k): pltpu.make_async_copy(self.dys[0].at[:,pl.ds(0,CW)],self.dy.at[k%4],self.dsem.at[k%4]).wait()
    def ccopy(self,k): return remote(self.sbuf.at[k%2],self.rbuf.at[k%4],self.csend.at[k%2],self.crecv.at[k%4],self.mate)
    def scopy(self,u,g,m):
        i=next(i for i,b in enumerate(self.orders[g]) if m&b); b=self.orders[g][i]
        a=self.send[g,m]; d=self.recv[g,i,m^b]
        return remote(self.sb.at[u,a],self.rb.at[u,d],self.ssem.at[u,a],self.rsem.at[u,d],self.rdev(b))
    def rwait(self,u,g,i,m):
        d=self.recv[g,i,m]
        remote(self.sb.at[u,0],self.rb.at[u,d],self.ssem.at[u,0],self.rsem.at[u,d],self.rdev(1)).wait_recv()
    def load(self):
        self.xcopy(0).start(); self.xcopy(1).start(); self.dstart(0,0); self.dstart(0,1)
        for i in range(2):
            self.xcopy(i).wait()
            self.xt[i]=self.xin[i].T
    def consume(self,u,k):
        g,m,i=self.pos[k]
        self.ccopy(k).wait_recv()
        total=self.obuf[k%2]+self.rbuf[k%4]
        if i==0 and m:
            self.sb[u,self.send[g,m]]=total.astype(bf)
            self.scopy(u,g,m).start()
        else: self.kf[u,self.keep[g,m]]=total.reshape(self.nz,self.own,CW)
    def products(self,u):
        nz,own=self.nz,self.own
        for k in range(NCH):
            if k+2<NCH: self.dstart(u,k+2)
            else:
                @pl.when(u<self.nu-1)
                def _(): self.dstart(u+1,k+2-NCH)
            self.dwait(k)
            p=mm(self.xt[self.xi(u,self.chunk(k))],self.dy[k%4]).reshape(nz,2,own,CW)
            even=p[:,0].reshape(nz*own,CW); odd=p[:,1].reshape(nz*own,CW)
            if k>=2: self.ccopy(k).wait_send()
            else:
                @pl.when(u>0)
                def _(): self.ccopy(k).wait_send()
            self.sbuf[k%2]=jnp.where(self.c==0,odd,even)
            self.obuf[k%2]=jnp.where(self.c==0,even,odd)
            self.ccopy(k).start()
            if k>0: self.consume(u,k-1)
            else:
                @pl.when(u>0)
                def _(): self.consume(u-1,NCH-1)
    def middle(self,u,i):
        for g,m,j in self.pos:
            if m and j==i:
                v=self.kf[u,self.keep[g,m]].reshape(self.nz*self.own,CW)
                for i2 in range(i):
                    self.rwait(u,g,i2,m); v=v+self.rb[u,self.recv[g,i2,m]].astype(f32)
                self.sb[u,self.send[g,m]]=v.astype(bf)
                self.scopy(u,g,m).start()
    def form(self):
        def one(t,_):
            self.products(t)
            if self.n>1:
                @pl.when(t>=1)
                def _(): self.middle(t-1,1)
            return 0
        lax.fori_loop(0,self.nu,one,0)
        self.consume(self.nu-1,NCH-1)
    def stage(self,i):
        if i<self.n:
            for u in range(self.nu-1 if i==1 else 0,self.nu): self.middle(u,i)
    def hold(self):
        for u in range(self.nu):
            for g in range(self.G):
                v=self.kf[u,self.keep[g,0]]
                for i2 in range(self.n):
                    self.rwait(u,g,i2,0); v=v+self.rb[u,self.recv[g,i2,0]].astype(f32).reshape(self.nz,self.own,CW)
                self.out[u,g]=v
    def finish(self):
        for u in range(self.nu):
            for g in range(self.G):
                for m in range(1,self.R): self.scopy(u,g,m).wait_send()
        self.ccopy(NCH-2).wait_send(); self.ccopy(NCH-1).wait_send()
class Tail:
    def __init__(self,R,nz,own,nu,fin,out_ref,scr):
        (self.zs,self.zr,self.az,self.zss,self.zrs,self.ass,self.ars,self.als)=scr
        self.R,self.nz,self.own,self.nu,self.fin,self.out,self.G=R,nz,own,nu,fin,out_ref,NCH//R
        self.rep=lax.axis_index("rep"); self.shard=lax.axis_index("shard")
        self.z=self.shard//2; self.c=lax.rem(self.shard,2)
    def xor(self,m): return jnp.bitwise_xor(self.rep,m)
    def zdev(self,k): return (self.rep,2*lax.rem(self.z+k,self.nz)+self.c)
    def rdev(self,m): return (self.xor(m),self.shard)
    def each(self): return [(u,g) for u in range(self.nu) for g in range(self.G)]
    def zcopy(self,u,g,k): return remote(self.zs.at[u,g,lax.rem(self.z+k,self.nz)],self.zr.at[u,g,k-1],self.zss.at[u,g,k-1],self.zrs.at[u,g,k-1],self.zdev(k))
    def acopy(self,u,g,m): return remote(self.az.at[u,g],self.out.at[u,g*self.R+self.rep],self.ass.at[u,g,m-1],self.ars.at[u,g,m-1],self.rdev(m))
    def arecv(self,u,g,m): return remote(self.az.at[u,g],self.out.at[u,g*self.R+self.xor(m)],self.ass.at[u,g,m-1],self.ars.at[u,g,m-1],self.rdev(m))
    def alocal(self,u,g): return pltpu.make_async_copy(self.az.at[u,g],self.out.at[u,g*self.R+self.rep],self.als.at[u,g])
    def along(self):
        for u,g in self.each():
            self.zs[u,g]=self.fin[u,g].astype(bf)
            for k in range(1,self.nz): self.zcopy(u,g,k).start()
    def spread(self):
        for u,g in self.each():
            v=self.fin[u,g,self.z]
            for k in range(1,self.nz):
                self.zcopy(u,g,k).wait_recv(); v=v+self.zr[u,g,k-1].astype(f32)
            self.az[u,g]=v
            self.alocal(u,g).start()
            for m in range(1,self.R): self.acopy(u,g,m).start()
    def finish(self):
        for u,g in self.each():
            self.alocal(u,g).wait()
            for m in range(1,self.R): self.arecv(u,g,m).wait_recv(); self.acopy(u,g,m).wait_send()
            for k in range(1,self.nz): self.zcopy(u,g,k).wait_send()
    def squares(self):
        v=jnp.zeros((8,128),f32)
        for u,g in self.each():
            b=self.az[u,g]; b=b*b
            for q in range(CW//128): v=v+jnp.sum(b[:,q*128:(q+1)*128].reshape(self.own//8,8,128),axis=0)
        return v
def sums_scratch(R,nz,own,T,nu):
    orders,n,pos,send,keep,recv=grad_plan(R)
    dma=pltpu.SemaphoreType.DMA; V=pltpu.VMEM
    ns,nk,nr=max(len(send),1),len(keep),max(len(recv),1)
    return [V((2,T,D),bf),V((2,D,T),bf),V((4,T,CW),bf),V((2,D//2,CW),f32),V((2,D//2,CW),f32),V((4,D//2,CW),f32),
            V((nu,ns,D//2,CW),bf),V((nu,nr,D//2,CW),bf),V((nu,nk,nz,own,CW),f32),
            dma((2,)),dma((4,)),dma((2,)),dma((4,)),dma((nu,ns)),dma((nu,nr))]
def tail_scratch(R,nz,own,nu):
    G=NCH//R; dma=pltpu.SemaphoreType.DMA; V=pltpu.VMEM
    return [V((nu,G,nz,own,CW),bf),V((nu,G,nz-1,own,CW),bf),V((nu,G,own,CW),f32),dma((nu,G,nz-1)),dma((nu,G,nz-1)),dma((nu,G,R-1)),dma((nu,G,R-1)),dma((nu,G))]
NSUM=15; NTAIL=8
def remote(src,dst,ssem,rsem,dev): return pltpu.make_async_remote_copy(src_ref=src,dst_ref=dst,send_sem=ssem,recv_sem=rsem,device_id=dev,device_id_type=MESH)
def everyone(R,nz):
    rep=lax.axis_index("rep"); shard=lax.axis_index("shard"); z=shard//2; c=lax.rem(shard,2)
    return [(rep,2*z+1-c)]+[(rep,2*lax.rem(z+k,nz)+c) for k in range(1,nz)]+[(jnp.bitwise_xor(rep,m),shard) for m in range(1,R)]
MLP_X=lambda u,ch: u
ATTN_X=lambda u,ch: ch//6
def carrier_kernel(R,nz,own,nu,xi,nt,compute,ci,co,extra,ei,eo,*refs):
    p=0; parts=[]
    t1=1 if nt else 0
    for cnt in (ci,2+nu,t1,ei,co,1,2*t1,eo,NSUM,NTAIL*t1,len(refs)): parts.append(refs[p:p+cnt]); p+=cnt
    cin,rin,tin,ein,cout,(hold_ref,),tout,eout,scr,tscr,escr=parts
    S_=Sums(R,nz,own,nu,xi,rin[:2],rin[2:],hold_ref,scr)
    T_=Tail(R,nz,own,nt,tin[0],tout[0],tscr) if nt else None
    events=extra(R,nz,ein,eout,escr) if extra else {}
    i=pl.program_id(0); last=pl.num_programs(0)-1
    @pl.when(i==0)
    def _():
        S_.load()
        meet(everyone(R,nz))
        if T_: T_.along()
        for f in events.get(0,[]): f()
        S_.form()
    for q in (1,2,3):
        @pl.when(i==q)
        def _():
            S_.stage(q)
            if T_ and q==2: T_.spread()
            for f in events.get(q,[]): f()
    compute(*cin,*cout)
    @pl.when(i==last)
    def _():
        S_.hold(); S_.finish()
        if T_:
            T_.finish(); tout[1][...]=T_.squares()
        for f in events.get(99,[]): f()
def carry(R,S,cid,xs,dys,xi,tail,compute,cargs,cspecs,coshapes,cospecs,cost,extra=None):
    T=xs[0].shape[0]; nz=S//2; own=D//S; nu=len(dys); G=NCH//R
    any_=pl.BlockSpec(memory_space=pl.ANY); sd=jax.ShapeDtypeStruct
    f,eargs,especs,eshapes,eospecs,escratch=extra or (None,[],[],[],[],[])
    nt=tail[0].shape[0] if tail else 0
    held=(nu,G,nz,own,CW)
    o=pl.pallas_call(functools.partial(carrier_kernel,R,nz,own,nu,xi,nt,compute,len(cargs),len(coshapes),f,len(eargs),len(eshapes)),grid=(T//TOK,),
        in_specs=list(cspecs)+[any_]*(2+nu)+[full(t.shape) for t in tail]+especs,
        out_specs=list(cospecs)+[full(held)]+([any_,full((8,128))] if nt else [])+eospecs,
        out_shape=list(coshapes)+[sd(held,f32)]+([sd((nt,NCH,own,CW),f32),sd((8,128),f32)] if nt else [])+eshapes,
        scratch_shapes=sums_scratch(R,nz,own,T,nu)+(tail_scratch(R,nz,own,nt) if nt else [])+escratch,
        compiler_params=pltpu.CompilerParams(collective_id=cid,has_side_effects=True,vmem_limit_bytes=VLIM),
        cost_estimate=cost)(*cargs,*xs,*dys,*tail,*eargs)
    a=len(coshapes); b=a+1+(2 if nt else 0)
    return o[:a],o[a],o[a+1:b],o[b:]
def last_kernel(R,nz,own,sums,nt,extra,ei,eo,*refs):
    k=1 if sums else 0; p=0; parts=[]
    for cnt in (3*k,k,ei,4*k,eo,NSUM*k,k,NTAIL*k,NTAIL*k,len(refs)): parts.append(refs[p:p+cnt]); p+=cnt
    rin,tin,ein,rout,eout,scr,held,t1scr,t2scr,escr=parts
    if sums:
        S_=Sums(R,nz,own,1,ATTN_X,rin[:2],rin[2:],held[0],scr)
        T1=Tail(R,nz,own,nt,tin[0],rout[0],t1scr); T2=Tail(R,nz,own,1,held[0],rout[2],t2scr)
    def squares():
        return T1.squares()+T2.squares()
    events=extra(R,nz,ein,eout,escr,squares if sums else None)
    run=lambda q: [f() for f in events.get(q,[])]
    if sums: S_.load()
    meet(everyone(R,nz))
    if sums: T1.along()
    run(0)
    if sums: S_.form(); S_.stage(1)
    run(1)
    if sums:
        for i in range(2,S_.n): S_.stage(i)
        T1.spread(); S_.hold(); T2.along()
    run(2)
    run(3)
    if sums: T2.spread()
    run(4)
    if sums:
        S_.finish(); T1.finish(); T2.finish()
        rout[1][...]=T1.squares(); rout[3][...]=T2.squares()
    run(99)
def last_call(R,S,cid,xs,dys,tail,extra):
    nz=S//2; own=D//S; sums=bool(xs); G=NCH//R
    any_=pl.BlockSpec(memory_space=pl.ANY); sd=jax.ShapeDtypeStruct; vm=pl.BlockSpec(memory_space=pltpu.VMEM)
    f,eargs,especs,eshapes,eospecs,escratch=extra
    nt=tail[0].shape[0] if sums else 0
    mine=[]
    if sums: mine=sums_scratch(R,nz,own,xs[0].shape[0],1)+[pltpu.VMEM((1,G,nz,own,CW),f32)]+tail_scratch(R,nz,own,nt)+tail_scratch(R,nz,own,1)
    return pl.pallas_call(functools.partial(last_kernel,R,nz,own,sums,nt,f,len(eargs),len(eshapes)),
        in_specs=[any_]*(len(xs)+len(dys))+[vm]*len(tail)+especs,out_specs=([any_,vm,any_,vm] if sums else [])+eospecs,
        out_shape=([sd((nt,NCH,own,CW),f32),sd((8,128),f32),sd((1,NCH,own,CW),f32),sd((8,128),f32)] if sums else [])+eshapes,
        scratch_shapes=mine+escratch,
        compiler_params=pltpu.CompilerParams(collective_id=cid,has_side_effects=True,vmem_limit_bytes=VLIM))(*xs,*dys,*tail,*eargs)
def sums_call(R,S,cid,xs,dys,tail):
    none=lambda R,nz,ins,outs,scr,squares: {}
    return last_call(R,S,cid,xs,dys,tail,(none,[],[],[],[],[]))

def rows_events(R,nz,ins,outs,scr):
    (w,),(g,)=ins,outs; rs,rr,zs,zr,cs,cr,ls=scr
    rep=lax.axis_index("rep"); shard=lax.axis_index("shard"); z=shard//2; c=lax.rem(shard,2)
    loc=lambda: pltpu.make_async_copy(w,g.at[z,c,rep],ls)
    rc=lambda m: remote(w,g.at[z,c,rep],rs.at[m-1],rr.at[m-1],(jnp.bitwise_xor(rep,m),shard))
    zc=lambda k: remote(g.at[z,c],g.at[z,c],zs.at[k-1],zr.at[k-1],(rep,2*lax.rem(z+k,nz)+c))
    cc=lambda: remote(g.at[:,c],g.at[:,c],cs,cr,(rep,2*z+1-c))
    def a():
        loc().start()
        for m in range(1,R): rc(m).start()
    def b():
        loc().wait()
        for m in range(1,R): rc(m).wait_recv()
        for k in range(1,nz): zc(k).start()
    def d():
        for k in range(1,nz): zc(k).wait_recv()
        cc().start()
    def e():
        cc().wait()
        for m in range(1,R): rc(m).wait_send()
        for k in range(1,nz): zc(k).wait_send()
    return {0:[a],1:[b],2:[d],99:[e]}
def rows_extra(w,R,S):
    nz=S//2; dma=pltpu.SemaphoreType.DMA
    return (rows_events,[w],[full(w.shape)],[jax.ShapeDtypeStruct((nz,2,R)+w.shape,bf)],[pl.BlockSpec(memory_space=pl.ANY)],
        [dma((R-1,)),dma((R-1,)),dma((nz-1,)),dma((nz-1,)),dma(()),dma(()),dma(())])

class ShardSum:
    def __init__(self,nz,x,mr,ps,zr,ms,mrs,zs,zrs):
        self.nz,self.x,self.mr,self.ps,self.zr=nz,x,mr,ps,zr
        self.ms,self.mrs,self.zs,self.zrs=ms,mrs,zs,zrs
        self.rep=lax.axis_index("rep"); shard=lax.axis_index("shard"); self.z=shard//2; self.c=lax.rem(shard,2)
    def mate(self): return remote(self.x.at[:,1-self.c],self.mr,self.ms,self.mrs,(self.rep,2*self.z+1-self.c))
    def far(self,k):
        t=lax.rem(self.z+k,self.nz)
        return remote(self.ps.at[t],self.zr.at[k-1],self.zs.at[k-1],self.zrs.at[k-1],(self.rep,2*t+self.c))
    def one(self): self.mate().start()
    def two(self):
        self.mate().wait_recv()
        self.ps[...]=self.x[:,self.c]+self.mr[...]
        for k in range(1,self.nz): self.far(k).start()
    def three(self):
        v=self.ps[self.z]
        for k in range(1,self.nz): self.far(k).wait_recv(); v=v+self.zr[k-1]
        return v
    def end(self):
        self.mate().wait_send()
        for k in range(1,self.nz): self.far(k).wait_send()
def shard_sum_scratch(nz,shape,own_input):
    V=pltpu.VMEM; dma=pltpu.SemaphoreType.DMA
    return ([V((nz,2)+shape,f32)] if own_input else [])+[V((nz,)+shape,f32),V((nz,)+shape,f32),V((nz-1,)+shape,f32),dma(()),dma(()),dma((nz-1,)),dma((nz-1,))]

def sig_back(v,g):
    t=1.0/(1.0+jnp.exp(-v))
    return g*(t*(1.0+v*(1.0-t)))
def fold(v):
    v=v*v; r,c=v.shape
    if r%8: v=jnp.concatenate([v,jnp.zeros((8-r%8,c),f32)],axis=0)
    v=jnp.sum(v.reshape(-1,8,c),axis=0)
    if c%128: v=jnp.concatenate([v,jnp.zeros((8,128-c%128),f32)],axis=1)
    t=v[:,:128]
    for q in range(1,v.shape[1]//128): t=t+v[:,q*128:(q+1)*128]
    return t
HEAD_ROWS=24; P_SIZE=16; FREQ=256; NCLASS=1000
ROW_SECOND=P_SIZE+2+FREQ; ROW_CLASS=P_SIZE+3+FREQ+D
FIN_ROW=45
def cond_events(R,nz,ins,outs,scr,squares):
    (rows_ref,fin_ref,cond_ref,call_ref,act_ref,pre_ref,lab_ref,feat_ref,ada_ref,finw_ref,t2_ref,w_ref)=ins[:12]
    pieces=ins[12:-1]; sq1_ref=ins[-1]
    adag,fin_t,emb_t,bias_t,head_t,norm_ref=outs
    S=2*nz
    fx,tx,sx,asm=scr[0],scr[8],scr[16],scr[24]
    fs=ShardSum(nz,*scr[0:8]); ts=ShardSum(nz,*scr[8:16]); ss=ShardSum(nz,*scr[16:24])
    g0=scr[25]
    re=rows_events(R,nz,(w_ref,),(g0,),scr[26:33])
    tot,rr,rsem,rrs,gc_s,hs,hr,hcs,hcr,nv,n1,n2,n3,nsem,nrec,headg=scr[33:]
    rep=lax.axis_index("rep"); shard=lax.axis_index("shard"); z=shard//2; c=lax.rem(shard,2)
    nr,own=tot.shape; nb=nr-HEAD_ROWS; FC=fin_ref.shape[1]
    mate=(rep,2*z+1-c); zdev=lambda k: (rep,2*lax.rem(z+k,nz)+c); rdev=lambda m: (jnp.bitwise_xor(rep,m),shard)
    rc=lambda m: remote(tot,rr.at[rep],rsem.at[m-1],rrs.at[m-1],rdev(m))
    hz=lambda k: remote(headg.at[z,c],headg.at[z,c],hs.at[k-1],hr.at[k-1],zdev(k))
    hc=lambda: remote(headg.at[:,c],headg.at[:,c],hcs,hcr,mate)
    M6=6*D
    def gather():
        asm[...]=jnp.zeros(asm.shape,f32)
        for l in range(2):
            db1,db2,dm1,dm2=pieces[4*l:4*l+4]; o=14*l
            asm[o:o+2]=db2[0:2]; asm[o+2:o+7]=db1[2:7]; asm[o+13:o+14]=db1[13:14]
            t1=jnp.sum(dm1[...],axis=0); t2=jnp.sum(dm2[...],axis=0)
            asm[o+7:o+9]=t2[0:2]; asm[o+9:o+13]=t1[2:6]
        pg,pb,gfm,hd=pieces[8:]
        asm[28:44]=pg[...]; asm[44:45]=pb[...]
        asm[FIN_ROW:FIN_ROW+2]=jnp.sum(gfm[...],axis=0)
        asm[nb:]=hd[...]
        for s in range(S):
            sx[s//2,s%2]=asm[:,s*own:(s+1)*own]
            for r in range(FC//own):
                p=s*FC+r*own; row=FIN_ROW+p//D
                sx[s//2,s%2,FIN_ROW+r:FIN_ROW+r+1,:]=asm[row:row+1,p%D:p%D+own]
        ss.one()
        fin=fin_ref[...]
        for s in range(S): fx[s//2,s%2]=mm_nt(finw_ref[s],fin)
        fs.one()
    def layer1():
        gc=jnp.zeros(gc_s.shape,f32)
        for q in range(6):
            o=slice(q*D,(q+1)*D); r=rows_ref[:,o]
            adag[1,:,o]=mm(cond_ref[...],r)
            gc=gc+mm_nt(ada_ref[1,:,o],r)
        gc_s[...]=gc
        f=mm_tn(fin_ref[...],call_ref[...])
        fin_t[:,:D]=f
        nv[...]=fold(f)
        fs.two(); ss.two()
    def total():
        tot[...]=ss.three()
        rr[rep]=tot[...]
        for m in range(1,R): rc(m).start()
    def layer0():
        for f in re[99]: f()
        N=cond_ref.shape[1]; M=4*N; B=M6//4
        g=g0[...].reshape(M,B)
        wide=jnp.zeros((own,M),f32)
        at=lax.broadcasted_iota(jnp.int32,(1,M),1)
        n_of=lax.broadcasted_iota(jnp.int32,(N,1),0)
        for j in range(4):
            o=slice(j*B,(j+1)*B)
            spot=jnp.where(at==4*n_of+j,1.0,0.0).astype(bf)
            adag[0,:,o]=mm(mm(cond_ref[...],spot).astype(bf),g)
            wide=wide+jnp.where(at-4*(at//4)==j,mm_nt(ada_ref[0,:,o],g),0.0)
        pick=jnp.where(lax.broadcasted_iota(jnp.int32,(M,1),0)//4==lax.broadcasted_iota(jnp.int32,(1,N),1),1.0,0.0)
        gc=gc_s[...]+lax.dot_general(wide,pick,(((1,),(0,)),((),())),precision=lax.Precision.HIGHEST,preferred_element_type=f32)
        g=sig_back(pre_ref[1],gc+fs.three())
        low=g.astype(bf)
        for s in range(S): tx[s//2,s%2]=mm_tn(t2_ref[s],low)
        ts.one()
        b=jnp.sum(g,axis=1,keepdims=True)
        second=mm(low,act_ref[...])
        emb_t[:,ROW_SECOND:ROW_SECOND+D]=second; emb_t[:,ROW_SECOND+D:ROW_SECOND+D+1]=b
        hot=jnp.where(lab_ref[...]==lax.broadcasted_iota(jnp.int32,(1,1024),1).astype(f32),1.0,0.0)
        table=lax.dot_general(g,hot,(((1,),(0,)),((),())),precision=lax.Precision.HIGHEST,preferred_element_type=f32)
        emb_t[:,ROW_CLASS:ROW_CLASS+NCLASS]=table[:,:NCLASS]
        nv[...]=nv[...]+fold(second)+fold(table)+fold(column(b))
    def column(b):
        return jnp.where(lax.broadcasted_iota(jnp.int32,(1,128),1)<1,jnp.broadcast_to(b,(b.shape[0],128)),0.0)
    def time_and_sums():
        ts.two()
        for m in range(1,R): rc(m).wait_recv()
        v=rr[0]
        for r in range(1,R): v=v+rr[r]
        headg[z,c]=v[nb:]
        for k in range(1,nz): hz(k).start()
        p=nv[...]+fold(v[:nb])
        for q in range(2): p=p+fold(adag[q])
        for l in range(2): bias_t[l,:,0:14]=v[14*l:14*l+14].T
        emb_t[:,0:P_SIZE+1]=v[28:28+P_SIZE+1].T
        last=v[FIN_ROW:FIN_ROW+FC//own].T
        for r in range(FC//own): fin_t[r*own:(r+1)*own,D:D+1]=last[:,r:r+1]
        g=sig_back(pre_ref[0],ts.three())
        b=jnp.sum(g,axis=1,keepdims=True)
        f=mm(g.astype(bf),feat_ref[...])
        emb_t[:,P_SIZE+1:P_SIZE+1+FREQ]=f; emb_t[:,P_SIZE+1+FREQ:P_SIZE+2+FREQ]=b
        nv[...]=jnp.where(rep==0,p+fold(f)+fold(column(b)),0.0)
        for k in range(1,nz): hz(k).wait_recv()
        hc().start()
    def end():
        hc().wait()
        for k in range(1,nz): hz(k).wait_send()
        for m in range(1,R): rc(m).wait_send()
        fs.end(); ts.end(); ss.end()
        nv[...]=nv[...]+sq1_ref[...]+(squares() if squares else 0.0)
        cp=remote(nv,n1,nsem.at[0],nrec.at[0],mate)
        cp.start(); cp.wait()
        n2[z]=nv[...]+n1[...]
        nz_=lambda k: remote(n2.at[z],n2.at[z],nsem.at[k],nrec.at[k],zdev(k))
        for k in range(1,nz): nz_(k).start()
        for k in range(1,nz): nz_(k).wait()
        v=n2[0]
        for q in range(1,nz): v=v+n2[q]
        n3[rep]=v
        nr_=lambda m: remote(n3.at[rep],n3.at[rep],nsem.at[nz-1+m],nrec.at[nz-1+m],rdev(m))
        for m in range(1,R): nr_(m).start()
        for m in range(1,R): nr_(m).wait()
        v=n3[0]
        for r in range(1,R): v=v+n3[r]
        for s in range(S):
            h=headg[s//2,s%2]
            v=v+fold(h[:HEAD_ROWS-1])
            head_t[:,s*own:(s+1)*own]=h[:P_SIZE]
        head_t[:,D:D+1]=headg[0,0][P_SIZE:P_SIZE+1,:P_SIZE].T
        norm=jnp.sqrt(jnp.sum(jnp.sum(v,axis=1,keepdims=True),axis=0,keepdims=True))
        loss=jnp.sum(headg[0,0][HEAD_ROWS-1:HEAD_ROWS,:P_SIZE],axis=1,keepdims=True)
        norm_ref[0:1,:]=jnp.broadcast_to(norm,(1,128))
        norm_ref[1:2,:]=jnp.broadcast_to(loss,(1,128))
    return {0:re[0]+[gather],1:re[1]+[layer1],2:re[2]+[total],3:[layer0],4:[time_and_sums],99:[end]}
def cond_extra(args,R,S):
    nz=S//2; own=D//S; N=args[2].shape[1]; nr=48+HEAD_ROWS; FC=args[1].shape[1]; w=args[11]
    vm=pl.BlockSpec(memory_space=pltpu.VMEM); sd=jax.ShapeDtypeStruct; dma=pltpu.SemaphoreType.DMA; V=pltpu.VMEM
    shapes=[sd((2,own,6*D),f32),sd((FC,D+128),f32),sd((own,2048),f32),sd((2,own,128),f32),sd((P_SIZE,D+128),f32),sd((8,128),f32)]
    scratch=shard_sum_scratch(nz,(own,N),True)*2+shard_sum_scratch(nz,(nr,own),True)+[V((nr,D),f32),V((nz,2,R)+w.shape,bf)]
    scratch+=[dma((R-1,)),dma((R-1,)),dma((nz-1,)),dma((nz-1,)),dma(()),dma(()),dma(())]
    scratch+=[V((nr,own),f32),V((R,nr,own),f32),dma((R-1,)),dma((R-1,)),V((own,N),f32),
        dma((nz-1,)),dma((nz-1,)),dma(()),dma(()),V((8,128),f32),V((8,128),f32),V((nz,8,128),f32),V((R,8,128),f32),dma((nz+R,)),dma((nz+R,)),V((nz,2,HEAD_ROWS,own),f32)]
    return (cond_events,list(args),[vm]*len(args),shapes,[vm]*len(shapes),scratch)

def head_kernel(inv,x_ref,fm_ref,hw_ref,hb_ref,tn_ref,gx_ref,gfm_ref,hg_ref):
    i=pl.program_id(0)
    x=x_ref[...]
    sh=fm_ref[0,0:1,:]; sc=fm_ref[0,1:2,:]
    xh,r=ln_parts(x)
    nrm=(xh*(1.0+sc)+sh).astype(bf)
    diff=mm(nrm,hw_ref[...])+hb_ref[0:1,:]-tn_ref[0].T
    g=2.0*(diff*inv)
    low=g.astype(bf)
    @pl.when(i==0)
    def _():
        hg_ref[...]=jnp.zeros_like(hg_ref)
    p=low.shape[1]
    hg_ref[:p]+=mm_tn(low,nrm)
    hg_ref[p:p+1,:p]+=jnp.sum(g,axis=0,keepdims=True)
    hg_ref[HEAD_ROWS-1:HEAD_ROWS,:p]+=jnp.sum(diff*diff,axis=0,keepdims=True)
    gn=mm_nt(low,hw_ref[...])
    gfm_ref[0,0:1,:]=jnp.sum(gn,axis=0,keepdims=True)
    gfm_ref[0,1:2,:]=jnp.sum(gn*xh,axis=0,keepdims=True)
    gx_ref[...]=ln_back(gn,xh,r,sc)
def head(x,fm,hw,hb,tn,inv):
    T=x.shape[0]; n=T//TOK; sd=jax.ShapeDtypeStruct; p=hw.shape[1]
    m2=pl.BlockSpec((1,2,D),lambda i:(i,0,0))
    fixed=lambda *s: pl.BlockSpec(s,lambda i:(0,)*len(s))
    return pl.pallas_call(functools.partial(head_kernel,inv),grid=(n,),
        in_specs=[rows(D),m2,fixed(D,p),fixed(1,p),pl.BlockSpec((1,p,TOK),lambda i:(i,0,0))],
        out_specs=[rows(D),m2,fixed(HEAD_ROWS,D)],
        out_shape=[sd((T,D),f32),sd((n,2,D),f32),sd((HEAD_ROWS,D),f32)],
        compiler_params=pltpu.CompilerParams(vmem_limit_bytes=VLIM))(x,fm,hw,hb,tn)
LAYERS=2
NB=4
beta_one=0.9; beta_two=0.999; adam_eps=1e-8; learn_rate=0.01; weight_decay=0.01; step_count=10.0
def adam_update(w,g,m,v,factor):
    s=g*factor
    m2=beta_one*m+(1.0-beta_one)*s
    v2=beta_two*v+(1.0-beta_two)*s*s
    mh=m2*(1.0/(1.0-beta_one**step_count))
    vh=v2*(1.0/(1.0-beta_two**step_count))
    w2=w-learn_rate*(mh/(jnp.sqrt(vh)+adam_eps)+weight_decay*w)
    return (w2,m2,v2,w2.astype(bf))
def inner_adam_kernel(f_ref,a0_ref,m0_ref,a1_ref,m1_ref,ada_ref,w_ref,m_ref,v_ref,*outs):
    factor=f_ref[0]; l=pl.program_id(0); j=pl.program_id(1)
    def put(sl,g):
        for o,val in zip(outs,adam_update(w_ref[0,:,sl],g,m_ref[0,:,sl],v_ref[0,:,sl],factor)): o[0,:,sl]=val
    for a in range(NB):
        sl=slice(a*CW,(a+1)*CW)
        for layer,refs in enumerate(((a0_ref,m0_ref),(a1_ref,m1_ref))):
            for part,ref in enumerate(refs):
                @pl.when(jnp.logical_and(j//(NCH//NB)==part,l==layer))
                def _(): put(sl,ref[0,a])
        @pl.when(j>=2*NCH//NB)
        def _(): put(sl,ada_ref[0,:,sl])
def inner_adam(factor,grads,ada,w,m,v):
    own=w.shape[1]; C=w.shape[2]; W=NB*CW
    blk=pl.BlockSpec((1,own,W),lambda l,j:(l,0,j))
    def gmap(layer,part):
        def index(l,j):
            jj=jnp.clip(j-(NCH//NB)*part,0,NCH//NB-1); on=jnp.where(l==layer,jj,(NCH//NB-1)*(l>layer))
            return (part,on,0,0)
        return pl.BlockSpec((1,NB,own,CW),index)
    sd=jax.ShapeDtypeStruct
    return pl.pallas_call(inner_adam_kernel,grid=(LAYERS,C//W),
        in_specs=[pl.BlockSpec(memory_space=pltpu.SMEM)]+[gmap(l,p) for l in range(2) for p in range(2)]+[pl.BlockSpec((1,own,W),lambda l,j:(l,0,jnp.maximum(j-2*NCH//NB,0))),blk,blk,blk],
        out_specs=[blk]*4,out_shape=[sd(w.shape,f32)]*3+[sd(w.shape,bf)],
        compiler_params=pltpu.CompilerParams(vmem_limit_bytes=VLIM))(factor,*grads,ada,w,m,v)
def outer_adam_kernel(f_ref,g0_ref,g1_ref,b_ref,w_ref,m_ref,v_ref,*outs):
    factor=f_ref[0]; l=pl.program_id(0); j=pl.program_id(1)
    def put(sl,g):
        for o,val in zip(outs,adam_update(w_ref[0,:,sl],g,m_ref[0,:,sl],v_ref[0,:,sl],factor)): o[0,:,sl]=val
    for a in range(NB):
        sl=slice(a*CW,(a+1)*CW)
        for layer,ref in enumerate((g0_ref,g1_ref)):
            @pl.when(jnp.logical_and(j<NCH//NB,l==layer))
            def _(): put(sl,ref[0,a])
    @pl.when(j==NCH//NB)
    def _(): put(slice(0,128),b_ref[0])
def outer_adam(factor,g0,g1,b,w,m,v):
    own=w.shape[1]; W=NB*CW
    blk=pl.BlockSpec((1,own,W),lambda l,j:(l,0,j))
    def gmap(layer):
        def index(l,j):
            jj=jnp.minimum(j,NCH//NB-1); on=jnp.where(l==layer,jj,(NCH//NB-1)*(l>layer))
            return (0, on, 0, 0)
        return pl.BlockSpec((1,NB,own,CW),index)
    sd=jax.ShapeDtypeStruct
    return pl.pallas_call(outer_adam_kernel,grid=(LAYERS,NCH//NB+1),
        in_specs=[pl.BlockSpec(memory_space=pltpu.SMEM),gmap(0),gmap(1),pl.BlockSpec((1,own,128),lambda l,j:(l,0,0)),blk,blk,blk],
        out_specs=[blk]*4,out_shape=[sd(w.shape,f32)]*3+[sd(w.shape,bf)],
        compiler_params=pltpu.CompilerParams(vmem_limit_bytes=VLIM))(factor,g0,g1,b,w,m,v)
GRID=16; LAT_DEV=4
clip_coef=2.5
BIAS=14
def position_table(grid_side, feature_width):
    quarter=feature_width//4
    omega=jnp.exp(-math.log(10000.0)*jnp.arange(quarter,dtype=f32)/quarter)
    ids=jnp.arange(grid_side*grid_side,dtype=jnp.int32)
    a=(ids%grid_side).astype(f32)[:,None]*omega[None,:]
    d=(ids//grid_side).astype(f32)[:,None]*omega[None,:]
    return jnp.concatenate([jnp.sin(a),jnp.cos(a),jnp.sin(d),jnp.cos(d)],axis=1)
def time_features(steps, count):
    half=count//2
    freq=jnp.exp(-math.log(10000.0)*jnp.arange(half,dtype=f32)/half)
    ang=steps.astype(f32)[:,None]*freq[None,:]
    return jnp.concatenate([jnp.cos(ang),jnp.sin(ang)],axis=1)
def dot32(pattern,a,b): return jnp.einsum(pattern,a,b,preferred_element_type=f32)
ALL=("rep","shard")

def per_device(latents,target_noise,labels,time_steps,inner_weights,outer_weights,embed_table,final_mod,head_weights,
               inner_moment,inner_square,outer_moment,outer_square,embed_moment,embed_square,final_moment,final_square,head_moment,head_square):
    R=lax.axis_size("rep"); S=lax.axis_size("shard")
    rep=lax.axis_index("rep"); shard=lax.axis_index("shard")
    own=D//S; W=4*D//R; N=LAT_DEV*R*S; G=LAT_DEV*S
    count=N*TOK*P_SIZE
    inner_low=inner_weights.astype(bf)
    outer_turn=lambda a: a.transpose(0,2,1)
    outer_low=outer_turn(outer_weights).astype(bf)
    def slab(l):
        s=jnp.stack([inner_low[l,:,:4*D],inner_low[l,:,4*D:8*D],outer_low[l,:,:FF]])
        return s.reshape(3,own,R,W).transpose(0,2,1,3)
    embed_low=embed_table.T.astype(bf); final_low=final_mod.astype(bf); head_low=head_weights.astype(bf)
    r1=P_SIZE+1; r2=P_SIZE+2+FREQ; r3=P_SIZE+3+FREQ+D
    fin_cols=2*D//S
    small=jnp.concatenate([outer_low[0,:,FF:],outer_low[1,:,FF:],embed_low[:,:P_SIZE+1]],axis=1).T
    small=jnp.pad(small,((0,48-small.shape[0]),(0,0)))
    mine_rows=jnp.concatenate([time_features(time_steps,FREQ).astype(bf).astype(f32),labels.astype(f32)[:,None],jnp.zeros((LAT_DEV,127),f32)],axis=1)
    mine_rows=jnp.concatenate([mine_rows,mine_rows],axis=0)
    second_w=embed_low[:,r2:r2+D]
    table=jnp.pad(embed_low[:,r3:],((0,0),(0,1024-NCLASS)))
    biases2=jnp.pad(jnp.stack([embed_low[:,r1+FREQ],embed_low[:,r2+D]]).astype(f32),((0,6),(0,0)))
    ada_own=inner_low[:,:,4*D+FF:]
    fin_bias=jnp.pad(final_low[D:].astype(f32),((0,7),(0,0)))
    first=first_call(slab(0),mine_rows,small,embed_low[:,r1:r1+FREQ],second_w.reshape(own,S,own).transpose(1,0,2),table,biases2,ada_own,final_low[:D].reshape(S,own,fin_cols),fin_bias,R,S,0)
    gather0,rows_all,small,hidden,time_act,condition,cond_all,modul,fin_mod=first
    rows_all=rows_all.reshape(S*R,8,384)[:,:LAT_DEV].reshape(N,384)
    features=rows_all[:,:FREQ].astype(bf)
    label_col=rows_all[:,FREQ:FREQ+1]
    before=jnp.stack([hidden,condition]).transpose(0,2,1)
    cond_own=lax.dynamic_index_in_dim(cond_all.reshape(S,N,own),shard,0,False).T
    time_act=time_act.reshape(S,N,own).transpose(1,0,2).reshape(N,D)
    cond_all=cond_all.reshape(S,N,own).transpose(1,0,2).reshape(N,D)
    small=small.reshape(S,48,own)
    small=small.transpose(1,0,2).reshape(48,D)
    biases=small[:LAYERS*BIAS].reshape(LAYERS,BIAS,D).astype(f32)
    patch_w=small[LAYERS*BIAS:LAYERS*BIAS+P_SIZE]; patch_b=small[LAYERS*BIAS+P_SIZE].astype(f32)
    modul=modul.reshape(LAYERS,LAT_DEV,6,D)+biases[:,None,7:13]
    modul=jnp.pad(modul,((0,0),(0,0),(0,2),(0,0)))
    fin_mod=fin_mod.transpose(1,0,2).reshape(LAT_DEV,2,D)
    ramp=0.0001+(0.02-0.0001)*jnp.arange(1000,dtype=f32)/999.0
    upto=jnp.arange(1000,dtype=jnp.int32)[None,:]<=time_steps[:,None]
    abar=jnp.exp(jnp.sum(jnp.where(upto,jnp.log(1.0-ramp)[None,:],0.0),axis=1))
    patches=(jnp.sqrt(abar)[:,None,None]*latents+jnp.sqrt(1.0-abar)[:,None,None]*target_noise).astype(bf)
    stream=dot32("gpt,pd->gtd",patches,patch_w)+patch_b+position_table(GRID,D)[None]
    stream=stream.reshape(LAT_DEV*TOK,D)
    saved=[]
    gathered=[unit_blocks(gather0,R)]
    for l in range(LAYERS):
        full_w=gathered[l]
        bias=jnp.pad(biases[l],((0,2),(0,0)))
        if l==0:
            o,gather1=layer_fwd_gather(stream,modul[l],bias,full_w,slab(1),R,S,1)
            gathered.append(unit_blocks(gather1,R))
        else: o=layer_fwd(stream,modul[l],bias,full_w)
        saved.append((stream,)+tuple(o))
        stream=o[-1]
    grad_stream,grad_fin,head_rows=head(stream,fin_mod,head_low[:D],head_low[D:].astype(f32),target_noise,1.0/count)
    def mlp_parts(l,g):
        x,normed,qkv,lse,mixed,attn,mid,ntwo,upper,activ,down,_=saved[l]
        return bwd_mlp_parts(g,modul[l],gathered[l],down,upper,mid,attn)
    def attn_parts(l,gmix,alow,gmid):
        x,normed,qkv,lse,mixed,attn,mid,ntwo,upper,activ,down,_=saved[l]
        return bwd_attn_parts(gmix,alow,gmid,modul[l],gathered[l],qkv,lse,x)
    mod_grad=lambda dm1,dm2: jnp.concatenate([dm2[:,:2],dm1[:,2:6]],axis=1).astype(bf).reshape(LAT_DEV,6*D)
    def mlp_sums(l,dlow,ulow): return (dlow,saved[l][7]),(saved[l][9],ulow)
    def attn_sums(l,low): return (saved[l][1],saved[l][4]),(low,)
    dlow,ulow,gmid,alow,gmix,dm1_1,db1_1=plain(*mlp_parts(1,grad_stream))
    (low,grad_stream,dm2_1,db2_1),held,_,_=carry(R,S,2,*mlp_sums(1,dlow,ulow),MLP_X,(),*attn_parts(1,gmix,alow,gmid))
    late=jnp.concatenate([mod_grad(dm1_1,dm2_1),grad_fin.astype(bf).reshape(LAT_DEV,2*D)],axis=1)
    (dlow,ulow,gmid,alow,gmix,dm1_0,db1_0),held,(mlp1,sq_a),(late,)=carry(R,S,3,*attn_sums(1,low),ATTN_X,(held,),*mlp_parts(0,grad_stream),
        extra=rows_extra(late.reshape(16,8*D*LAT_DEV//16),R,S))
    (low,grad_stream,dm2_0,db2_0),held,(attn1,sq_b),_=carry(R,S,4,*mlp_sums(0,dlow,ulow),MLP_X,(held,),*attn_parts(0,gmix,alow,gmid))
    late=late.reshape(N,8*D)
    fin_mine=lax.dynamic_slice_in_dim(late,6*D+shard*fin_cols,fin_cols,1)
    gs=grad_stream.reshape(LAT_DEV,TOK,D)
    patch_grad=dot32("gpt,gtd->pd",patches,gs.astype(bf))
    patch_bias=jnp.sum(grad_stream,axis=0)[None]
    cond_back=lambda squares: cond_extra((late,fin_mine,cond_own,cond_all,time_act,before,label_col,features,ada_own,final_low[:D].reshape(S,own,fin_cols),
        second_w.reshape(own,S,own).transpose(1,0,2),mod_grad(dm1_0,dm2_0).reshape(16,6*D*LAT_DEV//16),
        db1_0,db2_0,dm1_0,dm2_0,db1_1,db2_1,dm1_1,dm2_1,patch_grad,patch_bias,grad_fin,head_rows,squares),R,S)
    squares=sq_a+sq_b
    if N<=256: mlp0,_,attn0,_,*rest=last_call(R,S,5,*attn_sums(0,low),(held,),cond_back(squares))
    else:
        mlp0,sq_c,attn0,sq_d=sums_call(R,S,5,*attn_sums(0,low),(held,))
        rest=last_call(R,S,6,(),(),(),cond_back(squares+sq_c+sq_d))
    ada_grad,final_turn,embed_grad,bias_turn,head_total,numbers=rest
    embed_grad=embed_grad[:,:embed_table.shape[0]]; final_turn=final_turn[:,:D+1]; head_total=head_total[:,:D+1].T
    grad_norm=numbers[0,0]; mean_loss=numbers[1,0]/count
    factor=jnp.minimum(1.0,clip_coef*math.sqrt(D/count)/grad_norm)
    out=[mean_loss,grad_norm]
    out.extend(inner_adam(factor.reshape(1),(attn0,mlp0,attn1,mlp1),ada_grad,inner_weights,inner_moment,inner_square))
    out.extend(outer_turn(a) for a in outer_adam(factor.reshape(1),mlp0,mlp1,bias_turn,outer_turn(outer_weights),outer_turn(outer_moment),outer_turn(outer_square)))
    for w,g,m,v in ((embed_table,embed_grad.T,embed_moment,embed_square),(final_mod,final_turn.T,final_moment,final_square),
                    (head_weights,head_total,head_moment,head_square)):
        out.extend(adam_update(w,g,m,v,factor))
    return tuple(out)

def solution(mesh):
    lat=P(ALL,None,None); one=P(ALL); inn=P(None,"shard",None); oute=P(None,None,"shard"); col=P(None,"shard")
    in_specs=(lat,lat,one,one,inn,oute,col,col,P(),inn,inn,oute,oute,col,col,col,col,P(),P())
    out_specs=(P(),P())+(inn,)*4+(oute,)*4+(col,)*8+(P(),)*4
    return jax.shard_map(per_device,mesh=mesh,in_specs=in_specs,out_specs=out_specs,check_vma=False)
```

```python
from jax.sharding import PartitionSpec as P
import functools, math
import jax, jax.numpy as jnp
from jax import lax
from jax.experimental import pallas as pl
from jax.experimental.pallas import tpu as pltpu
D=768; HEADS=12; HDIM=64; FF=3072; TOK=256
norm_eps=1e-6
bf=jnp.bfloat16; f32=jnp.float32
VLIM=60*1024*1024
def mm(a,b): return lax.dot_general(a,b,(((1,),(0,)),((),())),preferred_element_type=f32)
def mm_nt(a,b): return lax.dot_general(a,b,(((1,),(1,)),((),())),preferred_element_type=f32)
def mm_tn(a,b): return lax.dot_general(a,b,(((0,),(0,)),((),())),preferred_element_type=f32)
def ln_parts(x):
    c=x-jnp.mean(x,axis=-1,keepdims=True)
    r=lax.rsqrt(jnp.mean(c*c,axis=-1,keepdims=True)+norm_eps)
    return c*r, r
def ln_back(dy, xhat, r, sc):
    dxh=dy*(1.0+sc)
    m1=jnp.mean(dxh,axis=-1,keepdims=True); m2=jnp.mean(dxh*xhat,axis=-1,keepdims=True)
    return r*(dxh-m1-xhat*m2)
def half_masks():
    lane=lax.broadcasted_iota(jnp.int32,(1,128),1)
    lo=(lane<HDIM)
    return lo
C0=math.sqrt(2.0/math.pi); C1=0.044715

def fwd_kernel(x_ref, mod_ref, bias_ref, wa_ref, w1_ref, w2_ref,
               normed_ref, qkv_ref, lse_ref, mixed_ref, attn_ref, mid_ref, ntwo_ref, upper_ref, activ_ref, down_ref, out_ref, hook=lambda p: None):
    hook(0)
    x=x_ref[...]
    mod=lambda j: mod_ref[0, j:j+1, :]
    bias=lambda j: bias_ref[j:j+1, :]
    xh,_=ln_parts(x)
    normed=(xh*(1.0+mod(1))+mod(0)).astype(bf)
    normed_ref[...]=normed
    qkv_ref[:, :D]=(mm(normed, wa_ref[0,0])+bias(0)).astype(bf)
    qkv_ref[:, D:2*D]=mm(normed, wa_ref[0,1]).astype(bf)
    qkv_ref[:, 2*D:]=(mm(normed, wa_ref[0,2])+bias(1)).astype(bf)
    lo=half_masks()
    for hp in range(HEADS//2):
        hook(1+hp)
        c=hp*128
        q=qkv_ref[:, c:c+128]; k=qkv_ref[:, D+c:D+c+128]; v=qkv_ref[:, 2*D+c:2*D+c+128]
        outs=[]
        for h in range(2):
            keep=lo if h==0 else jnp.logical_not(lo)
            qm=jnp.where(keep, q, jnp.zeros_like(q))
            s=mm_nt(qm,k)*(HDIM**-0.5)
            m=jnp.max(s,axis=-1,keepdims=True)
            e=jnp.exp(s-m)
            l=jnp.sum(e,axis=-1,keepdims=True)
            p=(e*(1.0/l)).astype(bf)
            lse_ref[:, 2*hp+h:2*hp+h+1]=m+jnp.log(l)
            outs.append(mm(p,v))
        mixed_ref[:, c:c+128]=jnp.where(lo, outs[0], outs[1]).astype(bf)
    hook(7)
    attn=mm(mixed_ref[...], wa_ref[0,3])+bias(2)
    attn_ref[...]=attn
    mid=x+mod(2)*attn
    mid_ref[...]=mid
    xh2,_=ln_parts(mid)
    ntwo=(xh2*(1.0+mod(4))+mod(3)).astype(bf)
    ntwo_ref[...]=ntwo
    down=jnp.broadcast_to(bias(13),(TOK,D))
    for j in range(4):
        hook(8+j)
        up=mm(ntwo, w1_ref[0,j])+bias(3+j)
        upper_ref[:, j*D:(j+1)*D]=up
        t=jnp.tanh(C0*(up+C1*(up*up*up)))
        act=(0.5*up*(1.0+t)).astype(bf)
        activ_ref[:, j*D:(j+1)*D]=act
        down=down+mm_nt(act, w2_ref[0,j])
    down_ref[...]=down
    out_ref[...]=mid_ref[...]+mod(5)*down

def full(shape):
    n=len(shape)
    return pl.BlockSpec(shape, lambda i: (0,)*n, pipeline_mode=pl.Buffered(1))
def unit(u,n=4): return pl.BlockSpec((1,n,D,D),lambda i:(u,0,0,0),pipeline_mode=pl.Buffered(1))
def rows(width): return pl.BlockSpec((TOK,width), lambda i:(i,0))
def layer_fwd(x, mod, bias, w):
    T=x.shape[0]; n=T//TOK
    sd=jax.ShapeDtypeStruct
    widths=[(D,bf),(3*D,bf),(128,f32),(D,bf),(D,f32),(D,f32),(D,bf),(FF,f32),(FF,bf),(D,f32),(D,f32)]
    return pl.pallas_call(fwd_kernel, grid=(n,),
        in_specs=[rows(D), pl.BlockSpec((1,8,D),lambda i:(i,0,0)), full((16,D)), unit(0), unit(1), unit(2)],
        out_specs=[rows(w) for w,_ in widths],
        out_shape=[sd((T,w),t) for w,t in widths],
        compiler_params=pltpu.CompilerParams(vmem_limit_bytes=VLIM),
        cost_estimate=pl.CostEstimate(flops=2*T*(9216*D+2*TOK*D), bytes_accessed=60_000_000, transcendentals=T*FF*2),
    )(x,mod,bias,w,w,w)

def bwd_mlp_kernel(g_ref, mod_ref, wa3_ref, w1_ref, w2_ref, down_ref, upper_ref, mid_ref, attn_ref,
                   dlow_ref, ulow_ref, gmid_ref, alow_ref, gmix_ref, dmod_ref, db_ref):
    i=pl.program_id(0)
    mod=lambda j: mod_ref[0, j:j+1, :]
    g=g_ref[...]
    gd=g*mod(5)
    dl=gd.astype(bf)
    dlow_ref[...]=dl
    @pl.when(i==0)
    def _(): db_ref[...]=jnp.zeros_like(db_ref)
    s0=lambda v: jnp.sum(v,axis=0,keepdims=True)
    dmod_ref[0,5:6,:]=s0(g*down_ref[...])
    db_ref[13:14,:]+=s0(gd)
    gn=jnp.zeros((TOK,D),f32)
    for j in range(4):
        ga=mm(dl, w2_ref[0,j])
        up=upper_ref[:, j*D:(j+1)*D]
        u2=up*up
        t=jnp.tanh(C0*(up+C1*(u2*up)))
        gu=ga*(0.5*(1.0+t)+(0.5*C0)*up*(1.0-t*t)*(1.0+(3.0*C1)*u2))
        db_ref[3+j:4+j,:]+=s0(gu)
        ul=gu.astype(bf)
        ulow_ref[:, j*D:(j+1)*D]=ul
        gn=gn+mm_nt(ul, w1_ref[0,j])
    xh,r=ln_parts(mid_ref[...])
    dmod_ref[0,3:4,:]=s0(gn)
    dmod_ref[0,4:5,:]=s0(gn*xh)
    gm=g_ref[...]+ln_back(gn,xh,r,mod(4))
    gmid_ref[...]=gm
    ga=gm*mod(2)
    dmod_ref[0,2:3,:]=s0(gm*attn_ref[...])
    db_ref[2:3,:]+=s0(ga)
    al=ga.astype(bf)
    alow_ref[...]=al
    gmix_ref[...]=mm_nt(al, wa3_ref[0,0]).astype(bf)
def bwd_mlp_parts(g, mod, w, down, upper, mid, attn):
    T=g.shape[0]; n=T//TOK
    sd=jax.ShapeDtypeStruct
    m3=pl.BlockSpec((1,8,D),lambda i:(i,0,0))
    return (bwd_mlp_kernel,(g,mod,w,w,w,down,upper,mid,attn),
        [rows(D), m3, pl.BlockSpec((1,1,D,D),lambda i:(0,3,0,0),pipeline_mode=pl.Buffered(1)), unit(1), unit(2), rows(D), rows(FF), rows(D), rows(D)],
        [sd((T,D),bf),sd((T,FF),bf),sd((T,D),f32),sd((T,D),bf),sd((T,D),bf),sd((n,8,D),f32),sd((16,D),f32)],
        [rows(D),rows(FF),rows(D),rows(D),rows(D),m3,pl.BlockSpec((16,D),lambda i:(0,0))],
        pl.CostEstimate(flops=2*T*D*(2*FF+D), bytes_accessed=50_000_000, transcendentals=T*FF))
def plain(kernel,args,specs,shapes,ospecs,cost):
    return pl.pallas_call(kernel,grid=(args[0].shape[0]//TOK,),in_specs=specs,out_specs=ospecs,out_shape=shapes,
        compiler_params=pltpu.CompilerParams(vmem_limit_bytes=VLIM),cost_estimate=cost)(*args)

def bwd_attn_kernel(gmix_ref, alow_ref, gmid_ref, mod_ref, wa_ref, qkv_ref, lse_ref, x_ref,
                    low_ref, gin_ref, dmod_ref, db_ref):
    i=pl.program_id(0)
    mod=lambda j: mod_ref[0, j:j+1, :]
    @pl.when(i==0)
    def _(): db_ref[...]=jnp.zeros_like(db_ref)
    s0=lambda v: jnp.sum(v,axis=0,keepdims=True)
    low_ref[:, 3*D:]=alow_ref[...]
    lo=half_masks()
    zero=jnp.zeros((TOK,128),bf)
    for hp in range(HEADS//2):
        c=hp*128
        q=qkv_ref[:, c:c+128]; k=qkv_ref[:, D+c:D+c+128]; v=qkv_ref[:, 2*D+c:2*D+c+128]
        gm=gmix_ref[:, c:c+128]
        res=[]
        for h in range(2):
            keep=lo if h==0 else jnp.logical_not(lo)
            qm=jnp.where(keep,q,zero); gmm=jnp.where(keep,gm,zero)
            s=mm_nt(qm,k)*(HDIM**-0.5)
            p=jnp.exp(s-lse_ref[:, 2*hp+h:2*hp+h+1])
            dp=mm_nt(gmm,v)
            ds=p*(dp-jnp.sum(p*dp,axis=-1,keepdims=True))
            dsl=ds.astype(bf)
            res.append((mm(dsl,k), mm_tn(dsl,q), mm_tn(p.astype(bf),gm)))
        for j in range(3):
            o=jnp.where(lo,res[0][j],res[1][j])
            if j<2: o=o*(HDIM**-0.5)
            ol=o.astype(bf)
            low_ref[:, j*D+c:j*D+c+128]=ol
            if j!=1:
                row=0 if j==0 else 1
                db_ref[row:row+1, c:c+128]+=s0(ol.astype(f32))
    gn=mm_nt(low_ref[:, :D], wa_ref[0,0])+mm_nt(low_ref[:, D:2*D], wa_ref[0,1])+mm_nt(low_ref[:, 2*D:3*D], wa_ref[0,2])
    xh,r=ln_parts(x_ref[...])
    dmod_ref[...]=jnp.zeros_like(dmod_ref)
    dmod_ref[0,0:1,:]=s0(gn)
    dmod_ref[0,1:2,:]=s0(gn*xh)
    gin_ref[...]=gmid_ref[...]+ln_back(gn,xh,r,mod(1))
def bwd_attn_parts(gmix, alow, gmid, mod, w, qkv, lse, x):
    T=gmix.shape[0]; n=T//TOK
    sd=jax.ShapeDtypeStruct
    m3=pl.BlockSpec((1,8,D),lambda i:(i,0,0))
    return (bwd_attn_kernel,(gmix,alow,gmid,mod,w,qkv,lse,x),
        [rows(D),rows(D),rows(D),m3,unit(0,3),rows(3*D),rows(128),rows(D)],
        [sd((T,4*D),bf),sd((T,D),f32),sd((n,8,D),f32),sd((8,D),f32)],
        [rows(4*D),rows(D),m3,pl.BlockSpec((8,D),lambda i:(0,0))],
        pl.CostEstimate(flops=2*T*D*(3*D+5*TOK), bytes_accessed=25_000_000, transcendentals=T*TOK*HEADS))
MESH=pl.DeviceIdType.MESH
class Gather:
    def __init__(self,R,nz,U,w_ref,out_ref,zs,zr,xs,xr,cs,cr,ls):
        self.R,self.nz,self.U=R,nz,U
        self.w,self.out=w_ref,out_ref
        self.zs,self.zr,self.xs,self.xr,self.cs,self.cr,self.ls=zs,zr,xs,xr,cs,cr,ls
        self.rep=lax.axis_index("rep"); self.shard=lax.axis_index("shard")
        self.z=self.shard//2; self.c=lax.rem(self.shard,2)
        self.relay=R==4
    def at(self,m,z,other=False): return (jnp.bitwise_xor(self.rep,m), 2*z+(1-self.c if other else self.c))
    def peers(self):
        return [self.at(0,lax.rem(self.z+k,self.nz)) for k in range(1,self.nz)]+[self.at(m,self.z) for m in range(1,self.R)]+[self.at(0,self.z,True)]
    def copy(self,src,dst,s,r,dev): return pltpu.make_async_remote_copy(src_ref=src,dst_ref=dst,send_sem=s,recv_sem=r,device_id=dev,device_id_type=MESH)
    def along(self,u,o,up):
        b=self.out.at[u,self.rep,o,self.c]
        return self.copy(b,b,self.zs.at[u,o,1 if up else 0],self.zr.at[u,o],self.at(0,self.z+(1 if up else -1)))
    def own(self,u,up):
        return self.copy(self.w.at[u,self.rep],self.out.at[u,self.rep,self.z,self.c],self.zs.at[u,self.z,1 if up else 0],self.zr.at[u,self.z],self.at(0,self.z+(1 if up else -1)))
    def across(self,u,o,m,q,to):
        b=self.out.at[u,jnp.bitwise_xor(self.rep,q),o,self.c]
        return self.copy(b,b,self.xs.at[u,m-1,o],self.xr.at[u,m-1,o],self.at(to,self.z))
    def swap(self,u,m):
        b=self.out.at[u,jnp.bitwise_xor(self.rep,m),:,self.c]
        return self.copy(b,b,self.cs.at[u,m],self.cr.at[u,m],self.at(0,self.z,True))
    def local(self,u): return pltpu.make_async_copy(self.w.at[u],self.out.at[u,:,self.z,self.c],self.ls.at[u])
    def start(self):
        for u in range(self.U):
            @pl.when(self.z<self.nz-1)
            def _(): self.own(u,True).start()
            @pl.when(self.z>0)
            def _(): self.own(u,False).start()
        for u in range(self.U): self.local(u).start()
    def sides(self,h):
        z,nz=self.z,self.nz
        return ((z>=h,z-h,True,z<nz-1),(z+h<nz,z+h,False,z>0))
    def arrive(self,h,u):
        for there,o,up,more in self.sides(h):
            @pl.when(there)
            def _():
                self.along(u,o,up).wait_recv()
                @pl.when(more)
                def _(): self.along(u,o,up).start()
                for m in range(1,self.R):
                    if not (self.relay and m==3): self.across(u,o,m,0,m).start()
    def pass_on(self,h,u):
        if not self.relay: return
        for there,o,up,more in self.sides(h):
            for par,(q,to) in enumerate(((1,2),(2,1))):
                @pl.when(jnp.logical_and(there,lax.rem(u+o+self.nz,2)==par))
                def _():
                    self.across(u,o,q,0,q).wait_recv()
                    self.across(u,o,3,q,to).start()
    def swap_own(self,u):
        self.local(u).wait(); self.swap(u,0).start()
    def swap_block(self,u,m):
        for o in range(self.nz):
            seen=self.relay and m<3
            cond=o!=self.z
            if seen: cond=jnp.logical_and(cond,(u+o+self.nz)%2!=m-1)
            if seen and (u+o+self.nz)%2==m-1: continue
            @pl.when(o!=self.z)
            def _(): self.across(u,o,m,0,m).wait_recv()
        self.swap(u,m).start()
    def ticks(self):
        U,nz=self.U,self.nz
        order=[(h,u) for h in range(1,nz) for u in range(U)]
        out=[]
        for i in range(len(order)+U):
            if i<len(order): out.append(functools.partial(self.arrive,*order[i]))
            if i>=U: out.append(functools.partial(self.pass_on,*order[i-U]))
            if i>=len(order): out.append(functools.partial(self.swap_own,i-len(order)))
        for u in range(U):
            for m in range(1,self.R): out.append(functools.partial(self.swap_block,u,m))
        return out
    def finish(self):
        for u in range(self.U):
            for m in range(self.R): self.swap(u,m).wait()
            @pl.when(self.z<self.nz-1)
            def _(): self.own(u,True).wait_send()
            @pl.when(self.z>0)
            def _(): self.own(u,False).wait_send()
            for h in range(1,self.nz):
                for there,o,up,more in self.sides(h):
                    @pl.when(there)
                    def _():
                        @pl.when(more)
                        def _(): self.along(u,o,up).wait_send()
                        for m in range(1,self.R): self.across(u,o,m,0,m).wait_send()
def gather_sems(R,nz,U):
    dma=pltpu.SemaphoreType.DMA
    return [dma((U,nz,2)),dma((U,nz)),dma((U,R-1,nz)),dma((U,R-1,nz)),dma((U,R)),dma((U,R)),dma((U,))]
def unit_blocks(out,R):
    U=out.shape[0]; W=out.shape[-1]
    out=out.reshape(U,R,D,W)
    if R==4: return out
    m=R//4
    return out.reshape(U,4,m,D,W).transpose(0,1,3,2,4).reshape(U,4,D,D)
def meet(peers):
    bar=pltpu.get_barrier_semaphore()
    for p in peers: pl.semaphore_signal(bar,inc=1,device_id=p,device_id_type=MESH)
    pl.semaphore_wait(bar,len(peers))

def first_kernel(R,nz,U,own, w_ref,fo_ref,sm_ref,t1_ref,t2_ref,cls_ref,tb_ref,ada_ref,fin_ref,finb_ref,
                 out_ref,feat_ref,lab_ref,sg_ref,pre_ref,act_ref,cown_ref,call_ref,mod_ref,fm_ref,
                 f_ref,cgs,pm,mr,ps,zrv,fps, fs1,fr1,ms,mrs,pz,pzr,vs,vr, sz,szr,sc_,scr, *gsems):
    S=2*nz; N=S*R*4
    ga=Gather(R,nz,U,w_ref,out_ref,*gsems)
    rep=lax.axis_index("rep"); shard=lax.axis_index("shard"); z=shard//2; c=lax.rem(shard,2)
    rpeer=lambda m: (jnp.bitwise_xor(rep,m),shard)
    speer=lambda k: (rep,lax.rem(shard+k,S))
    zpeer=lambda k: (rep,2*lax.rem(z+k,nz)+c)
    mate=(rep,2*z+1-c)
    peers=[rpeer(m) for m in range(1,R)]+[speer(k) for k in range(1,S)]
    def send(src,dst,s,r,dev): return pltpu.make_async_remote_copy(src_ref=src,dst_ref=dst,send_sem=s,recv_sem=r,device_id=dev,device_id_type=MESH)
    def far(n,ref,k): return send(ref.at[z,c],ref.at[z,c],sz.at[n,k-1],szr.at[n,k-1],zpeer(k))
    def near(n,ref): return send(ref.at[:,c],ref.at[:,c],sc_.at[n],scr.at[n],mate)
    def go(n,ref):
        for k in range(1,nz): far(n,ref,k).start()
    def turn(n,ref):
        for k in range(1,nz): far(n,ref,k).wait_recv()
        near(n,ref).start()
    def got(n,ref): near(n,ref).wait_recv()
    small=((0,f_ref),(1,sg_ref),(2,act_ref),(3,call_ref))
    meet(peers)
    f1=lambda m: send(fo_ref,f_ref.at[z,c,rep],fs1.at[m-1],fr1.at[m-1],rpeer(m))
    for m in range(1,R): f1(m).start()
    f_ref[z,c,rep]=fo_ref[...]
    sg_ref[z,c]=sm_ref[...]
    for m in range(1,R): f1(m).wait_recv()
    go(*small[0]); go(*small[1])
    ga.start(); ticks=ga.ticks()
    turn(*small[0]); turn(*small[1])
    got(*small[0])
    feats=jnp.concatenate([f_ref[s//2,s%2,r,:4] for s in range(S) for r in range(R)],axis=0)
    hidden=mm_nt(feats[:,:256].astype(bf),t1_ref[...])+tb_ref[0:1,:]
    feat_ref[...]=feats[:,:256].astype(bf); lab_ref[...]=feats[:,256:257]
    act_ref[z,c]=(hidden/(1.0+jnp.exp(-hidden))).astype(bf)
    go(*small[2])
    for t in ticks[:U]: t()
    hot=(feats[:,256:257].astype(jnp.int32)==lax.broadcasted_iota(jnp.int32,(1,cls_ref.shape[1]),1))
    con=mm_nt(jnp.where(hot,1.0,0.0).astype(bf),cls_ref[...])
    turn(*small[2]); got(*small[2])
    sec=mm_nt(act_ref[0,0],t2_ref[0])
    for s in range(1,S): sec=sec+mm_nt(act_ref[s//2,s%2],t2_ref[s])
    con=(sec+tb_ref[1:2,:])+con
    cond=con/(1.0+jnp.exp(-con))
    call_ref[z,c]=cond.astype(bf)
    go(*small[3])
    cgs[...]=cond.reshape(S,R,4,own)
    cg=jnp.concatenate([v for s in range(S) for v in (cgs[s,rep],)*2],axis=0).astype(bf)
    first=lax.rem(lax.broadcasted_iota(jnp.int32,(S*8,1),0),8)<4
    for b in range(6):
        sl=slice(b*D,(b+1)*D)
        v=jnp.where(first,mm(cg,ada_ref[0,:,sl]),mm(cg,ada_ref[1,:,sl]))
        pm[:,:,:,sl]=v.reshape(nz,2,8,D)
    mc=send(pm.at[:,1-c],mr,ms,mrs,mate)
    mc.start()
    pre_ref[0]=hidden.T; pre_ref[1]=con.T; cown_ref[...]=cond.T.astype(bf)
    for t in ticks[U:U+2]: t()
    mc.wait_recv()
    ps[...]=pm[:,c]+mr[...]
    zc=lambda k: send(ps.at[lax.rem(z+k,nz)],zrv.at[k-1],pz.at[k-1],pzr.at[k-1],zpeer(k))
    for k in range(1,nz): zc(k).start()
    for t in ticks[U+2:3*U]: t()
    turn(*small[3]); got(*small[3])
    fp=mm(call_ref[0,0],fin_ref[0])
    for s in range(1,S): fp=fp+mm(call_ref[s//2,s%2],fin_ref[s])
    fps[...]=(fp+finb_ref[0:1,:]).reshape(S,R,4,fin_ref.shape[2])
    vc=lambda k: send(fps.at[lax.rem(shard+k,S),rep],fm_ref.at[shard],vs.at[k-1],vr.at[k-1],speer(k))
    for k in range(1,S): vc(k).start()
    fm_ref[shard]=fps[shard,rep]
    for t in ticks[3*U:]: t()
    total=ps[z]
    for k in range(1,nz): zc(k).wait_recv(); total=total+zrv[k-1]
    mod_ref[...]=total
    got(*small[1])
    for k in range(1,S): vc(k).wait_recv(); vc(k).wait_send()
    for m in range(1,R): f1(m).wait_send()
    for n,ref in small:
        near(n,ref).wait_send()
        for k in range(1,nz): far(n,ref,k).wait_send()
    mc.wait_send()
    for k in range(1,nz): zc(k).wait_send()
    ga.finish()

def first_call(w,fo,sm,t1,t2,cls,tb,ada,fin,finb,R,S,cid):
    U,_,own,W=w.shape; nz=S//2; N=S*R*4; FC=fin.shape[2]
    dma=pltpu.SemaphoreType.DMA; V=pltpu.VMEM; sd=jax.ShapeDtypeStruct
    any_=pl.BlockSpec(memory_space=pl.ANY); vm=pl.BlockSpec(memory_space=pltpu.VMEM)
    return pl.pallas_call(functools.partial(first_kernel,R,nz,U,own),
        in_specs=[vm]*10, out_specs=[any_]+[vm]*9,
        out_shape=[sd((U,R,nz,2,own,W),bf),sd((N,256),bf),sd((N,1),f32),sd((nz,2)+sm.shape,bf),sd((2,own,N),f32),sd((nz,2,N,own),bf),sd((own,N),bf),sd((nz,2,N,own),bf),sd((8,6*D),f32),sd((S,4,FC),f32)],
        scratch_shapes=[V((nz,2,R,8,384),f32),V((S,R,4,own),f32),V((nz,2,8,6*D),f32),V((nz,8,6*D),f32),V((nz,8,6*D),f32),V((max(nz-1,1),8,6*D),f32),V((S,R,4,FC),f32),
            dma((R-1,)),dma((R-1,)),dma(()),dma(()),dma((nz-1,)),dma((nz-1,)),dma((S-1,)),dma((S-1,)),dma((4,nz-1)),dma((4,nz-1)),dma((4,)),dma((4,))]+gather_sems(R,nz,U),
        compiler_params=pltpu.CompilerParams(collective_id=cid,has_side_effects=True,vmem_limit_bytes=VLIM),
    )(w,fo,sm,t1,t2,cls,tb,ada,fin,finb)

def fwd_gather_kernel(R,nz,U,x_ref,mod_ref,bias_ref,wa_ref,w1_ref,w2_ref,w_ref,*rest):
    outs=rest[:11]; out_ref=rest[11]; gsems=rest[12:]
    i=pl.program_id(0); last=pl.num_programs(0)-1
    ga=Gather(R,nz,U,w_ref,out_ref,*gsems)
    @pl.when(i==0)
    def _():
        meet(ga.peers()); ga.start()
    ticks=ga.ticks(); used=set()
    def hook(p):
        for step in range(4):
            n=12*step+p-6
            if n>=0 and n%2==0 and n//2<len(ticks):
                used.add(n//2)
                pl.when(i==step)(ticks[n//2])
    fwd_kernel(x_ref,mod_ref,bias_ref,wa_ref,w1_ref,w2_ref,*outs,hook=hook)
    @pl.when(i==last)
    def _():
        for n,t in enumerate(ticks):
            if n not in used: t()
        ga.finish()
FWD_WIDTHS=[(D,bf),(3*D,bf),(128,f32),(D,bf),(D,f32),(D,f32),(D,bf),(FF,f32),(FF,bf),(D,f32),(D,f32)]
def layer_fwd_gather(x,mod,bias,full_w,w,R,S,cid):
    T=x.shape[0]; n=T//TOK; U,_,own,W=w.shape; nz=S//2
    sd=jax.ShapeDtypeStruct
    any_=pl.BlockSpec(memory_space=pl.ANY)
    o=pl.pallas_call(functools.partial(fwd_gather_kernel,R,nz,U),grid=(n,),
        in_specs=[rows(D),pl.BlockSpec((1,8,D),lambda i:(i,0,0)),full((16,D)),unit(0),unit(1),unit(2),pl.BlockSpec(memory_space=pltpu.VMEM)],
        out_specs=[rows(v) for v,_ in FWD_WIDTHS]+[any_],
        out_shape=[sd((T,v),t) for v,t in FWD_WIDTHS]+[sd((U,R,nz,2,own,W),bf)],
        scratch_shapes=gather_sems(R,nz,U),
        compiler_params=pltpu.CompilerParams(collective_id=cid,has_side_effects=True,vmem_limit_bytes=VLIM),
        cost_estimate=pl.CostEstimate(flops=2*T*(9216*D+2*TOK*D),bytes_accessed=60_000_000,transcendentals=T*FF*2),
    )(x,mod,bias,full_w,full_w,full_w,w)
    return o[:11],o[11]
CW=384; NCH=8
def bit_orders(R):
    bits=[1<<i for i in range(R.bit_length()-1)]
    return [bits[g%len(bits):]+bits[:g%len(bits)] if bits else [] for g in range(NCH//R)]
def grad_plan(R):
    orders=bit_orders(R); G=NCH//R; n=len(orders[0])
    def stage(g,m): return next(i for i,b in enumerate(orders[g]) if m&b)
    pos=[]
    for i in range(n+1):
        ms=[[m for m in range(R) if (m==0 and i==n) or (m and stage(g,m)==i)] for g in range(G)]
        if i<n: ms=[sorted(v,key=lambda m,g=g:(-bin(m).count("1"),m)) for g,v in enumerate(ms)]
        for a in range(len(ms[0])):
            for g in range(G): pos.append((g,ms[g][a],i))
    send={}; keep={}; recv={}
    for g,m,i in pos:
        if m: send[g,m]=len(send)
        if i>0 or m==0: keep[g,m]=len(keep)
    for i in range(n):
        for g in range(G):
            for m in range(R):
                if not any(m&b for b in orders[g][:i+1]): recv[g,i,m]=len(recv)
    return orders,n,pos,send,keep,recv

def remote(src,dst,ssem,rsem,dev): return pltpu.make_async_remote_copy(src_ref=src,dst_ref=dst,send_sem=ssem,recv_sem=rsem,device_id=dev,device_id_type=MESH)
def everyone(R,nz):
    rep=lax.axis_index("rep"); shard=lax.axis_index("shard"); z=shard//2; c=lax.rem(shard,2)
    return [(rep,2*z+1-c)]+[(rep,2*lax.rem(z+k,nz)+c) for k in range(1,nz)]+[(jnp.bitwise_xor(rep,m),shard) for m in range(1,R)]
class Sums:
    def __init__(self,R,nz,own,nu,xi,xs,dys,out_ref,scr):
        (self.xin,self.xt,self.dy,self.sbuf,self.obuf,self.rbuf,self.sb,self.rb,self.kf,
         self.xsem,self.dsem,self.csend,self.crecv,self.ssem,self.rsem)=scr
        self.R,self.nz,self.own,self.nu,self.xi,self.xs,self.dys,self.out=R,nz,own,nu,xi,xs,dys,out_ref
        self.orders,self.n,self.pos,self.send,self.keep,self.recv=grad_plan(R)
        self.G=NCH//R
        self.rep=lax.axis_index("rep"); self.shard=lax.axis_index("shard")
        self.z=self.shard//2; self.c=lax.rem(self.shard,2)
        self.mate=(self.rep,2*self.z+1-self.c)
    def xor(self,m): return jnp.bitwise_xor(self.rep,m)
    def rdev(self,m): return (self.xor(m),self.shard)
    def chunk(self,k): return self.pos[k][0]*self.R+self.xor(self.pos[k][1])
    def xcopy(self,i): return pltpu.make_async_copy(self.xs[i],self.xin.at[i],self.xsem.at[i])
    def dstart(self,u,k):
        for i,ref in enumerate(self.dys):
            @pl.when(u==i)
            def _(): pltpu.make_async_copy(ref.at[:,pl.ds(pl.multiple_of(self.chunk(k)*CW,128),CW)],self.dy.at[k%4],self.dsem.at[k%4]).start()
    def dwait(self,k): pltpu.make_async_copy(self.dys[0].at[:,pl.ds(0,CW)],self.dy.at[k%4],self.dsem.at[k%4]).wait()
    def ccopy(self,k): return remote(self.sbuf.at[k%2],self.rbuf.at[k%4],self.csend.at[k%2],self.crecv.at[k%4],self.mate)
    def scopy(self,u,g,m):
        i=next(i for i,b in enumerate(self.orders[g]) if m&b); b=self.orders[g][i]
        a=self.send[g,m]; d=self.recv[g,i,m^b]
        return remote(self.sb.at[u,a],self.rb.at[u,d],self.ssem.at[u,a],self.rsem.at[u,d],self.rdev(b))
    def rwait(self,u,g,i,m):
        d=self.recv[g,i,m]
        remote(self.sb.at[u,0],self.rb.at[u,d],self.ssem.at[u,0],self.rsem.at[u,d],self.rdev(1)).wait_recv()
    def load(self):
        self.xcopy(0).start(); self.xcopy(1).start(); self.dstart(0,0); self.dstart(0,1)
        for i in range(2):
            self.xcopy(i).wait()
            self.xt[i]=self.xin[i].T
    def consume(self,u,k):
        g,m,i=self.pos[k]
        self.ccopy(k).wait_recv()
        total=self.obuf[k%2]+self.rbuf[k%4]
        if i==0 and m:
            self.sb[u,self.send[g,m]]=total.astype(bf)
            self.scopy(u,g,m).start()
        else: self.kf[u,self.keep[g,m]]=total.reshape(self.nz,self.own,CW)
    def products(self,u):
        nz,own=self.nz,self.own
        for k in range(NCH):
            if k+2<NCH: self.dstart(u,k+2)
            else:
                @pl.when(u<self.nu-1)
                def _(): self.dstart(u+1,k+2-NCH)
            self.dwait(k)
            p=mm(self.xt[self.xi(u,self.chunk(k))],self.dy[k%4]).reshape(nz,2,own,CW)
            even=p[:,0].reshape(nz*own,CW); odd=p[:,1].reshape(nz*own,CW)
            if k>=2: self.ccopy(k).wait_send()
            else:
                @pl.when(u>0)
                def _(): self.ccopy(k).wait_send()
            self.sbuf[k%2]=jnp.where(self.c==0,odd,even)
            self.obuf[k%2]=jnp.where(self.c==0,even,odd)
            self.ccopy(k).start()
            if k>0: self.consume(u,k-1)
            else:
                @pl.when(u>0)
                def _(): self.consume(u-1,NCH-1)
    def middle(self,u,i):
        for g,m,j in self.pos:
            if m and j==i:
                v=self.kf[u,self.keep[g,m]].reshape(self.nz*self.own,CW)
                for i2 in range(i):
                    self.rwait(u,g,i2,m); v=v+self.rb[u,self.recv[g,i2,m]].astype(f32)
                self.sb[u,self.send[g,m]]=v.astype(bf)
                self.scopy(u,g,m).start()
    def form(self):
        def one(t,_):
            self.products(t)
            if self.n>1:
                @pl.when(t>=1)
                def _(): self.middle(t-1,1)
            return 0
        lax.fori_loop(0,self.nu,one,0)
        self.consume(self.nu-1,NCH-1)
    def stage(self,i):
        if i<self.n:
            for u in range(self.nu-1 if i==1 else 0,self.nu): self.middle(u,i)
    def hold(self):
        for u in range(self.nu):
            for g in range(self.G):
                v=self.kf[u,self.keep[g,0]]
                for i2 in range(self.n):
                    self.rwait(u,g,i2,0); v=v+self.rb[u,self.recv[g,i2,0]].astype(f32).reshape(self.nz,self.own,CW)
                self.out[u,g]=v
    def finish(self):
        for u in range(self.nu):
            for g in range(self.G):
                for m in range(1,self.R): self.scopy(u,g,m).wait_send()
        self.ccopy(NCH-2).wait_send(); self.ccopy(NCH-1).wait_send()
class Tail:
    def __init__(self,R,nz,own,nu,fin,out_ref,scr):
        (self.zs,self.zr,self.az,self.zss,self.zrs,self.ass,self.ars,self.als)=scr
        self.R,self.nz,self.own,self.nu,self.fin,self.out,self.G=R,nz,own,nu,fin,out_ref,NCH//R
        self.rep=lax.axis_index("rep"); self.shard=lax.axis_index("shard")
        self.z=self.shard//2; self.c=lax.rem(self.shard,2)
    def xor(self,m): return jnp.bitwise_xor(self.rep,m)
    def zdev(self,k): return (self.rep,2*lax.rem(self.z+k,self.nz)+self.c)
    def rdev(self,m): return (self.xor(m),self.shard)
    def each(self): return [(u,g) for u in range(self.nu) for g in range(self.G)]
    def zcopy(self,u,g,k): return remote(self.zs.at[u,g,lax.rem(self.z+k,self.nz)],self.zr.at[u,g,k-1],self.zss.at[u,g,k-1],self.zrs.at[u,g,k-1],self.zdev(k))
    def acopy(self,u,g,m): return remote(self.az.at[u,g],self.out.at[u,g*self.R+self.rep],self.ass.at[u,g,m-1],self.ars.at[u,g,m-1],self.rdev(m))
    def arecv(self,u,g,m): return remote(self.az.at[u,g],self.out.at[u,g*self.R+self.xor(m)],self.ass.at[u,g,m-1],self.ars.at[u,g,m-1],self.rdev(m))
    def alocal(self,u,g): return pltpu.make_async_copy(self.az.at[u,g],self.out.at[u,g*self.R+self.rep],self.als.at[u,g])
    def along(self):
        for u,g in self.each():
            self.zs[u,g]=self.fin[u,g].astype(bf)
            for k in range(1,self.nz): self.zcopy(u,g,k).start()
    def spread(self):
        for u,g in self.each():
            v=self.fin[u,g,self.z]
            for k in range(1,self.nz):
                self.zcopy(u,g,k).wait_recv(); v=v+self.zr[u,g,k-1].astype(f32)
            self.az[u,g]=v
            self.alocal(u,g).start()
            for m in range(1,self.R): self.acopy(u,g,m).start()
    def finish(self):
        for u,g in self.each():
            self.alocal(u,g).wait()
            for m in range(1,self.R): self.arecv(u,g,m).wait_recv(); self.acopy(u,g,m).wait_send()
            for k in range(1,self.nz): self.zcopy(u,g,k).wait_send()
    def squares(self):
        v=jnp.zeros((8,128),f32)
        for u,g in self.each():
            b=self.az[u,g]; b=b*b
            for q in range(CW//128): v=v+jnp.sum(b[:,q*128:(q+1)*128].reshape(self.own//8,8,128),axis=0)
        return v
def sums_scratch(R,nz,own,T,nu):
    orders,n,pos,send,keep,recv=grad_plan(R)
    dma=pltpu.SemaphoreType.DMA; V=pltpu.VMEM
    ns,nk,nr=max(len(send),1),len(keep),max(len(recv),1)
    return [V((2,T,D),bf),V((2,D,T),bf),V((4,T,CW),bf),V((2,D//2,CW),f32),V((2,D//2,CW),f32),V((4,D//2,CW),f32),
            V((nu,ns,D//2,CW),bf),V((nu,nr,D//2,CW),bf),V((nu,nk,nz,own,CW),f32),
            dma((2,)),dma((4,)),dma((2,)),dma((4,)),dma((nu,ns)),dma((nu,nr))]
def tail_scratch(R,nz,own,nu):
    G=NCH//R; dma=pltpu.SemaphoreType.DMA; V=pltpu.VMEM
    return [V((nu,G,nz,own,CW),bf),V((nu,G,nz-1,own,CW),bf),V((nu,G,own,CW),f32),dma((nu,G,nz-1)),dma((nu,G,nz-1)),dma((nu,G,R-1)),dma((nu,G,R-1)),dma((nu,G))]
NSUM=15; NTAIL=8
def remote(src,dst,ssem,rsem,dev): return pltpu.make_async_remote_copy(src_ref=src,dst_ref=dst,send_sem=ssem,recv_sem=rsem,device_id=dev,device_id_type=MESH)
def everyone(R,nz):
    rep=lax.axis_index("rep"); shard=lax.axis_index("shard"); z=shard//2; c=lax.rem(shard,2)
    return [(rep,2*z+1-c)]+[(rep,2*lax.rem(z+k,nz)+c) for k in range(1,nz)]+[(jnp.bitwise_xor(rep,m),shard) for m in range(1,R)]
MLP_X=lambda u,ch: u
ATTN_X=lambda u,ch: ch//6
def carrier_kernel(R,nz,own,nu,xi,nt,compute,ci,co,extra,ei,eo,*refs):
    p=0; parts=[]
    t1=1 if nt else 0
    for cnt in (ci,2+nu,t1,ei,co,1,2*t1,eo,NSUM,NTAIL*t1,len(refs)): parts.append(refs[p:p+cnt]); p+=cnt
    cin,rin,tin,ein,cout,(hold_ref,),tout,eout,scr,tscr,escr=parts
    S_=Sums(R,nz,own,nu,xi,rin[:2],rin[2:],hold_ref,scr)
    T_=Tail(R,nz,own,nt,tin[0],tout[0],tscr) if nt else None
    events=extra(R,nz,ein,eout,escr) if extra else {}
    i=pl.program_id(0); last=pl.num_programs(0)-1
    @pl.when(i==0)
    def _():
        S_.load()
        meet(everyone(R,nz))
        if T_: T_.along()
        for f in events.get(0,[]): f()
        S_.form()
    for q in (1,2,3):
        @pl.when(i==q)
        def _():
            S_.stage(q)
            if T_ and q==2: T_.spread()
            for f in events.get(q,[]): f()
    compute(*cin,*cout)
    @pl.when(i==last)
    def _():
        S_.hold(); S_.finish()
        if T_:
            T_.finish(); tout[1][...]=T_.squares()
        for f in events.get(99,[]): f()
def carry(R,S,cid,xs,dys,xi,tail,compute,cargs,cspecs,coshapes,cospecs,cost,extra=None):
    T=xs[0].shape[0]; nz=S//2; own=D//S; nu=len(dys); G=NCH//R
    any_=pl.BlockSpec(memory_space=pl.ANY); sd=jax.ShapeDtypeStruct
    f,eargs,especs,eshapes,eospecs,escratch=extra or (None,[],[],[],[],[])
    nt=tail[0].shape[0] if tail else 0
    held=(nu,G,nz,own,CW)
    o=pl.pallas_call(functools.partial(carrier_kernel,R,nz,own,nu,xi,nt,compute,len(cargs),len(coshapes),f,len(eargs),len(eshapes)),grid=(T//TOK,),
        in_specs=list(cspecs)+[any_]*(2+nu)+[full(t.shape) for t in tail]+especs,
        out_specs=list(cospecs)+[full(held)]+([any_,full((8,128))] if nt else [])+eospecs,
        out_shape=list(coshapes)+[sd(held,f32)]+([sd((nt,NCH,own,CW),f32),sd((8,128),f32)] if nt else [])+eshapes,
        scratch_shapes=sums_scratch(R,nz,own,T,nu)+(tail_scratch(R,nz,own,nt) if nt else [])+escratch,
        compiler_params=pltpu.CompilerParams(collective_id=cid,has_side_effects=True,vmem_limit_bytes=VLIM),
        cost_estimate=cost)(*cargs,*xs,*dys,*tail,*eargs)
    a=len(coshapes); b=a+1+(2 if nt else 0)
    return o[:a],o[a],o[a+1:b],o[b:]
def last_kernel(R,nz,own,sums,nt,extra,ei,eo,*refs):
    k=1 if sums else 0; p=0; parts=[]
    for cnt in (3*k,k,ei,4*k,eo,NSUM*k,k,NTAIL*k,NTAIL*k,len(refs)): parts.append(refs[p:p+cnt]); p+=cnt
    rin,tin,ein,rout,eout,scr,held,t1scr,t2scr,escr=parts
    if sums:
        S_=Sums(R,nz,own,1,ATTN_X,rin[:2],rin[2:],held[0],scr)
        T1=Tail(R,nz,own,nt,tin[0],rout[0],t1scr); T2=Tail(R,nz,own,1,held[0],rout[2],t2scr)
    def squares():
        return T1.squares()+T2.squares()
    events=extra(R,nz,ein,eout,escr,squares if sums else None)
    run=lambda q: [f() for f in events.get(q,[])]
    if sums: S_.load()
    meet(everyone(R,nz))
    if sums: T1.along()
    run(0)
    if sums: S_.form(); S_.stage(1)
    run(1)
    if sums:
        for i in range(2,S_.n): S_.stage(i)
        T1.spread(); S_.hold(); T2.along()
    run(2)
    run(3)
    if sums: T2.spread()
    run(4)
    if sums:
        S_.finish(); T1.finish(); T2.finish()
        rout[1][...]=T1.squares(); rout[3][...]=T2.squares()
    run(99)
def last_call(R,S,cid,xs,dys,tail,extra):
    nz=S//2; own=D//S; sums=bool(xs); G=NCH//R
    any_=pl.BlockSpec(memory_space=pl.ANY); sd=jax.ShapeDtypeStruct; vm=pl.BlockSpec(memory_space=pltpu.VMEM)
    f,eargs,especs,eshapes,eospecs,escratch=extra
    nt=tail[0].shape[0] if sums else 0
    mine=[]
    if sums: mine=sums_scratch(R,nz,own,xs[0].shape[0],1)+[pltpu.VMEM((1,G,nz,own,CW),f32)]+tail_scratch(R,nz,own,nt)+tail_scratch(R,nz,own,1)
    return pl.pallas_call(functools.partial(last_kernel,R,nz,own,sums,nt,f,len(eargs),len(eshapes)),
        in_specs=[any_]*(len(xs)+len(dys))+[vm]*len(tail)+especs,out_specs=([any_,vm,any_,vm] if sums else [])+eospecs,
        out_shape=([sd((nt,NCH,own,CW),f32),sd((8,128),f32),sd((1,NCH,own,CW),f32),sd((8,128),f32)] if sums else [])+eshapes,
        scratch_shapes=mine+escratch,
        compiler_params=pltpu.CompilerParams(collective_id=cid,has_side_effects=True,vmem_limit_bytes=VLIM))(*xs,*dys,*tail,*eargs)
def sums_call(R,S,cid,xs,dys,tail):
    none=lambda R,nz,ins,outs,scr,squares: {}
    return last_call(R,S,cid,xs,dys,tail,(none,[],[],[],[],[]))

def rows_events(R,nz,ins,outs,scr):
    (w,),(g,)=ins,outs; rs,rr,zs,zr,cs,cr,ls=scr
    rep=lax.axis_index("rep"); shard=lax.axis_index("shard"); z=shard//2; c=lax.rem(shard,2)
    loc=lambda: pltpu.make_async_copy(w,g.at[z,c,rep],ls)
    rc=lambda m: remote(w,g.at[z,c,rep],rs.at[m-1],rr.at[m-1],(jnp.bitwise_xor(rep,m),shard))
    zc=lambda k: remote(g.at[z,c],g.at[z,c],zs.at[k-1],zr.at[k-1],(rep,2*lax.rem(z+k,nz)+c))
    cc=lambda: remote(g.at[:,c],g.at[:,c],cs,cr,(rep,2*z+1-c))
    def a():
        loc().start()
        for m in range(1,R): rc(m).start()
    def b():
        loc().wait()
        for m in range(1,R): rc(m).wait_recv()
        for k in range(1,nz): zc(k).start()
    def d():
        for k in range(1,nz): zc(k).wait_recv()
        cc().start()
    def e():
        cc().wait()
        for m in range(1,R): rc(m).wait_send()
        for k in range(1,nz): zc(k).wait_send()
    return {0:[a],1:[b],2:[d],99:[e]}
def rows_extra(w,R,S):
    nz=S//2; dma=pltpu.SemaphoreType.DMA
    return (rows_events,[w],[full(w.shape)],[jax.ShapeDtypeStruct((nz,2,R)+w.shape,bf)],[pl.BlockSpec(memory_space=pl.ANY)],
        [dma((R-1,)),dma((R-1,)),dma((nz-1,)),dma((nz-1,)),dma(()),dma(()),dma(())])

class ShardSum:
    def __init__(self,nz,x,mr,ps,zr,ms,mrs,zs,zrs):
        self.nz,self.x,self.mr,self.ps,self.zr=nz,x,mr,ps,zr
        self.ms,self.mrs,self.zs,self.zrs=ms,mrs,zs,zrs
        self.rep=lax.axis_index("rep"); shard=lax.axis_index("shard"); self.z=shard//2; self.c=lax.rem(shard,2)
    def mate(self): return remote(self.x.at[:,1-self.c],self.mr,self.ms,self.mrs,(self.rep,2*self.z+1-self.c))
    def far(self,k):
        t=lax.rem(self.z+k,self.nz)
        return remote(self.ps.at[t],self.zr.at[k-1],self.zs.at[k-1],self.zrs.at[k-1],(self.rep,2*t+self.c))
    def one(self): self.mate().start()
    def two(self):
        self.mate().wait_recv()
        self.ps[...]=self.x[:,self.c]+self.mr[...]
        for k in range(1,self.nz): self.far(k).start()
    def three(self):
        v=self.ps[self.z]
        for k in range(1,self.nz): self.far(k).wait_recv(); v=v+self.zr[k-1]
        return v
    def end(self):
        self.mate().wait_send()
        for k in range(1,self.nz): self.far(k).wait_send()
def shard_sum_scratch(nz,shape,own_input):
    V=pltpu.VMEM; dma=pltpu.SemaphoreType.DMA
    return ([V((nz,2)+shape,f32)] if own_input else [])+[V((nz,)+shape,f32),V((nz,)+shape,f32),V((nz-1,)+shape,f32),dma(()),dma(()),dma((nz-1,)),dma((nz-1,))]

def sig_back(v,g):
    t=1.0/(1.0+jnp.exp(-v))
    return g*(t*(1.0+v*(1.0-t)))
def fold(v):
    v=v*v; r,c=v.shape
    if r%8: v=jnp.concatenate([v,jnp.zeros((8-r%8,c),f32)],axis=0)
    v=jnp.sum(v.reshape(-1,8,c),axis=0)
    if c%128: v=jnp.concatenate([v,jnp.zeros((8,128-c%128),f32)],axis=1)
    t=v[:,:128]
    for q in range(1,v.shape[1]//128): t=t+v[:,q*128:(q+1)*128]
    return t
HEAD_ROWS=24; P_SIZE=16; FREQ=256; NCLASS=1000
ROW_SECOND=P_SIZE+2+FREQ; ROW_CLASS=P_SIZE+3+FREQ+D
FIN_ROW=45
def cond_events(R,nz,ins,outs,scr,squares):
    (rows_ref,fin_ref,cond_ref,call_ref,act_ref,pre_ref,lab_ref,feat_ref,ada_ref,finw_ref,t2_ref,w_ref)=ins[:12]
    pieces=ins[12:-1]; sq1_ref=ins[-1]
    adag,fin_t,emb_t,bias_t,head_t,norm_ref=outs
    S=2*nz
    fx,tx,sx,asm=scr[0],scr[8],scr[16],scr[24]
    fs=ShardSum(nz,*scr[0:8]); ts=ShardSum(nz,*scr[8:16]); ss=ShardSum(nz,*scr[16:24])
    g0=scr[25]
    re=rows_events(R,nz,(w_ref,),(g0,),scr[26:33])
    tot,rr,rsem,rrs,gc_s,hs,hr,hcs,hcr,nv,n1,n2,n3,nsem,nrec,headg=scr[33:]
    rep=lax.axis_index("rep"); shard=lax.axis_index("shard"); z=shard//2; c=lax.rem(shard,2)
    nr,own=tot.shape; nb=nr-HEAD_ROWS; FC=fin_ref.shape[1]
    mate=(rep,2*z+1-c); zdev=lambda k: (rep,2*lax.rem(z+k,nz)+c); rdev=lambda m: (jnp.bitwise_xor(rep,m),shard)
    rc=lambda m: remote(tot,rr.at[rep],rsem.at[m-1],rrs.at[m-1],rdev(m))
    hz=lambda k: remote(headg.at[z,c],headg.at[z,c],hs.at[k-1],hr.at[k-1],zdev(k))
    hc=lambda: remote(headg.at[:,c],headg.at[:,c],hcs,hcr,mate)
    M6=6*D
    def gather():
        asm[...]=jnp.zeros(asm.shape,f32)
        for l in range(2):
            db1,db2,dm1,dm2=pieces[4*l:4*l+4]; o=14*l
            asm[o:o+2]=db2[0:2]; asm[o+2:o+7]=db1[2:7]; asm[o+13:o+14]=db1[13:14]
            t1=jnp.sum(dm1[...],axis=0); t2=jnp.sum(dm2[...],axis=0)
            asm[o+7:o+9]=t2[0:2]; asm[o+9:o+13]=t1[2:6]
        pg,pb,gfm,hd=pieces[8:]
        asm[28:44]=pg[...]; asm[44:45]=pb[...]
        asm[FIN_ROW:FIN_ROW+2]=jnp.sum(gfm[...],axis=0)
        asm[nb:]=hd[...]
        for s in range(S):
            sx[s//2,s%2]=asm[:,s*own:(s+1)*own]
            for r in range(FC//own):
                p=s*FC+r*own; row=FIN_ROW+p//D
                sx[s//2,s%2,FIN_ROW+r:FIN_ROW+r+1,:]=asm[row:row+1,p%D:p%D+own]
        ss.one()
        fin=fin_ref[...]
        for s in range(S): fx[s//2,s%2]=mm_nt(finw_ref[s],fin)
        fs.one()
    def layer1():
        gc=jnp.zeros(gc_s.shape,f32)
        for q in range(6):
            o=slice(q*D,(q+1)*D); r=rows_ref[:,o]
            adag[1,:,o]=mm(cond_ref[...],r)
            gc=gc+mm_nt(ada_ref[1,:,o],r)
        gc_s[...]=gc
        f=mm_tn(fin_ref[...],call_ref[...])
        fin_t[:,:D]=f
        nv[...]=fold(f)
        fs.two(); ss.two()
    def total():
        tot[...]=ss.three()
        rr[rep]=tot[...]
        for m in range(1,R): rc(m).start()
    def layer0():
        for f in re[99]: f()
        N=cond_ref.shape[1]; M=4*N; B=M6//4
        g=g0[...].reshape(M,B)
        wide=jnp.zeros((own,M),f32)
        at=lax.broadcasted_iota(jnp.int32,(1,M),1)
        n_of=lax.broadcasted_iota(jnp.int32,(N,1),0)
        for j in range(4):
            o=slice(j*B,(j+1)*B)
            spot=jnp.where(at==4*n_of+j,1.0,0.0).astype(bf)
            adag[0,:,o]=mm(mm(cond_ref[...],spot).astype(bf),g)
            wide=wide+jnp.where(at-4*(at//4)==j,mm_nt(ada_ref[0,:,o],g),0.0)
        pick=jnp.where(lax.broadcasted_iota(jnp.int32,(M,1),0)//4==lax.broadcasted_iota(jnp.int32,(1,N),1),1.0,0.0)
        gc=gc_s[...]+lax.dot_general(wide,pick,(((1,),(0,)),((),())),precision=lax.Precision.HIGHEST,preferred_element_type=f32)
        g=sig_back(pre_ref[1],gc+fs.three())
        low=g.astype(bf)
        for s in range(S): tx[s//2,s%2]=mm_tn(t2_ref[s],low)
        ts.one()
        b=jnp.sum(g,axis=1,keepdims=True)
        second=mm(low,act_ref[...])
        emb_t[:,ROW_SECOND:ROW_SECOND+D]=second; emb_t[:,ROW_SECOND+D:ROW_SECOND+D+1]=b
        hot=jnp.where(lab_ref[...]==lax.broadcasted_iota(jnp.int32,(1,1024),1).astype(f32),1.0,0.0)
        table=lax.dot_general(g,hot,(((1,),(0,)),((),())),precision=lax.Precision.HIGHEST,preferred_element_type=f32)
        emb_t[:,ROW_CLASS:ROW_CLASS+NCLASS]=table[:,:NCLASS]
        nv[...]=nv[...]+fold(second)+fold(table)+fold(column(b))
    def column(b):
        return jnp.where(lax.broadcasted_iota(jnp.int32,(1,128),1)<1,jnp.broadcast_to(b,(b.shape[0],128)),0.0)
    def time_and_sums():
        ts.two()
        for m in range(1,R): rc(m).wait_recv()
        v=rr[0]
        for r in range(1,R): v=v+rr[r]
        headg[z,c]=v[nb:]
        for k in range(1,nz): hz(k).start()
        p=nv[...]+fold(v[:nb])
        for q in range(2): p=p+fold(adag[q])
        for l in range(2): bias_t[l,:,0:14]=v[14*l:14*l+14].T
        emb_t[:,0:P_SIZE+1]=v[28:28+P_SIZE+1].T
        last=v[FIN_ROW:FIN_ROW+FC//own].T
        for r in range(FC//own): fin_t[r*own:(r+1)*own,D:D+1]=last[:,r:r+1]
        g=sig_back(pre_ref[0],ts.three())
        b=jnp.sum(g,axis=1,keepdims=True)
        f=mm(g.astype(bf),feat_ref[...])
        emb_t[:,P_SIZE+1:P_SIZE+1+FREQ]=f; emb_t[:,P_SIZE+1+FREQ:P_SIZE+2+FREQ]=b
        nv[...]=jnp.where(rep==0,p+fold(f)+fold(column(b)),0.0)
        for k in range(1,nz): hz(k).wait_recv()
        hc().start()
    def end():
        hc().wait()
        for k in range(1,nz): hz(k).wait_send()
        for m in range(1,R): rc(m).wait_send()
        fs.end(); ts.end(); ss.end()
        nv[...]=nv[...]+sq1_ref[...]+(squares() if squares else 0.0)
        cp=remote(nv,n1,nsem.at[0],nrec.at[0],mate)
        cp.start(); cp.wait()
        n2[z]=nv[...]+n1[...]
        nz_=lambda k: remote(n2.at[z],n2.at[z],nsem.at[k],nrec.at[k],zdev(k))
        for k in range(1,nz): nz_(k).start()
        for k in range(1,nz): nz_(k).wait()
        v=n2[0]
        for q in range(1,nz): v=v+n2[q]
        n3[rep]=v
        nr_=lambda m: remote(n3.at[rep],n3.at[rep],nsem.at[nz-1+m],nrec.at[nz-1+m],rdev(m))
        for m in range(1,R): nr_(m).start()
        for m in range(1,R): nr_(m).wait()
        v=n3[0]
        for r in range(1,R): v=v+n3[r]
        for s in range(S):
            h=headg[s//2,s%2]
            v=v+fold(h[:HEAD_ROWS-1])
            head_t[:,s*own:(s+1)*own]=h[:P_SIZE]
        head_t[:,D:D+1]=headg[0,0][P_SIZE:P_SIZE+1,:P_SIZE].T
        norm=jnp.sqrt(jnp.sum(jnp.sum(v,axis=1,keepdims=True),axis=0,keepdims=True))
        loss=jnp.sum(headg[0,0][HEAD_ROWS-1:HEAD_ROWS,:P_SIZE],axis=1,keepdims=True)
        norm_ref[0:1,:]=jnp.broadcast_to(norm,(1,128))
        norm_ref[1:2,:]=jnp.broadcast_to(loss,(1,128))
    return {0:re[0]+[gather],1:re[1]+[layer1],2:re[2]+[total],3:[layer0],4:[time_and_sums],99:[end]}
def cond_extra(args,R,S):
    nz=S//2; own=D//S; N=args[2].shape[1]; nr=48+HEAD_ROWS; FC=args[1].shape[1]; w=args[11]
    vm=pl.BlockSpec(memory_space=pltpu.VMEM); sd=jax.ShapeDtypeStruct; dma=pltpu.SemaphoreType.DMA; V=pltpu.VMEM
    shapes=[sd((2,own,6*D),f32),sd((FC,D+128),f32),sd((own,2048),f32),sd((2,own,128),f32),sd((P_SIZE,D+128),f32),sd((8,128),f32)]
    scratch=shard_sum_scratch(nz,(own,N),True)*2+shard_sum_scratch(nz,(nr,own),True)+[V((nr,D),f32),V((nz,2,R)+w.shape,bf)]
    scratch+=[dma((R-1,)),dma((R-1,)),dma((nz-1,)),dma((nz-1,)),dma(()),dma(()),dma(())]
    scratch+=[V((nr,own),f32),V((R,nr,own),f32),dma((R-1,)),dma((R-1,)),V((own,N),f32),
        dma((nz-1,)),dma((nz-1,)),dma(()),dma(()),V((8,128),f32),V((8,128),f32),V((nz,8,128),f32),V((R,8,128),f32),dma((nz+R,)),dma((nz+R,)),V((nz,2,HEAD_ROWS,own),f32)]
    return (cond_events,list(args),[vm]*len(args),shapes,[vm]*len(shapes),scratch)

def head_kernel(inv,x_ref,fm_ref,hw_ref,hb_ref,tn_ref,gx_ref,gfm_ref,hg_ref):
    i=pl.program_id(0)
    x=x_ref[...]
    sh=fm_ref[0,0:1,:]; sc=fm_ref[0,1:2,:]
    xh,r=ln_parts(x)
    nrm=(xh*(1.0+sc)+sh).astype(bf)
    diff=mm(nrm,hw_ref[...])+hb_ref[0:1,:]-tn_ref[0].T
    g=2.0*(diff*inv)
    low=g.astype(bf)
    @pl.when(i==0)
    def _():
        hg_ref[...]=jnp.zeros_like(hg_ref)
    p=low.shape[1]
    hg_ref[:p]+=mm_tn(low,nrm)
    hg_ref[p:p+1,:p]+=jnp.sum(g,axis=0,keepdims=True)
    hg_ref[HEAD_ROWS-1:HEAD_ROWS,:p]+=jnp.sum(diff*diff,axis=0,keepdims=True)
    gn=mm_nt(low,hw_ref[...])
    gfm_ref[0,0:1,:]=jnp.sum(gn,axis=0,keepdims=True)
    gfm_ref[0,1:2,:]=jnp.sum(gn*xh,axis=0,keepdims=True)
    gx_ref[...]=ln_back(gn,xh,r,sc)
def head(x,fm,hw,hb,tn,inv):
    T=x.shape[0]; n=T//TOK; sd=jax.ShapeDtypeStruct; p=hw.shape[1]
    m2=pl.BlockSpec((1,2,D),lambda i:(i,0,0))
    fixed=lambda *s: pl.BlockSpec(s,lambda i:(0,)*len(s))
    return pl.pallas_call(functools.partial(head_kernel,inv),grid=(n,),
        in_specs=[rows(D),m2,fixed(D,p),fixed(1,p),pl.BlockSpec((1,p,TOK),lambda i:(i,0,0))],
        out_specs=[rows(D),m2,fixed(HEAD_ROWS,D)],
        out_shape=[sd((T,D),f32),sd((n,2,D),f32),sd((HEAD_ROWS,D),f32)],
        compiler_params=pltpu.CompilerParams(vmem_limit_bytes=VLIM))(x,fm,hw,hb,tn)
LAYERS=2
NB=4
beta_one=0.9; beta_two=0.999; adam_eps=1e-8; learn_rate=0.01; weight_decay=0.01; step_count=10.0
def adam_update(w,g,m,v,factor):
    s=g*factor
    m2=beta_one*m+(1.0-beta_one)*s
    v2=beta_two*v+(1.0-beta_two)*s*s
    mh=m2*(1.0/(1.0-beta_one**step_count))
    vh=v2*(1.0/(1.0-beta_two**step_count))
    w2=w-learn_rate*(mh/(jnp.sqrt(vh)+adam_eps)+weight_decay*w)
    return (w2,m2,v2,w2.astype(bf))
def inner_adam_kernel(f_ref,a0_ref,m0_ref,a1_ref,m1_ref,ada_ref,w_ref,m_ref,v_ref,*outs):
    factor=f_ref[0]; l=pl.program_id(0); j=pl.program_id(1)
    def put(sl,g):
        for o,val in zip(outs,adam_update(w_ref[0,:,sl],g,m_ref[0,:,sl],v_ref[0,:,sl],factor)): o[0,:,sl]=val
    for a in range(NB):
        sl=slice(a*CW,(a+1)*CW)
        for layer,refs in enumerate(((a0_ref,m0_ref),(a1_ref,m1_ref))):
            for part,ref in enumerate(refs):
                @pl.when(jnp.logical_and(j//(NCH//NB)==part,l==layer))
                def _(): put(sl,ref[0,a])
        @pl.when(j>=2*NCH//NB)
        def _(): put(sl,ada_ref[0,:,sl])
def inner_adam(factor,grads,ada,w,m,v):
    own=w.shape[1]; C=w.shape[2]; W=NB*CW
    blk=pl.BlockSpec((1,own,W),lambda l,j:(l,0,j))
    def gmap(layer,part):
        def index(l,j):
            jj=jnp.clip(j-(NCH//NB)*part,0,NCH//NB-1); on=jnp.where(l==layer,jj,(NCH//NB-1)*(l>layer))
            return (part,on,0,0)
        return pl.BlockSpec((1,NB,own,CW),index)
    sd=jax.ShapeDtypeStruct
    return pl.pallas_call(inner_adam_kernel,grid=(LAYERS,C//W),
        in_specs=[pl.BlockSpec(memory_space=pltpu.SMEM)]+[gmap(l,p) for l in range(2) for p in range(2)]+[pl.BlockSpec((1,own,W),lambda l,j:(l,0,jnp.maximum(j-2*NCH//NB,0))),blk,blk,blk],
        out_specs=[blk]*4,out_shape=[sd(w.shape,f32)]*3+[sd(w.shape,bf)],
        compiler_params=pltpu.CompilerParams(vmem_limit_bytes=VLIM))(factor,*grads,ada,w,m,v)
def outer_adam_kernel(f_ref,g0_ref,g1_ref,b_ref,w_ref,m_ref,v_ref,*outs):
    factor=f_ref[0]; l=pl.program_id(0); j=pl.program_id(1)
    def put(sl,g):
        for o,val in zip(outs,adam_update(w_ref[0,:,sl],g,m_ref[0,:,sl],v_ref[0,:,sl],factor)): o[0,:,sl]=val
    for a in range(NB):
        sl=slice(a*CW,(a+1)*CW)
        for layer,ref in enumerate((g0_ref,g1_ref)):
            @pl.when(jnp.logical_and(j<NCH//NB,l==layer))
            def _(): put(sl,ref[0,a])
    @pl.when(j==NCH//NB)
    def _(): put(slice(0,128),b_ref[0])
def outer_adam(factor,g0,g1,b,w,m,v):
    own=w.shape[1]; W=NB*CW
    blk=pl.BlockSpec((1,own,W),lambda l,j:(l,0,j))
    def gmap(layer):
        def index(l,j):
            jj=jnp.minimum(j,NCH//NB-1); on=jnp.where(l==layer,jj,(NCH//NB-1)*(l>layer))
            return (0, on, 0, 0)
        return pl.BlockSpec((1,NB,own,CW),index)
    sd=jax.ShapeDtypeStruct
    return pl.pallas_call(outer_adam_kernel,grid=(LAYERS,NCH//NB+1),
        in_specs=[pl.BlockSpec(memory_space=pltpu.SMEM),gmap(0),gmap(1),pl.BlockSpec((1,own,128),lambda l,j:(l,0,0)),blk,blk,blk],
        out_specs=[blk]*4,out_shape=[sd(w.shape,f32)]*3+[sd(w.shape,bf)],
        compiler_params=pltpu.CompilerParams(vmem_limit_bytes=VLIM))(factor,g0,g1,b,w,m,v)
GRID=16; LAT_DEV=4
clip_coef=2.5
BIAS=14
def position_table(grid_side, feature_width):
    quarter=feature_width//4
    omega=jnp.exp(-math.log(10000.0)*jnp.arange(quarter,dtype=f32)/quarter)
    ids=jnp.arange(grid_side*grid_side,dtype=jnp.int32)
    a=(ids%grid_side).astype(f32)[:,None]*omega[None,:]
    d=(ids//grid_side).astype(f32)[:,None]*omega[None,:]
    return jnp.concatenate([jnp.sin(a),jnp.cos(a),jnp.sin(d),jnp.cos(d)],axis=1)
def time_features(steps, count):
    half=count//2
    freq=jnp.exp(-math.log(10000.0)*jnp.arange(half,dtype=f32)/half)
    ang=steps.astype(f32)[:,None]*freq[None,:]
    return jnp.concatenate([jnp.cos(ang),jnp.sin(ang)],axis=1)
def dot32(pattern,a,b): return jnp.einsum(pattern,a,b,preferred_element_type=f32)
ALL=("rep","shard")

def per_device(latents,target_noise,labels,time_steps,inner_weights,outer_weights,embed_table,final_mod,head_weights,
               inner_moment,inner_square,outer_moment,outer_square,embed_moment,embed_square,final_moment,final_square,head_moment,head_square):
    R=lax.axis_size("rep"); S=lax.axis_size("shard")
    rep=lax.axis_index("rep"); shard=lax.axis_index("shard")
    own=D//S; W=4*D//R; N=LAT_DEV*R*S; G=LAT_DEV*S
    count=N*TOK*P_SIZE
    inner_low=inner_weights.astype(bf)
    outer_turn=lambda a: a.transpose(0,2,1)
    outer_low=outer_turn(outer_weights).astype(bf)
    def slab(l):
        s=jnp.stack([inner_low[l,:,:4*D],inner_low[l,:,4*D:8*D],outer_low[l,:,:FF]])
        return s.reshape(3,own,R,W).transpose(0,2,1,3)
    embed_low=embed_table.T.astype(bf); final_low=final_mod.astype(bf); head_low=head_weights.astype(bf)
    r1=P_SIZE+1; r2=P_SIZE+2+FREQ; r3=P_SIZE+3+FREQ+D
    fin_cols=2*D//S
    small=jnp.concatenate([outer_low[0,:,FF:],outer_low[1,:,FF:],embed_low[:,:P_SIZE+1]],axis=1).T
    small=jnp.pad(small,((0,48-small.shape[0]),(0,0)))
    mine_rows=jnp.concatenate([time_features(time_steps,FREQ).astype(bf).astype(f32),labels.astype(f32)[:,None],jnp.zeros((LAT_DEV,127),f32)],axis=1)
    mine_rows=jnp.concatenate([mine_rows,mine_rows],axis=0)
    second_w=embed_low[:,r2:r2+D]
    table=jnp.pad(embed_low[:,r3:],((0,0),(0,1024-NCLASS)))
    biases2=jnp.pad(jnp.stack([embed_low[:,r1+FREQ],embed_low[:,r2+D]]).astype(f32),((0,6),(0,0)))
    ada_own=inner_low[:,:,4*D+FF:]
    fin_bias=jnp.pad(final_low[D:].astype(f32),((0,7),(0,0)))
    first=first_call(slab(0),mine_rows,small,embed_low[:,r1:r1+FREQ],second_w.reshape(own,S,own).transpose(1,0,2),table,biases2,ada_own,final_low[:D].reshape(S,own,fin_cols),fin_bias,R,S,0)
    gather0,features,label_col,small,before,time_act,cond_own,cond_all,modul,fin_mod=first
    time_act=time_act.reshape(S,N,own).transpose(1,0,2).reshape(N,D)
    cond_all=cond_all.reshape(S,N,own).transpose(1,0,2).reshape(N,D)
    small=small.reshape(S,48,own)
    small=small.transpose(1,0,2).reshape(48,D)
    biases=small[:LAYERS*BIAS].reshape(LAYERS,BIAS,D).astype(f32)
    patch_w=small[LAYERS*BIAS:LAYERS*BIAS+P_SIZE]; patch_b=small[LAYERS*BIAS+P_SIZE].astype(f32)
    modul=modul.reshape(LAYERS,LAT_DEV,6,D)+biases[:,None,7:13]
    modul=jnp.pad(modul,((0,0),(0,0),(0,2),(0,0)))
    fin_mod=fin_mod.transpose(1,0,2).reshape(LAT_DEV,2,D)
    ramp=0.0001+(0.02-0.0001)*jnp.arange(1000,dtype=f32)/999.0
    upto=jnp.arange(1000,dtype=jnp.int32)[None,:]<=time_steps[:,None]
    abar=jnp.exp(jnp.sum(jnp.where(upto,jnp.log(1.0-ramp)[None,:],0.0),axis=1))
    patches=(jnp.sqrt(abar)[:,None,None]*latents+jnp.sqrt(1.0-abar)[:,None,None]*target_noise).astype(bf)
    stream=dot32("gpt,pd->gtd",patches,patch_w)+patch_b+position_table(GRID,D)[None]
    stream=stream.reshape(LAT_DEV*TOK,D)
    saved=[]
    gathered=[unit_blocks(gather0,R)]
    for l in range(LAYERS):
        full_w=gathered[l]
        bias=jnp.pad(biases[l],((0,2),(0,0)))
        if l==0:
            o,gather1=layer_fwd_gather(stream,modul[l],bias,full_w,slab(1),R,S,1)
            gathered.append(unit_blocks(gather1,R))
        else: o=layer_fwd(stream,modul[l],bias,full_w)
        saved.append((stream,)+tuple(o))
        stream=o[-1]
    grad_stream,grad_fin,head_rows=head(stream,fin_mod,head_low[:D],head_low[D:].astype(f32),target_noise,1.0/count)
    def mlp_parts(l,g):
        x,normed,qkv,lse,mixed,attn,mid,ntwo,upper,activ,down,_=saved[l]
        return bwd_mlp_parts(g,modul[l],gathered[l],down,upper,mid,attn)
    def attn_parts(l,gmix,alow,gmid):
        x,normed,qkv,lse,mixed,attn,mid,ntwo,upper,activ,down,_=saved[l]
        return bwd_attn_parts(gmix,alow,gmid,modul[l],gathered[l],qkv,lse,x)
    mod_grad=lambda dm1,dm2: jnp.concatenate([dm2[:,:2],dm1[:,2:6]],axis=1).astype(bf).reshape(LAT_DEV,6*D)
    def mlp_sums(l,dlow,ulow): return (dlow,saved[l][7]),(saved[l][9],ulow)
    def attn_sums(l,low): return (saved[l][1],saved[l][4]),(low,)
    dlow,ulow,gmid,alow,gmix,dm1_1,db1_1=plain(*mlp_parts(1,grad_stream))
    (low,grad_stream,dm2_1,db2_1),held,_,_=carry(R,S,2,*mlp_sums(1,dlow,ulow),MLP_X,(),*attn_parts(1,gmix,alow,gmid))
    late=jnp.concatenate([mod_grad(dm1_1,dm2_1),grad_fin.astype(bf).reshape(LAT_DEV,2*D)],axis=1)
    (dlow,ulow,gmid,alow,gmix,dm1_0,db1_0),held,(mlp1,sq_a),(late,)=carry(R,S,3,*attn_sums(1,low),ATTN_X,(held,),*mlp_parts(0,grad_stream),
        extra=rows_extra(late.reshape(16,8*D*LAT_DEV//16),R,S))
    (low,grad_stream,dm2_0,db2_0),held,(attn1,sq_b),_=carry(R,S,4,*mlp_sums(0,dlow,ulow),MLP_X,(held,),*attn_parts(0,gmix,alow,gmid))
    late=late.reshape(N,8*D)
    fin_mine=lax.dynamic_slice_in_dim(late,6*D+shard*fin_cols,fin_cols,1)
    gs=grad_stream.reshape(LAT_DEV,TOK,D)
    patch_grad=dot32("gpt,gtd->pd",patches,gs.astype(bf))
    patch_bias=jnp.sum(grad_stream,axis=0)[None]
    cond_back=lambda squares: cond_extra((late,fin_mine,cond_own,cond_all,time_act,before,label_col,features,ada_own,final_low[:D].reshape(S,own,fin_cols),
        second_w.reshape(own,S,own).transpose(1,0,2),mod_grad(dm1_0,dm2_0).reshape(16,6*D*LAT_DEV//16),
        db1_0,db2_0,dm1_0,dm2_0,db1_1,db2_1,dm1_1,dm2_1,patch_grad,patch_bias,grad_fin,head_rows,squares),R,S)
    squares=sq_a+sq_b
    if N<=256: mlp0,_,attn0,_,*rest=last_call(R,S,5,*attn_sums(0,low),(held,),cond_back(squares))
    else:
        mlp0,sq_c,attn0,sq_d=sums_call(R,S,5,*attn_sums(0,low),(held,))
        rest=last_call(R,S,6,(),(),(),cond_back(squares+sq_c+sq_d))
    ada_grad,final_turn,embed_grad,bias_turn,head_total,numbers=rest
    embed_grad=embed_grad[:,:embed_table.shape[0]]; final_turn=final_turn[:,:D+1]; head_total=head_total[:,:D+1].T
    grad_norm=numbers[0,0]; mean_loss=numbers[1,0]/count
    factor=jnp.minimum(1.0,clip_coef*math.sqrt(D/count)/grad_norm)
    out=[mean_loss,grad_norm]
    out.extend(inner_adam(factor.reshape(1),(attn0,mlp0,attn1,mlp1),ada_grad,inner_weights,inner_moment,inner_square))
    out.extend(outer_turn(a) for a in outer_adam(factor.reshape(1),mlp0,mlp1,bias_turn,outer_turn(outer_weights),outer_turn(outer_moment),outer_turn(outer_square)))
    for w,g,m,v in ((embed_table,embed_grad.T,embed_moment,embed_square),(final_mod,final_turn.T,final_moment,final_square),
                    (head_weights,head_total,head_moment,head_square)):
        out.extend(adam_update(w,g,m,v,factor))
    return tuple(out)

def solution(mesh):
    lat=P(ALL,None,None); one=P(ALL); inn=P(None,"shard",None); oute=P(None,None,"shard"); col=P(None,"shard")
    in_specs=(lat,lat,one,one,inn,oute,col,col,P(),inn,inn,oute,oute,col,col,col,col,P(),P())
    out_specs=(P(),P())+(inn,)*4+(oute,)*4+(col,)*8+(P(),)*4
    return jax.shard_map(per_device,mesh=mesh,in_specs=in_specs,out_specs=out_specs,check_vma=False)
```
